32 devices in a mesh: seq: 8 (over y, x, core), dp: 4 (over z).
Axes of the slice: x: 2, y: 2, z: 4, core: 2. Of those that a mesh axis runs over, the one named last changes fastest.
Arguments:
- queries: bfloat16 [4, 2048, 3072], P('dp', 'seq'), may hold values from -30 to 30
- keys: bfloat16 [4, 2048, 3072], P('dp', 'seq'), may hold values from -6 to 6
- values: bfloat16 [4, 2048, 3072], P('dp', 'seq'), may hold values from -6 to 6
- grad_out: bfloat16 [4, 2048, 3072], P('dp', 'seq'), may hold values from -96 to 96
- bias_table: float32 [24, 128], P('dp'), may hold values from -4 to 4
- slot_tiles: int32 [8, 5], replicated, may hold values from 0 to 15, as said below
- live: int32 [8, 7], P('seq'), may hold values from 0 to 1, as said below
- buckets: int32 [8, 7], P('seq'), may hold values from 0 to 81
Outputs:
- query_grad: bfloat16 [4, 2048, 3072], P('dp', 'seq')
- key_grad: bfloat16 [4, 2048, 3072], P('dp', 'seq')
- value_grad: bfloat16 [4, 2048, 3072], P('dp', 'seq')
- table_grad: float32 [24, 128], P('dp')
The draws below stay inside these ranges and needn't reach their ends.
Inputs may be any that keep to these rules, and one draw needn't show every extreme that they name: Entry s of row i names a key tile of query tile i - 1, i + 1, i - 2, i + 2 for s = 0, 1, 2, 3 and of query tile (i + 4) mod 8 for s = 4, that is, slot_tiles[i, s] // 2 is that query tile; where that query tile would lie outside 0 to 7 the entry names one of query tile i's own key tiles and is not live. `live`: entry 0 of every row is 1. Row 4 is 1 everywhere. Row 0 is 1 everywhere except entries 2 and 4.
All inputs are finite; a program needn't handle non-finite values.
Results may differ from the reference program's by a relative error of at most 0.008.
Values may be sent and summed in bfloat16 or wider, within the bound.
No kernel may reach another device: no remote copies, remote signals or barrier semaphores. Data moves between devices by JAX's collectives and lax.ppermute only.
A program may use at most 192 MiB of HBM per device.

```python
import jax
import jax.numpy as jnp
from jax import lax

HEADS = 24
HEAD_DIM = 128
TOK_DEV = 256
TILE = 128
TILE_COLS = 16
SLOTS = 5
BUCKETS = 82
WIDTH = 3072
TILES_DEV = 2
QUERY_TILES = 8
KEY_TILES = 16
LENGTH = 2048
WINDOWS = 4
TABLE = 128


def draw_pattern(key):
    index = jnp.arange(QUERY_TILES, dtype=jnp.int32)[:, None]
    near = index + jnp.array([-1, 1, -2, 2], jnp.int32)[None, :]
    near_valid = (near >= 0) & (near < QUERY_TILES)
    far = (index + QUERY_TILES // 2) % QUERY_TILES
    partner = jnp.concatenate([jnp.where(near_valid, near, index), far], axis=1)
    valid = jnp.concatenate([near_valid, jnp.ones((QUERY_TILES, 1), dtype=bool)], axis=1)
    sub_tile = jax.random.randint(jax.random.fold_in(key, 11), (QUERY_TILES, SLOTS), 0, TILES_DEV)
    tiles = partner * TILES_DEV + sub_tile
    level = jax.random.randint(jax.random.fold_in(key, 12), (QUERY_TILES, 1), 0, 3)
    level = jnp.where((index == QUERY_TILES // 2) | (index == 0), 2, level)
    own_roll = jax.random.randint(jax.random.fold_in(key, 13), (QUERY_TILES, TILES_DEV), 0, 4)
    own_limit = jnp.where(level == 0, 1, jnp.where(level == 1, 2, 4))
    own_live = (own_roll < own_limit) | (jnp.arange(TILES_DEV, dtype=jnp.int32)[None, :] == 0)
    slot_roll = jax.random.randint(jax.random.fold_in(key, 14), (QUERY_TILES, SLOTS), 0, 4)
    slot_limit = jnp.where(level == 0, 0, jnp.where(level == 1, 2, 4))
    slot_live = (slot_roll < slot_limit) & valid
    live_table = jnp.concatenate([own_live, slot_live], axis=1).astype(jnp.int32)
    return (tiles.astype(jnp.int32), live_table)


def draw_slot_tiles(key, part):
    return draw_pattern(key)[0]


def draw_live(key, part):
    return draw_pattern(key)[1]


def draw_query_key(key):
    shape = (WINDOWS, LENGTH, WIDTH)
    seed_query = jax.random.fold_in(key, 21)
    seed_key = jax.random.fold_in(key, 22)
    query_value = jax.random.truncated_normal(seed_query, -6.0, 6.0, shape, jnp.float32)
    key_value = jax.random.truncated_normal(seed_key, -6.0, 6.0, shape, jnp.float32)
    return (query_value, key_value)


def draw_queries(key, part):
    return draw_query_key(key)[0].astype(jnp.bfloat16)


def draw_keys(key, part):
    return draw_query_key(key)[1].astype(jnp.bfloat16)


def touch_ends(drawn, own_key, least, high):
    index_at = [jax.random.randint(jax.random.fold_in(own_key, axis), (), 0, length) for axis, length in enumerate(drawn.shape)]
    longest = drawn.shape.index(max(drawn.shape))
    neighbour = index_at[:longest] + [(index_at[longest] + 1) % drawn.shape[longest]] + index_at[longest + 1:]
    return drawn.at[tuple(index_at)].set(least).at[tuple(neighbour)].set(high)


def levels(stream_key, extent, split, low, top_value):
    level = 1.0
    for position, shards_of in split:
        heights = jax.random.uniform(jax.random.fold_in(jax.random.fold_in(stream_key, 6), position), (shards_of,), jnp.float32, low / len(split), top_value / len(split))
        level = level * jnp.repeat(jnp.exp(heights), extent[position] // shards_of).reshape((-1,) + (1,) * (len(extent) - 1 - position))
    return level


def normal_values(stream_key, shape, width, limit, cuts=(), kind=jnp.bfloat16):
    values = jax.random.normal(stream_key, shape, jnp.float32) * width
    if len(cuts) > 0:
        values = levels(stream_key, shape, cuts, -0.22, 0.18) * values
    return jnp.clip(values, min=-limit, max=limit).astype(kind)


def setup_inputs(seed: int = 0) -> dict:
    arg_keys = jax.random.split(jax.random.key(seed), 9)
    queries = draw_queries(jax.random.fold_in(arg_keys[8], 71), 0)
    keys = draw_keys(jax.random.fold_in(arg_keys[8], 71), 0)
    values = normal_values(arg_keys[2], (WINDOWS, LENGTH, WIDTH), 1.0, 6.0, ((0, 4), (1, 8)))
    grad_out = normal_values(arg_keys[3], (WINDOWS, LENGTH, WIDTH), 16.0, 96.0, ((0, 4), (1, 8)))
    bias_table = normal_values(arg_keys[4], (HEADS, TABLE), 1.0, 4.0, ((0, 4),), jnp.float32)
    slot_tiles = draw_slot_tiles(jax.random.fold_in(arg_keys[8], 71), 0)
    live = draw_live(jax.random.fold_in(arg_keys[8], 71), 0)
    buckets = touch_ends(jax.random.randint(arg_keys[7], (QUERY_TILES, TILES_DEV + SLOTS), 0, BUCKETS), jax.random.fold_in(arg_keys[7], 1), 0, BUCKETS - 1).astype(jnp.int32)
    return dict(queries=queries, keys=keys, values=values, grad_out=grad_out, bias_table=bias_table, slot_tiles=slot_tiles, live=live, buckets=buckets)


NEGATIVE = -1e30


def rounded(array):
    low = array.astype(jnp.bfloat16)
    low = lax.optimization_barrier(low)
    return low.astype(jnp.float32)


def offset_indices():
    tile_rows = TILE // TILE_COLS
    query_pos = jnp.arange(TOK_DEV, dtype=jnp.int32)[:, None]
    key_pos = jnp.arange(TILE, dtype=jnp.int32)[None, :]
    column_index = key_pos % TILE_COLS - query_pos % TILE_COLS + TILE_COLS - 1
    row_index = key_pos // TILE_COLS - (query_pos // TILE_COLS) % tile_rows + tile_rows - 1
    return column_index, row_index


def reference(queries, keys, values, grad_out, bias_table, slot_tiles, live, buckets):
    scale = HEAD_DIM ** -0.5
    set_size = TILES_DEV + SLOTS
    column_width = 2 * TILE_COLS - 1
    row_width = 2 * (TILE // TILE_COLS) - 1
    column_index, row_index = offset_indices()
    column_table = bias_table[:, BUCKETS:BUCKETS + column_width]
    row_table = bias_table[:, BUCKETS + column_width:]
    fine_bias = column_table[:, column_index] + row_table[:, row_index]
    own_range = jnp.arange(TILES_DEV, dtype=jnp.int32)
    remote_flag = (jnp.arange(set_size, dtype=jnp.int32) >= TILES_DEV)[:, None, None]

    def one_window(arrays):
        query_all, key_all, value_all, upstream_all = arrays
        key_tiles = key_all.reshape(KEY_TILES, TILE, WIDTH)
        value_tiles = value_all.reshape(KEY_TILES, TILE, WIDTH)

        def one_tile(carry, index):
            key_grad, value_grad, table_grad = carry
            chosen = jnp.concatenate([index * TILES_DEV + own_range, slot_tiles[index].astype(jnp.int32)]).astype(jnp.int32)
            alive = live[index] > 0
            bucket_row = buckets[index].astype(jnp.int32)
            start = (index * TOK_DEV).astype(jnp.int32)
            query_block = lax.dynamic_slice_in_dim(query_all, start, TOK_DEV, 0).astype(jnp.float32).reshape(TOK_DEV, HEADS, HEAD_DIM)
            upstream = lax.dynamic_slice_in_dim(upstream_all, start, TOK_DEV, 0).astype(jnp.float32).reshape(TOK_DEV, HEADS, HEAD_DIM)
            key_set = key_tiles[chosen].astype(jnp.float32).reshape(set_size, TILE, HEADS, HEAD_DIM)
            value_set = value_tiles[chosen].astype(jnp.float32).reshape(set_size, TILE, HEADS, HEAD_DIM)
            coarse = bias_table[:, bucket_row]
            scores = jnp.einsum("qhd,skhd->hqsk", query_block, key_set) * scale
            scores = scores + coarse[:, None, :, None] + fine_bias[:, :, None, :]
            mask = alive[None, None, :, None]
            masked = jnp.where(mask, scores, NEGATIVE)
            top = jnp.max(masked, axis=(2, 3), keepdims=True)
            total = jnp.sum(jnp.where(mask, jnp.exp(masked - top), 0.0), axis=(2, 3), keepdims=True)
            log_total = top + jnp.log(total)
            attend = jnp.where(mask, jnp.exp(scores - log_total), 0.0)
            attend_grad = jnp.einsum("qhd,skhd->hqsk", upstream, value_set)
            delta = jnp.sum(attend * attend_grad, axis=(2, 3), keepdims=True)
            score_grad = attend * (attend_grad - delta)
            attend_low = rounded(attend)
            grad_low = rounded(score_grad)
            value_part = jnp.einsum("hqsk,qhd->skhd", attend_low, upstream).reshape(set_size, TILE, WIDTH)
            key_part = (jnp.einsum("hqsk,qhd->skhd", grad_low, query_block) * scale).reshape(set_size, TILE, WIDTH)
            value_part = jnp.where(remote_flag, rounded(value_part), value_part)
            key_part = jnp.where(remote_flag, rounded(key_part), key_part)
            query_grad = jnp.einsum("hqsk,skhd->qhd", grad_low, key_set) * scale
            block_sums = jnp.sum(score_grad, axis=(1, 3))
            fine_sum = jnp.sum(score_grad, axis=2)
            coarse_grad = jnp.zeros((HEADS, BUCKETS), jnp.float32).at[:, bucket_row].add(block_sums)
            column_grad = jnp.zeros((HEADS, column_width), jnp.float32).at[:, column_index].add(fine_sum)
            row_grad = jnp.zeros((HEADS, row_width), jnp.float32).at[:, row_index].add(fine_sum)
            table_grad = table_grad + jnp.concatenate([coarse_grad, column_grad, row_grad], axis=1)
            key_grad = key_grad.at[chosen].add(key_part)
            value_grad = value_grad.at[chosen].add(value_part)
            return (key_grad, value_grad, table_grad), query_grad.reshape(TOK_DEV, WIDTH).astype(jnp.bfloat16)

        start_state = (jnp.zeros((KEY_TILES, TILE, WIDTH), jnp.float32), jnp.zeros((KEY_TILES, TILE, WIDTH), jnp.float32), jnp.zeros((HEADS, TABLE), jnp.float32))
        final_state, query_rows = lax.scan(one_tile, start_state, jnp.arange(QUERY_TILES, dtype=jnp.int32))
        key_grad, value_grad, table_grad = final_state
        return (query_rows.reshape(LENGTH, WIDTH), key_grad.reshape(LENGTH, WIDTH).astype(jnp.bfloat16), value_grad.reshape(LENGTH, WIDTH).astype(jnp.bfloat16), table_grad)

    query_grad, key_grad, value_grad, table_grads = lax.map(one_window, (queries, keys, values, grad_out))
    return query_grad, key_grad, value_grad, jnp.sum(table_grads, axis=0)
```

```python
import functools

import jax
import jax.numpy as jnp
from jax import lax
from jax.experimental import pallas as pl
from jax.experimental.pallas import tpu as pltpu
from jax.sharding import PartitionSpec as P

HEADS = 24
HEAD_DIM = 128
TOK_DEV = 256
TILE = 128
TILE_COLS = 16
SLOTS = 5
BUCKETS = 82
WIDTH = 3072
TILES_DEV = 2
ENTRIES = TILES_DEV + SLOTS
TILE_ROWS = TILE // TILE_COLS
COLUMN_WIDTH = 2 * TILE_COLS - 1
ROW_WIDTH = 2 * TILE_ROWS - 1

NEGATIVE = -1e30
HIGHEST = lax.Precision.HIGHEST
NEAR_OFFSETS = (-1, 1, -2, 2)
LOG2E = 1.4426950408889634
SCALE = HEAD_DIM ** (-0.5)
VMEM_LIMIT = 40 * 1024 * 1024


def pack(arrays, first, heads, count):
    number = len(arrays)

    def body(*refs):
        out = refs[number]
        for a in range(number):
            for h in range(heads):
                out[0, a, h] = refs[a][:, h * HEAD_DIM : (h + 1) * HEAD_DIM]

    start = first // heads
    return pl.pallas_call(
        body,
        grid=(count,),
        in_specs=[
            pl.BlockSpec((TOK_DEV, heads * HEAD_DIM), lambda j: (0, start + j)) for _ in range(number)
        ],
        out_specs=pl.BlockSpec((1, number, heads, TOK_DEV, HEAD_DIM), lambda j: (j, 0, 0, 0, 0)),
        out_shape=jax.ShapeDtypeStruct((count, number, heads, TOK_DEV, HEAD_DIM), jnp.bfloat16),
        compiler_params=pltpu.CompilerParams(vmem_limit_bytes=VMEM_LIMIT),
        cost_estimate=pl.CostEstimate(
            flops=0,
            bytes_accessed=2 * 2 * count * number * heads * TOK_DEV * HEAD_DIM,
            transcendentals=0,
        ),
    )(*arrays)


def unpack(blocks, first, heads, count, onto):
    number = blocks.shape[1]
    held = 0 if onto is None else number

    def body(*refs):
        outs = refs[1 + held :]
        for a in range(number):
            for h in range(heads):
                outs[a][:, h * HEAD_DIM : (h + 1) * HEAD_DIM] = refs[0][0, a, h]

    start = first // heads
    in_specs = [pl.BlockSpec((1, number, heads, TOK_DEV, HEAD_DIM), lambda j: (j, 0, 0, 0, 0))]
    in_specs += [pl.BlockSpec(memory_space=pl.ANY)] * held
    return pl.pallas_call(
        body,
        grid=(count,),
        in_specs=in_specs,
        out_specs=[
            pl.BlockSpec((TOK_DEV, heads * HEAD_DIM), lambda j: (0, start + j)) for _ in range(number)
        ],
        out_shape=[jax.ShapeDtypeStruct((TOK_DEV, WIDTH), jnp.bfloat16) for _ in range(number)],
        input_output_aliases={1 + a: a for a in range(held)},
        compiler_params=pltpu.CompilerParams(vmem_limit_bytes=VMEM_LIMIT),
        cost_estimate=pl.CostEstimate(
            flops=0,
            bytes_accessed=2 * 2 * count * number * heads * TOK_DEV * HEAD_DIM,
            transcendentals=0,
        ),
    )(blocks, *(onto if onto is not None else ()))


def fold(array, combine):
    parts = [array[r : r + 8] for r in range(0, array.shape[0], 8)]
    while len(parts) > 1:
        parts = [combine(parts[2 * k], parts[2 * k + 1]) for k in range(len(parts) // 2)]
    return parts[0]


def grad_body(
    count,
    tiles_ref,
    coarse_ref,
    x_ref,
    bias_ref,
    out_ref,
    fine_ref,
    block_ref,
    score_ref,
    product_ref,
    low_ref,
    key_ref,
    key_grad_ref,
    value_grad_ref,
):
    head = pl.program_id(0)
    key_grad_ref[...] = jnp.zeros_like(key_grad_ref)
    value_grad_ref[...] = jnp.zeros_like(value_grad_ref)
    fine_ref[...] = jnp.zeros_like(fine_ref)
    transposed = (((1,), (1,)), ((), ()))

    @pl.loop(0, count)
    def _(i):
        query = x_ref[i, 0, 0]
        upstream = x_ref[i, 3, 0]
        tiles = [tiles_ref[i * ENTRIES + e] for e in range(ENTRIES)]
        coarse = [coarse_ref[head, i * ENTRIES + e] for e in range(ENTRIES)]
        top = None
        for e in range(ENTRIES):
            rows = pl.ds(pl.multiple_of((tiles[e] % TILES_DEV) * TILE, TILE), TILE)
            key = x_ref[tiles[e] // TILES_DEV, 1, 0, rows, :]
            key_ref[e * TILE : (e + 1) * TILE] = key
            raw = lax.dot_general(key, query, transposed, preferred_element_type=jnp.float32)
            score = raw * (SCALE * LOG2E) + bias_ref[0]
            score_ref[e] = score
            best = fold(score, jnp.maximum) + coarse[e]
            top = best if top is None else jnp.maximum(top, best)
        top = jnp.max(top, axis=0, keepdims=True)
        total = jnp.zeros((8, TOK_DEV), jnp.float32)
        weighted = jnp.zeros((8, TOK_DEV), jnp.float32)
        for e in range(ENTRIES):
            rows = pl.ds(pl.multiple_of((tiles[e] % TILES_DEV) * TILE, TILE), TILE)
            value = x_ref[tiles[e] // TILES_DEV, 2, 0, rows, :]
            product = lax.dot_general(value, upstream, transposed, preferred_element_type=jnp.float32)
            expo = jnp.exp2(score_ref[e] - (top - coarse[e]))
            score_ref[e] = expo
            product_ref[e] = product
            total = total + fold(expo, jnp.add)
            weighted = weighted + fold(expo * product, jnp.add)
        inverse = 1.0 / jnp.sum(total, axis=0, keepdims=True)
        delta = jnp.sum(weighted, axis=0, keepdims=True) * inverse
        for e in range(ENTRIES):
            attend = score_ref[e] * inverse
            grad = attend * (product_ref[e] - delta)
            fine_ref[0] += grad
            sums = fold(grad, jnp.add)
            block_ref[0, i * ENTRIES + e] = sums[:, :TILE] + sums[:, TILE:]
            grad_low = grad.astype(jnp.bfloat16)
            low_ref[e * TILE : (e + 1) * TILE] = grad_low
            value_grad_ref[tiles[e]] += jnp.dot(
                attend.astype(jnp.bfloat16), upstream, preferred_element_type=jnp.float32
            )
            key_grad_ref[tiles[e]] += jnp.dot(grad_low, query, preferred_element_type=jnp.float32)
        query_grad = lax.dot_general(
            key_ref[...], low_ref[...], (((0,), (0,)), ((), ())), preferred_element_type=jnp.float32
        )
        out_ref[i, 0, 0] = (query_grad.T * SCALE).astype(jnp.bfloat16)

    @pl.loop(0, count)
    def _(i):
        for t in range(TILES_DEV):
            rows = slice(t * TILE, (t + 1) * TILE)
            out_ref[i, 1, 0, rows] = (key_grad_ref[i * TILES_DEV + t] * SCALE).astype(jnp.bfloat16)
            out_ref[i, 2, 0, rows] = value_grad_ref[i * TILES_DEV + t].astype(jnp.bfloat16)


def window_grads(tiles, coarse, blocks, bias):
    count, _, heads = blocks.shape[:3]
    smem = pl.BlockSpec(memory_space=pltpu.SMEM)
    pairs = heads * count * ENTRIES * TILE * TOK_DEV
    return pl.pallas_call(
        functools.partial(grad_body, count),
        grid=(heads,),
        in_specs=[
            smem,
            smem,
            pl.BlockSpec((count, 4, 1, TOK_DEV, HEAD_DIM), lambda h: (0, 0, h, 0, 0)),
            pl.BlockSpec((1, TILE, TOK_DEV), lambda h: (h, 0, 0)),
        ],
        out_specs=[
            pl.BlockSpec((count, 3, 1, TOK_DEV, HEAD_DIM), lambda h: (0, 0, h, 0, 0)),
            pl.BlockSpec((1, TILE, TOK_DEV), lambda h: (h, 0, 0)),
            pl.BlockSpec((1, count * ENTRIES, 8, TILE), lambda h: (h, 0, 0, 0)),
        ],
        out_shape=[
            jax.ShapeDtypeStruct((count, 3, heads, TOK_DEV, HEAD_DIM), jnp.bfloat16),
            jax.ShapeDtypeStruct((heads, TILE, TOK_DEV), jnp.float32),
            jax.ShapeDtypeStruct((heads, count * ENTRIES, 8, TILE), jnp.float32),
        ],
        scratch_shapes=[
            pltpu.VMEM((ENTRIES, TILE, TOK_DEV), jnp.float32),
            pltpu.VMEM((ENTRIES, TILE, TOK_DEV), jnp.float32),
            pltpu.VMEM((ENTRIES * TILE, TOK_DEV), jnp.bfloat16),
            pltpu.VMEM((ENTRIES * TILE, HEAD_DIM), jnp.bfloat16),
            pltpu.VMEM((count * TILES_DEV, TILE, HEAD_DIM), jnp.float32),
            pltpu.VMEM((count * TILES_DEV, TILE, HEAD_DIM), jnp.float32),
        ],
        compiler_params=pltpu.CompilerParams(vmem_limit_bytes=VMEM_LIMIT),
        cost_estimate=pl.CostEstimate(
            flops=10 * pairs * HEAD_DIM, bytes_accessed=2 * blocks.size * 2, transcendentals=pairs
        ),
    )(tiles, coarse, blocks, bias)


def fine_bias_of(columns, rows):
    heads = columns.shape[0]
    column = jnp.stack(
        [columns[:, TILE_COLS - 1 - a : 2 * TILE_COLS - 1 - a] for a in range(TILE_COLS)], axis=2
    )
    row = jnp.stack(
        [rows[:, TILE_ROWS - 1 - a : 2 * TILE_ROWS - 1 - a] for a in range(TILE_ROWS)], axis=2
    )
    row = jnp.tile(row, (1, 1, TOK_DEV // TILE))
    column = jnp.tile(column, (1, TILE_ROWS, TOK_DEV // TILE_COLS))
    row = jnp.repeat(jnp.repeat(row, TILE_COLS, axis=1), TILE_COLS, axis=2)
    return (column + row).reshape(heads, TILE, TOK_DEV)


def table_grad_of(fine, blocks, bucket_hot):
    heads = fine.shape[0]
    coarse = jnp.dot(jnp.sum(blocks, axis=(2, 3)), bucket_hot, precision=HIGHEST)
    groups = TOK_DEV // TILE
    split = fine.reshape(heads, TILE_ROWS, TILE_COLS, groups, TILE_ROWS, TILE_COLS)
    column = jnp.sum(split, axis=(1, 3, 4)).reshape(heads, -1)
    row = jnp.sum(split, axis=(2, 3, 5)).reshape(heads, -1)

    def hot(size):
        at = jnp.arange(size, dtype=jnp.int32)
        offset = (at[:, None] - at[None, :] + size - 1).reshape(-1, 1)
        return (offset == jnp.arange(2 * size - 1, dtype=jnp.int32)[None, :]).astype(jnp.float32)

    column = jnp.dot(column, hot(TILE_COLS), precision=HIGHEST)
    row = jnp.dot(row, hot(TILE_ROWS), precision=HIGHEST)
    return jnp.concatenate([coarse, column, row], axis=1)


def by_heads(queries, keys, values, grad_out, bias_table, slot_tiles, live, buckets):
    count = lax.axis_size("seq")
    position = lax.axis_index("seq")
    each = HEADS // count
    chunks = [each - each // 3, each // 3]
    starts = [0, chunks[0] * count]
    arrays = (queries[0], keys[0], values[0], grad_out[0])

    def to_heads(array):
        return lax.all_to_all(array, "seq", 0, 0)

    received = [to_heads(pack(arrays, first, heads, count)) for first, heads in zip(starts, chunks)]

    table = lax.all_gather(bias_table, "dp", axis=0, tiled=True)
    both = lax.all_gather(jnp.concatenate([live, buckets], axis=1), "seq", axis=0, tiled=True)
    alive = both[:, :ENTRIES].reshape(-1) > 0
    bucket_hot = (
        both[:, ENTRIES:].reshape(-1, 1) == jnp.arange(BUCKETS, dtype=jnp.int32)[None, :]
    ).astype(jnp.float32)
    own = jnp.arange(count * TILES_DEV, dtype=jnp.int32).reshape(count, TILES_DEV)
    tiles = jnp.concatenate([own, slot_tiles], axis=1).reshape(-1)

    outs = None
    table_grad = jnp.zeros((HEADS, bias_table.shape[1]), jnp.float32)
    for first, heads, blocks in zip(starts, chunks, received):
        row = first + position * heads
        part = lax.dynamic_slice_in_dim(table, row, heads, 0)
        coarse = jnp.sum(part[:, None, :BUCKETS] * bucket_hot[None], axis=2) * LOG2E
        coarse = jnp.where(alive[None, :], coarse, NEGATIVE)
        bias = fine_bias_of(
            part[:, BUCKETS : BUCKETS + COLUMN_WIDTH], part[:, BUCKETS + COLUMN_WIDTH :]
        )
        grads, fine, sums = window_grads(tiles, coarse, blocks, bias * LOG2E)
        outs = unpack(to_heads(grads), first, heads, count, outs)
        table_grad = lax.dynamic_update_slice_in_dim(
            table_grad, table_grad_of(fine, sums, bucket_hot), row, 0
        )
    summed = lax.psum(table_grad, ("seq", "dp"))
    rows = bias_table.shape[0]
    table_out = lax.dynamic_slice_in_dim(summed, lax.axis_index("dp") * rows, rows, 0)
    return (outs[0][None], outs[1][None], outs[2][None], table_out)


def from_behind(block, axis, distance):
    devices = range(lax.axis_size(axis))
    route = [(i - distance, i) for i in devices if i - distance in devices]
    return lax.ppermute(block, axis, route)


def from_behind_2(value, axis, by):
    count = lax.axis_size(axis)
    return lax.ppermute(value, axis, [(i, (i + by) % count) for i in range(count)])


def offset_hots():
    tile_rows = TILE // TILE_COLS
    query_pos = jnp.arange(TOK_DEV, dtype=jnp.int32)[:, None]
    key_pos = jnp.arange(TILE, dtype=jnp.int32)[None, :]
    column_index = key_pos % TILE_COLS - query_pos % TILE_COLS + TILE_COLS - 1
    row_index = key_pos // TILE_COLS - query_pos // TILE_COLS % tile_rows + tile_rows - 1
    column_hot = (
        column_index.reshape(1, -1) == jnp.arange(2 * TILE_COLS - 1, dtype=jnp.int32)[:, None]
    ).astype(jnp.float32)
    row_hot = (
        row_index.reshape(1, -1) == jnp.arange(2 * tile_rows - 1, dtype=jnp.int32)[:, None]
    ).astype(jnp.float32)
    return (column_hot, row_hot)


def by_tiles(queries, keys, values, grad_out, bias_table, slot_tiles, live, buckets):
    axis_size = lax.axis_size("seq")
    position = lax.axis_index("seq")
    half = axis_size // 2
    scale = HEAD_DIM ** (-0.5)
    column_width = 2 * TILE_COLS - 1
    table = lax.all_gather(bias_table, "dp", axis=0, tiled=True)
    column_hot, row_hot = offset_hots()
    fine_bias = jnp.dot(table[:, BUCKETS : BUCKETS + column_width], column_hot, precision=HIGHEST)
    fine_bias = fine_bias + jnp.dot(table[:, BUCKETS + column_width :], row_hot, precision=HIGHEST)
    fine_bias = fine_bias.reshape(HEADS, TOK_DEV, TILE)
    bucket_hot = (buckets[0][:, None] == jnp.arange(BUCKETS, dtype=jnp.int32)[None, :]).astype(
        jnp.float32
    )
    coarse = jnp.dot(bucket_hot, table[:, :BUCKETS].T, precision=HIGHEST)
    alive = live[0].astype(jnp.float32)
    query_heads = queries[0].reshape(TOK_DEV, HEADS, HEAD_DIM)
    upstream_heads = grad_out[0].reshape(TOK_DEV, HEADS, HEAD_DIM)
    own_pairs = jnp.stack(
        [keys[0].reshape(TILES_DEV, TILE, WIDTH), values[0].reshape(TILES_DEV, TILE, WIDTH)], axis=1
    )

    def requested(slot, requester):
        wanted = jnp.clip(slot_tiles[requester, slot] - position * TILES_DEV, 0, TILES_DEV - 1)
        return lax.dynamic_index_in_dim(own_pairs, wanted, 0, keepdims=False)

    fetched = []
    for slot, offset in enumerate(NEAR_OFFSETS):
        requester = jnp.clip(position - offset, 0, axis_size - 1)
        fetched.append(from_behind(requested(slot, requester), "seq", -offset))
    far_requester = (position + half) % axis_size
    fetched.append(from_behind_2(requested(SLOTS - 1, far_requester), "seq", half))
    remote_pairs = jnp.stack(fetched)
    own_group = (own_pairs, coarse[:TILES_DEV], alive[:TILES_DEV])
    remote_group = (remote_pairs, coarse[TILES_DEV:], alive[TILES_DEV:])

    def scores_of(pair, coarse_row):
        key_heads = pair[0].reshape(TILE, HEADS, HEAD_DIM)
        raw = jnp.einsum("qhd,khd->hqk", query_heads, key_heads, preferred_element_type=jnp.float32)
        return raw * scale + coarse_row[:, None, None] + fine_bias

    def products_of(pair):
        value_heads = pair[1].reshape(TILE, HEADS, HEAD_DIM)
        return jnp.einsum(
            "qhd,khd->hqk", upstream_heads, value_heads, preferred_element_type=jnp.float32
        )

    def stats_step(carry, item):
        top, total, weighted = carry
        pair, coarse_row, flag = item
        scores = scores_of(pair, coarse_row)
        attend_grad = products_of(pair)
        keep = flag > 0
        new_top = jnp.where(keep, jnp.maximum(top, jnp.max(scores, axis=2, keepdims=True)), top)
        factor = jnp.exp(top - new_top)
        expo = jnp.exp(scores - new_top) * flag
        added = jnp.sum(expo, axis=2, keepdims=True)
        added_weighted = jnp.sum(expo * attend_grad, axis=2, keepdims=True)
        return ((new_top, total * factor + added, weighted * factor + added_weighted), None)

    stats = (
        jnp.full((HEADS, TOK_DEV, 1), NEGATIVE, jnp.float32),
        jnp.zeros((HEADS, TOK_DEV, 1), jnp.float32),
        jnp.zeros((HEADS, TOK_DEV, 1), jnp.float32),
    )
    stats, _ = lax.scan(stats_step, stats, own_group)
    stats, _ = lax.scan(stats_step, stats, remote_group)
    log_total = stats[0] + jnp.log(stats[1])
    delta = stats[2] / stats[1]

    def grad_step(carry, item):
        query_grad, fine_sum = carry
        pair, coarse_row, flag = item
        scores = scores_of(pair, coarse_row)
        attend = jnp.exp(scores - log_total) * flag
        attend_grad = products_of(pair)
        score_grad = attend * (attend_grad - delta)
        attend_low = attend.astype(jnp.bfloat16)
        grad_low = score_grad.astype(jnp.bfloat16)
        key_heads = pair[0].reshape(TILE, HEADS, HEAD_DIM)
        value_part = jnp.einsum(
            "hqk,qhd->khd", attend_low, upstream_heads, preferred_element_type=jnp.float32
        ).reshape(TILE, WIDTH)
        key_part = (
            jnp.einsum(
                "hqk,qhd->khd", grad_low, query_heads, preferred_element_type=jnp.float32
            ).reshape(TILE, WIDTH)
            * scale
        )
        query_grad = (
            query_grad
            + jnp.einsum("hqk,khd->qhd", grad_low, key_heads, preferred_element_type=jnp.float32)
            * scale
        )
        return (
            (query_grad, fine_sum + score_grad),
            (key_part, value_part, jnp.sum(score_grad, axis=(1, 2))),
        )

    carry = (
        jnp.zeros((TOK_DEV, HEADS, HEAD_DIM), jnp.float32),
        jnp.zeros((HEADS, TOK_DEV, TILE), jnp.float32),
    )
    carry, own_out = lax.scan(grad_step, carry, own_group)
    carry, remote_out = lax.scan(grad_step, carry, remote_group)
    query_grad, fine_sum = carry
    remote_low = jnp.stack([remote_out[0], remote_out[1]], axis=1).astype(jnp.bfloat16)

    def deposit(totals, slot, requester, arrived, weight):
        wanted = jnp.clip(slot_tiles[requester, slot] - position * TILES_DEV, 0, TILES_DEV - 1)
        pick = (jnp.arange(TILES_DEV, dtype=jnp.int32) == wanted).astype(jnp.float32)[
            :, None, None
        ] * weight
        return (
            totals[0] + pick * arrived[0].astype(jnp.float32)[None],
            totals[1] + pick * arrived[1].astype(jnp.float32)[None],
        )

    totals = (own_out[0], own_out[1])
    for slot, offset in enumerate(NEAR_OFFSETS):
        arrived = from_behind(remote_low[slot], "seq", offset)
        requester = jnp.clip(position - offset, 0, axis_size - 1)
        totals = deposit(totals, slot, requester, arrived, 1.0)
    arrived = from_behind_2(remote_low[SLOTS - 1], "seq", half)
    totals = deposit(totals, SLOTS - 1, (position + half) % axis_size, arrived, 1.0)
    block_sums = jnp.concatenate([own_out[2], remote_out[2]], axis=0)
    coarse_grad = jnp.dot(block_sums.T, bucket_hot, precision=HIGHEST)
    flat_sum = fine_sum.reshape(HEADS, TOK_DEV * TILE)
    column_grad = jnp.dot(flat_sum, column_hot.T, precision=HIGHEST)
    row_grad = jnp.dot(flat_sum, row_hot.T, precision=HIGHEST)
    table_grad = jnp.concatenate([coarse_grad, column_grad, row_grad], axis=1)
    summed = lax.psum(table_grad, "seq")
    table_out = lax.psum_scatter(summed, "dp", scatter_dimension=0, tiled=True)
    query_out = query_grad.reshape(1, TOK_DEV, WIDTH).astype(jnp.bfloat16)
    key_out = totals[0].reshape(1, TOK_DEV, WIDTH).astype(jnp.bfloat16)
    value_out = totals[1].reshape(1, TOK_DEV, WIDTH).astype(jnp.bfloat16)
    return (query_out, key_out, value_out, table_out)


def solution(mesh):
    plan = by_heads if HEADS % mesh.shape["seq"] == 0 else by_tiles
    return jax.shard_map(
        plan,
        mesh=mesh,
        in_specs=(
            P("dp", "seq", None),
            P("dp", "seq", None),
            P("dp", "seq", None),
            P("dp", "seq", None),
            P("dp", None),
            P(),
            P("seq", None),
            P("seq", None),
        ),
        out_specs=(P("dp", "seq", None), P("dp", "seq", None), P("dp", "seq", None), P("dp", None)),
        check_vma=False,
    )
```

```python
import functools

import jax
import jax.numpy as jnp
from jax import lax
from jax.experimental import pallas as pl
from jax.experimental.pallas import tpu as pltpu
from jax.sharding import PartitionSpec as P

HEADS = 24
HEAD_DIM = 128
TOK_DEV = 256
TILE = 128
TILE_COLS = 16
SLOTS = 5
BUCKETS = 82
WIDTH = 3072
TILES_DEV = 2
ENTRIES = TILES_DEV + SLOTS
TILE_ROWS = TILE // TILE_COLS
COLUMN_WIDTH = 2 * TILE_COLS - 1
ROW_WIDTH = 2 * TILE_ROWS - 1

NEGATIVE = -1e30
HIGHEST = lax.Precision.HIGHEST
NEAR_OFFSETS = (-1, 1, -2, 2)
LOG2E = 1.4426950408889634
SCALE = HEAD_DIM ** (-0.5)
VMEM_LIMIT = 56 * 1024 * 1024


SIZES = (2, 4, 5, ENTRIES)
ABSOLUTE = 1 << 16
STAMP = 32
META = 16
HBM = pl.BlockSpec(memory_space=pltpu.HBM)
SMEM = pl.BlockSpec(memory_space=pltpu.SMEM)


def pack_body(number, heads, first, count, targets, *refs):
    place_ref, live_ref, bucket_ref = refs[:3]
    arrays = refs[3 : 3 + number]
    outs = refs[3 + number : -4]
    held_ref, meta_ref, in_sem, out_sem = refs[-4:]
    width = heads * HEAD_DIM
    position = place_ref[0]
    span = pl.ds(first * HEAD_DIM, count * width)
    arriving = [
        pltpu.make_async_copy(arrays[a].at[:, span], held_ref.at[a], in_sem.at[a])
        for a in range(number)
    ]
    for copy in arriving:
        copy.start()
    row = lax.broadcasted_iota(jnp.int32, (META, width), 0)
    lane = lax.broadcasted_iota(jnp.int32, (META, width), 1)
    meta = jnp.zeros((META, width), jnp.int32)
    for e in range(ENTRIES):
        meta = jnp.where((row == e) & (lane == 0), bucket_ref[0, e], meta)
        meta = jnp.where((row == e) & (lane == 1), live_ref[0, e], meta)
    meta_ref[...] = meta.astype(jnp.float32).astype(jnp.bfloat16)
    columns, messages = [], []
    for k, (out, at) in targets.items():
        column = (k - ABSOLUTE) * width if k >= ABSOLUTE else (position ^ k) * width
        columns.append(column if k >= ABSOLUTE else pl.multiple_of(column, HEAD_DIM))
        messages.append(outs[out] if at is None else outs[out].at[at])
    leaving = [
        pltpu.make_async_copy(meta_ref, message.at[pl.ds(number * TOK_DEV, META)], out_sem)
        for message in messages
    ]
    for copy in leaving:
        copy.start()
    for a in range(number):
        arriving[a].wait()
        for message, column in zip(messages, columns):
            leaving.append(
                pltpu.make_async_copy(
                    held_ref.at[a, :, pl.ds(column, width)],
                    message.at[pl.ds(a * TOK_DEV, TOK_DEV)],
                    out_sem,
                )
            )
            leaving[-1].start()
    for copy in leaving:
        copy.wait()


def pack(place, live, buckets, arrays, first, heads, count, targets, sizes):
    number = len(arrays)
    rows = number * TOK_DEV + META
    width = heads * HEAD_DIM
    return pl.pallas_call(
        functools.partial(pack_body, number, heads, first, count, targets),
        in_specs=[SMEM] * 3 + [HBM] * number,
        out_specs=[HBM] * len(sizes),
        out_shape=[
            jax.ShapeDtypeStruct((() if size is None else (size,)) + (rows, width), jnp.bfloat16)
            for size in sizes
        ],
        scratch_shapes=[
            pltpu.VMEM((number, TOK_DEV, count * width), jnp.bfloat16),
            pltpu.VMEM((META, width), jnp.bfloat16),
            pltpu.SemaphoreType.DMA((number,)),
            pltpu.SemaphoreType.DMA,
        ],
        compiler_params=pltpu.CompilerParams(vmem_limit_bytes=VMEM_LIMIT),
        cost_estimate=pl.CostEstimate(
            flops=0, bytes_accessed=4 * count * rows * width, transcendentals=0
        ),
    )(place, live, buckets, *arrays)


def unpack_body(number, heads, first, count, held, owned, *refs):
    place_ref = refs[0]
    pairs = count // 2
    blocks = [refs[1 + k // 2].at[k % 2] for k in range(count)]
    outs = refs[1 + pairs + held : 1 + pairs + held + number]
    scratch = refs[1 + pairs + held + number :]
    if owned:
        table_ref, held_ref, in_sem, out_sem, stamp_ref, whole_ref, stamp_sem = scratch
        stamps = [
            pltpu.make_async_copy(
                blocks[k].at[pl.ds(number * TOK_DEV, STAMP)], stamp_ref.at[k], stamp_sem
            )
            for k in range(count)
        ]
    else:
        held_ref, in_sem, out_sem = scratch
    width = heads * HEAD_DIM
    position = place_ref[0]
    arriving = []
    for a in range(number):
        for k in range(count):
            column = pl.multiple_of((position ^ k) * width, HEAD_DIM)
            arriving.append(
                pltpu.make_async_copy(
                    blocks[k].at[pl.ds(a * TOK_DEV, TOK_DEV)],
                    held_ref.at[a, :, pl.ds(column, width)],
                    in_sem.at[a],
                )
            )
            arriving[-1].start()
    if owned:
        for copy in stamps:
            copy.start()
    leaving = []
    for a in range(number):
        for copy in arriving[a * count : (a + 1) * count]:
            copy.wait()
        leaving.append(
            pltpu.make_async_copy(
                held_ref.at[a],
                outs[a].at[:, pl.ds(first * HEAD_DIM, count * width)],
                out_sem,
            )
        )
        leaving[-1].start()
    if owned:
        for copy in stamps:
            copy.wait()
        each = HEADS // count
        for k in range(count):
            parts = stamp_ref[k].astype(jnp.float32)
            rows = parts[0:each] + parts[each : 2 * each] + parts[2 * each : 3 * each]
            source = position ^ k
            for r in range(each):
                head = source * (each - heads) + r if r < each - heads else first + source * heads + r - (each - heads)
                whole_ref[pl.ds(head, 1)] = rows[r : r + 1]
        for r in range(owned):
            table_ref[r : r + 1] = whole_ref[pl.ds(place_ref[1] * owned + r, 1)]
    for copy in leaving:
        copy.wait()


def unpack(place, blocks, number, first, heads, onto, owned):
    pairs = len(blocks)
    count = 2 * pairs
    held = 0 if onto is None else number
    out_specs = [HBM] * number
    out_shape = [jax.ShapeDtypeStruct((TOK_DEV, WIDTH), jnp.bfloat16)] * number
    scratch_shapes = [
        pltpu.VMEM((number, TOK_DEV, count * heads * HEAD_DIM), jnp.bfloat16),
        pltpu.SemaphoreType.DMA((number,)),
        pltpu.SemaphoreType.DMA,
    ]
    if owned:
        out_specs = out_specs + [pl.BlockSpec(memory_space=pltpu.VMEM)]
        out_shape = out_shape + [jax.ShapeDtypeStruct((owned, TILE), jnp.float32)]
        scratch_shapes += [
            pltpu.VMEM((count, STAMP, heads * HEAD_DIM), jnp.bfloat16),
            pltpu.VMEM((HEADS, TILE), jnp.float32),
            pltpu.SemaphoreType.DMA,
        ]
    return pl.pallas_call(
        functools.partial(unpack_body, number, heads, first, count, held, owned),
        in_specs=[SMEM] + [HBM] * (pairs + held),
        out_specs=out_specs,
        out_shape=out_shape,
        input_output_aliases={1 + pairs + a: a for a in range(held)},
        scratch_shapes=scratch_shapes,
        compiler_params=pltpu.CompilerParams(vmem_limit_bytes=VMEM_LIMIT),
        cost_estimate=pl.CostEstimate(
            flops=0, bytes_accessed=4 * count * number * TOK_DEV * heads * HEAD_DIM, transcendentals=0
        ),
    )(place, *blocks, *(onto if onto is not None else ()))


def merge_body(pairs, rows, stamped, *refs):
    cross_ref = refs[0]
    outs = refs[1 + stamped + pairs : 1 + stamped + 2 * pairs]
    held_ref, low_ref, in_sem, out_sem = refs[1 + stamped + 2 * pairs :]
    arriving = [
        pltpu.make_async_copy(
            cross_ref.at[d], held_ref.at[d, pl.ds(0, rows)], in_sem.at[d]
        )
        for d in range(pairs)
    ]
    for copy in arriving:
        copy.start()
    leaving = []
    if stamped:
        low_ref[...] = jnp.zeros_like(low_ref)
        for s in range(2):
            rest = refs[1][s]
            number = rest.shape[0]
            for part in range(3):
                low = rest.astype(jnp.bfloat16).astype(jnp.float32)
                low_ref[s, part * number : (part + 1) * number] = low
                rest = rest - low
        whole = low_ref[...].astype(jnp.bfloat16)
        held_ref[0:2, rows : rows + STAMP] = whole
        for d in range(pairs):
            leaving += [
                pltpu.make_async_copy(
                    held_ref.at[s, pl.ds(rows, STAMP)], outs[d].at[s, pl.ds(rows, STAMP)], out_sem
                )
                for s in range(2)
            ]
            leaving[-2].start()
            leaving[-1].start()
    for d in range(pairs):
        arriving[d].wait()
        leaving.append(
            pltpu.make_async_copy(
                held_ref.at[d, pl.ds(0, rows)], outs[d].at[1, pl.ds(0, rows)], out_sem
            )
        )
        leaving[-1].start()
    for copy in leaving:
        copy.wait()


def merge(cross, messages, table_rows):
    pairs, rows, width = cross.shape
    stamped = 0 if table_rows is None else 1
    shape = messages[0].shape
    return pl.pallas_call(
        functools.partial(merge_body, pairs, rows, stamped),
        in_specs=[HBM] + [pl.BlockSpec(memory_space=pltpu.VMEM)] * stamped + [HBM] * pairs,
        out_specs=[HBM] * pairs,
        out_shape=[jax.ShapeDtypeStruct(shape, jnp.bfloat16)] * pairs,
        input_output_aliases={1 + stamped + d: d for d in range(pairs)},
        scratch_shapes=[
            pltpu.VMEM((pairs,) + shape[1:], jnp.bfloat16),
            pltpu.VMEM((2, STAMP, TILE), jnp.float32),
            pltpu.SemaphoreType.DMA((pairs,)),
            pltpu.SemaphoreType.DMA,
        ],
        compiler_params=pltpu.CompilerParams(vmem_limit_bytes=VMEM_LIMIT),
        cost_estimate=pl.CostEstimate(
            flops=0, bytes_accessed=4 * cross.size, transcendentals=0
        ),
    )(cross, *(() if table_rows is None else (table_rows,)), *messages)


def fold(array, combine):
    parts = [array[r : r + 8] for r in range(0, array.shape[0], 8)]
    while len(parts) > 1:
        parts = [combine(parts[2 * k], parts[2 * k + 1]) for k in range(len(parts) // 2)]
    return parts[0]


def grad_body(count, heads, sources, *refs):
    place_ref, slots_ref, table_ref, bias_ref = refs[:4]
    refs = refs[4:]
    inputs = 1 + max(source for source, _ in sources.values())
    blocks, refs = refs[:inputs], refs[inputs:]
    cross_ref, refs = refs[0], refs[1:]
    pairs, refs = refs[: count // 2], refs[count // 2 :]
    outs = [(pairs[k // 2].at[0], cross_ref.at[k // 2])[k % 2] for k in range(count)]
    fine_ref, coarse_out_ref = refs[:2]
    (
        x_ref,
        y_ref,
        coarse_ref,
        sums_ref,
        score_ref,
        product_ref,
        low_ref,
        key_ref,
        key_grad_ref,
        value_grad_ref,
        in_sem,
        out_sem,
        list_ref,
        tile_ref,
        number_ref,
    ) = refs[2:]
    position = place_ref[0]

    def lanes(h):
        return pl.ds(h * HEAD_DIM, HEAD_DIM)

    arriving = []
    for h in range(heads):
        arriving.append([])
        for k, (source, at) in sources.items():
            block = blocks[source] if at is None else blocks[source].at[at]
            tile = k - ABSOLUTE if k >= ABSOLUTE else position ^ k
            arriving[h].append(
                pltpu.make_async_copy(
                    block.at[:, lanes(h)], x_ref.at[tile, :, lanes(h)], in_sem.at[h]
                )
            )
    leaving = [
        pltpu.make_async_copy(
            y_ref.at[position ^ k, :, lanes(h)],
            outs[k].at[pl.ds(0, 3 * TOK_DEV), lanes(h)],
            out_sem,
        )
        for h in range(heads)
        for k in range(count)
    ]
    for copies in arriving:
        for copy in copies:
            copy.start()
    lane = lax.broadcasted_iota(jnp.int32, (8, TILE), 1)
    transposed = (((1,), (1,)), ((), ()))

    def array_rows(a, begin=0, size=TOK_DEV):
        return pl.ds(a * TOK_DEV + begin, size)

    def meta_of(i):
        meta = x_ref[i, 4 * TOK_DEV : 4 * TOK_DEV + META, 0:TILE].astype(jnp.float32)[:8]
        hot = (lane == meta[:, 0:1].astype(jnp.int32)).astype(jnp.float32)
        return hot, meta[:, 1:2]

    def list_live(i, flag):
        row = lax.broadcasted_iota(jnp.int32, (8, 1), 0)
        code = jnp.sum(jnp.where(flag > 0, 1 << row, 0).astype(jnp.float32)).astype(jnp.int32)
        for e in range(8):
            list_ref[i * 8 + e] = ENTRIES
            tile_ref[i * 8 + e] = (
                slots_ref[i, e - TILES_DEV]
                if TILES_DEV <= e < ENTRIES
                else i * TILES_DEV + e % TILES_DEV
            )
        number = jnp.int32(0)
        for e in range(ENTRIES):
            list_ref[i * 8 + number] = e
            number = number + ((code >> e) & 1)
        list_ref[i * 8 + number] = ENTRIES
        number_ref[i] = number

    for h in range(heads):
        columns = slice(h * HEAD_DIM, (h + 1) * HEAD_DIM)
        key_grad_ref[...] = jnp.zeros_like(key_grad_ref)
        value_grad_ref[...] = jnp.zeros_like(value_grad_ref)
        fine_ref[h] = jnp.zeros_like(fine_ref[h])
        for copy in arriving[h]:
            copy.wait()
        sums_ref[...] = jnp.zeros_like(sums_ref)
        for i in range(count):
            hot, flag = meta_of(i)
            if h == 0:
                list_live(i, flag)
            coarse = jnp.sum(hot * table_ref[h : h + 1, :], axis=1, keepdims=True) * LOG2E
            coarse = jnp.where(flag > 0, coarse, NEGATIVE)
            coarse_ref[i] = jnp.broadcast_to(coarse, (8, TOK_DEV))

        def query_tile(i, size):
            query = x_ref[i, array_rows(0), columns]
            upstream = x_ref[i, array_rows(3), columns]
            entries = [list_ref[i * 8 + s] for s in range(size)]
            tiles = [tile_ref[i * 8 + e] for e in entries]
            coarse = [coarse_ref[i, pl.ds(e, 1)] for e in entries]

            def tile_of(a, s):
                begin = pl.multiple_of(a * TOK_DEV + (tiles[s] % TILES_DEV) * TILE, TILE)
                return x_ref[tiles[s] // TILES_DEV, pl.ds(begin, TILE), columns]

            top = None
            for s in range(size):
                key = tile_of(1, s)
                key_ref[s * TILE : (s + 1) * TILE] = key
                raw = lax.dot_general(key, query, transposed, preferred_element_type=jnp.float32)
                score = raw * (SCALE * LOG2E) + bias_ref[h]
                score_ref[s] = score
                best = fold(score, jnp.maximum) + coarse[s]
                top = best if top is None else jnp.maximum(top, best)
            top = jnp.max(top, axis=0, keepdims=True)
            total = jnp.zeros((8, TOK_DEV), jnp.float32)
            weighted = jnp.zeros((8, TOK_DEV), jnp.float32)
            for s in range(size):
                product = lax.dot_general(
                    tile_of(2, s), upstream, transposed, preferred_element_type=jnp.float32
                )
                expo = jnp.exp2(score_ref[s] - (top - coarse[s]))
                score_ref[s] = expo
                product_ref[s] = product
                total = total + fold(expo, jnp.add)
                weighted = weighted + fold(expo * product, jnp.add)
            inverse = 1.0 / jnp.sum(total, axis=0, keepdims=True)
            delta = jnp.sum(weighted, axis=0, keepdims=True) * inverse
            for s in range(size):
                attend = score_ref[s] * inverse
                grad = attend * (product_ref[s] - delta)
                fine_ref[h] += grad
                sums = jnp.sum(fold(grad, jnp.add), axis=0, keepdims=True)
                sums_ref[i, pl.ds(entries[s], 1)] = sums[:, :TILE] + sums[:, TILE:]
                grad_low = grad.astype(jnp.bfloat16)
                low_ref[s * TILE : (s + 1) * TILE] = grad_low
                value_grad_ref[tiles[s]] += jnp.dot(
                    attend.astype(jnp.bfloat16), upstream, preferred_element_type=jnp.float32
                )
                key_grad_ref[tiles[s]] += jnp.dot(
                    grad_low, query, preferred_element_type=jnp.float32
                )
            query_grad = lax.dot_general(
                key_ref[: size * TILE],
                low_ref[: size * TILE],
                (((0,), (0,)), ((), ())),
                preferred_element_type=jnp.float32,
            )
            y_ref[i, array_rows(0), columns] = (query_grad.T * SCALE).astype(jnp.bfloat16)

        @pl.loop(0, count)
        def _(i):
            number = number_ref[i]
            below = 0
            for size in SIZES:
                pl.when((number > below) & (number <= size))(
                    functools.partial(query_tile, i, size)
                )
                below = size

        coarse_grad = jnp.zeros((1, TILE), jnp.float32)
        for i in range(count):
            hot, _ = meta_of(i)
            sums = jnp.sum(sums_ref[i], axis=1, keepdims=True)
            real = lax.broadcasted_iota(jnp.int32, (8, 1), 0) < ENTRIES
            spread = hot * jnp.where(real, sums, 0.0)
            coarse_grad = coarse_grad + jnp.sum(spread, axis=0, keepdims=True)
        coarse_out_ref[h : h + 1] = coarse_grad

        @pl.loop(0, count)
        def _(i):
            for t in range(TILES_DEV):
                tile = i * TILES_DEV + t
                y_ref[i, array_rows(1, t * TILE, TILE), columns] = (
                    key_grad_ref[tile] * SCALE
                ).astype(jnp.bfloat16)
                y_ref[i, array_rows(2, t * TILE, TILE), columns] = value_grad_ref[tile].astype(
                    jnp.bfloat16
                )

        for copy in leaving[h * count : (h + 1) * count]:
            copy.start()

    for copy in leaving:
        copy.wait()


def window_grads(place, slots, table, bias, blocks, sources, count, more):
    heads = table.shape[0]
    width = heads * HEAD_DIM
    rows = 3 * TOK_DEV
    pairs = count // 2
    work = heads * count * ENTRIES * TILE * TOK_DEV
    vmem = pl.BlockSpec(memory_space=pltpu.VMEM)
    results = pl.pallas_call(
        functools.partial(grad_body, count, heads, sources),
        in_specs=[SMEM, SMEM, vmem, vmem] + [HBM] * len(blocks),
        out_specs=[HBM] * (1 + pairs) + [vmem] * 2,
        out_shape=[jax.ShapeDtypeStruct((pairs, rows, width), jnp.bfloat16)]
        + [jax.ShapeDtypeStruct((2, rows + more, width), jnp.bfloat16)] * pairs
        + [
            jax.ShapeDtypeStruct((heads, TILE, TOK_DEV), jnp.float32),
            jax.ShapeDtypeStruct((heads, TILE), jnp.float32),
        ],
        scratch_shapes=[
            pltpu.VMEM((count, 4 * TOK_DEV + META, width), jnp.bfloat16),
            pltpu.VMEM((count, rows, width), jnp.bfloat16),
            pltpu.VMEM((count, 8, TOK_DEV), jnp.float32),
            pltpu.VMEM((count, 8, TILE), jnp.float32),
            pltpu.VMEM((ENTRIES, TILE, TOK_DEV), jnp.float32),
            pltpu.VMEM((ENTRIES, TILE, TOK_DEV), jnp.float32),
            pltpu.VMEM((ENTRIES * TILE, TOK_DEV), jnp.bfloat16),
            pltpu.VMEM((ENTRIES * TILE, HEAD_DIM), jnp.bfloat16),
            pltpu.VMEM((count * TILES_DEV, TILE, HEAD_DIM), jnp.float32),
            pltpu.VMEM((count * TILES_DEV, TILE, HEAD_DIM), jnp.float32),
            pltpu.SemaphoreType.DMA((heads,)),
            pltpu.SemaphoreType.DMA,
            pltpu.SMEM((count * 8,), jnp.int32),
            pltpu.SMEM((count * 8,), jnp.int32),
            pltpu.SMEM((count,), jnp.int32),
        ],
        compiler_params=pltpu.CompilerParams(vmem_limit_bytes=VMEM_LIMIT),
        cost_estimate=pl.CostEstimate(
            flops=10 * work * HEAD_DIM,
            bytes_accessed=2 * 7 * count * TOK_DEV * width,
            transcendentals=work,
        ),
    )(place, slots, table, bias, *blocks)
    return results[0], list(results[1 : 1 + pairs]), results[1 + pairs], results[2 + pairs]


def fine_bias_of(columns, rows):
    heads = columns.shape[0]
    column = jnp.stack(
        [columns[:, TILE_COLS - 1 - a : 2 * TILE_COLS - 1 - a] for a in range(TILE_COLS)], axis=2
    )
    row = jnp.stack(
        [rows[:, TILE_ROWS - 1 - a : 2 * TILE_ROWS - 1 - a] for a in range(TILE_ROWS)], axis=2
    )
    row = jnp.tile(row, (1, 1, TOK_DEV // TILE))
    column = jnp.tile(column, (1, TILE_ROWS, TOK_DEV // TILE_COLS))
    row = jnp.repeat(jnp.repeat(row, TILE_COLS, axis=1), TILE_COLS, axis=2)
    return (column + row).reshape(heads, TILE, TOK_DEV)


def fine_grads_of(fine):
    heads = fine.shape[0]
    groups = TOK_DEV // TILE
    split = fine.reshape(heads, TILE_ROWS, TILE_COLS, groups, TILE_ROWS, TILE_COLS)
    column = jnp.sum(split, axis=(1, 3, 4)).reshape(heads, -1)
    row = jnp.sum(split, axis=(2, 3, 5)).reshape(heads, -1)

    def hot(size):
        at = jnp.arange(size, dtype=jnp.int32)
        offset = (at[:, None] - at[None, :] + size - 1).reshape(-1, 1)
        return (offset == jnp.arange(2 * size - 1, dtype=jnp.int32)[None, :]).astype(jnp.float32)

    column = jnp.dot(column, hot(TILE_COLS), precision=HIGHEST)
    row = jnp.dot(row, hot(TILE_ROWS), precision=HIGHEST)
    return jnp.concatenate([column, row], axis=1)


def after(array, *others):
    return lax.optimization_barrier((array, *others))[0]


def by_heads(queries, keys, values, grad_out, bias_table, slot_tiles, live, buckets):
    count = lax.axis_size("seq")
    windows = lax.axis_size("dp")
    position = lax.axis_index("seq").astype(jnp.int32)
    place = jnp.stack([position, lax.axis_index("dp").astype(jnp.int32)])
    each = HEADS // count
    chunks = [each - each // 3, each // 3]
    starts = [0, chunks[0] * count]
    arrays = (queries[0], keys[0], values[0], grad_out[0])
    pairs = sorted(range(1, count // 2), key=lambda d: (-bin(d).count("1"), d))
    bent = [d for d in pairs if bin(d).count("1") > 1]
    straight = [d for d in pairs if d not in bent]

    def send(message, k):
        return lax.ppermute(message, "seq", [(i, i ^ k) for i in range(count)])

    def packed(where, chunk, targets, sizes):
        return list(
            pack(where, live, buckets, arrays, starts[chunk], chunks[chunk], count, targets, sizes)
        )

    def grads_of(chunk, blocks, sources, more):
        row = starts[chunk] + position * chunks[chunk]
        part = lax.dynamic_slice_in_dim(table, row, chunks[chunk], 0)
        bias = fine_bias_of(
            part[:, BUCKETS : BUCKETS + COLUMN_WIDTH], part[:, BUCKETS + COLUMN_WIDTH :]
        )
        return window_grads(
            place, slot_tiles, part, bias * LOG2E, blocks, sources, count, more
        )

    def table_rows(fine, coarse):
        return jnp.concatenate([coarse[:, :BUCKETS], fine_grads_of(fine)], axis=1)

    table = bias_table
    step = 1
    while step < windows:
        other = lax.ppermute(table, "dp", [(i, i ^ step) for i in range(windows)])
        table = jnp.where(
            place[1] & step == 0,
            jnp.concatenate([table, other], axis=0),
            jnp.concatenate([other, table], axis=0),
        )
        step *= 2

    held = [0] + straight
    targets = {2 * d: (i, 0) for i, d in enumerate(held)}
    targets.update({2 * d + 1: (len(held), i) for i, d in enumerate(held)})
    direct = [2 * d + core for core in range(2) for d in bent]
    targets.update({k: (len(held) + 1 + i, None) for i, k in enumerate(direct)})
    first = packed(place, 0, targets, [2] * len(held) + [len(held)] + [None] * len(direct))
    ready, cross, single = first[: len(held)], first[len(held)], first[len(held) + 1 :]
    half = len(bent)
    single[:half] = [send(m, k) for m, k in zip(single[:half], direct[:half])]
    ready = list(merge(send(cross, 1), ready, None))
    single[half:] = [send(after(m, ready[0]), k) for m, k in zip(single[half:], direct[half:])]
    ready[1:] = [send(m, 2 * d) for m, d in zip(ready[1:], straight)]
    sources = {2 * d + core: (i, core) for i, d in enumerate(held) for core in range(2)}
    sources.update({k: (len(held) + i, None) for i, k in enumerate(direct)})
    every = {ABSOLUTE + i: (0, i) for i in range(count)}
    (second,) = packed(after(place, ready[0]), 1, every, [count])
    second = lax.all_to_all(after(second, ready[1]), "seq", 0, 0)
    cross, first, fine, coarse = grads_of(0, ready + single, sources, 0)

    first_rows = table_rows(fine, coarse)
    first = list(merge(send(cross, 1), first, None))
    for d in pairs:
        first[d] = send(first[d], 2 * d)
    cross, second, fine, coarse = grads_of(1, [second], every, STAMP)
    rows = jnp.concatenate([first_rows, table_rows(fine, coarse)], axis=0)
    step = 1
    while step < windows:
        rows = rows + lax.ppermute(rows, "dp", [(i, i ^ step) for i in range(windows)])
        step *= 2
    second = list(merge(send(cross, 1), second, jnp.stack([rows, send(rows, 1)])))
    for d in pairs:
        second[d] = send(second[d], 2 * d)
    outs = unpack(place, first, 3, starts[0], chunks[0], None, 0)
    outs = unpack(place, second, 3, starts[1], chunks[1], outs, bias_table.shape[0])
    return (outs[0][None], outs[1][None], outs[2][None], outs[3])


def from_behind(block, axis, distance):
    devices = range(lax.axis_size(axis))
    route = [(i - distance, i) for i in devices if i - distance in devices]
    return lax.ppermute(block, axis, route)


def from_behind_2(value, axis, by):
    count = lax.axis_size(axis)
    return lax.ppermute(value, axis, [(i, (i + by) % count) for i in range(count)])


def offset_hots():
    tile_rows = TILE // TILE_COLS
    query_pos = jnp.arange(TOK_DEV, dtype=jnp.int32)[:, None]
    key_pos = jnp.arange(TILE, dtype=jnp.int32)[None, :]
    column_index = key_pos % TILE_COLS - query_pos % TILE_COLS + TILE_COLS - 1
    row_index = key_pos // TILE_COLS - query_pos // TILE_COLS % tile_rows + tile_rows - 1
    column_hot = (
        column_index.reshape(1, -1) == jnp.arange(2 * TILE_COLS - 1, dtype=jnp.int32)[:, None]
    ).astype(jnp.float32)
    row_hot = (
        row_index.reshape(1, -1) == jnp.arange(2 * tile_rows - 1, dtype=jnp.int32)[:, None]
    ).astype(jnp.float32)
    return (column_hot, row_hot)


def by_tiles(queries, keys, values, grad_out, bias_table, slot_tiles, live, buckets):
    axis_size = lax.axis_size("seq")
    position = lax.axis_index("seq")
    half = axis_size // 2
    scale = HEAD_DIM ** (-0.5)
    column_width = 2 * TILE_COLS - 1
    table = lax.all_gather(bias_table, "dp", axis=0, tiled=True)
    column_hot, row_hot = offset_hots()
    fine_bias = jnp.dot(table[:, BUCKETS : BUCKETS + column_width], column_hot, precision=HIGHEST)
    fine_bias = fine_bias + jnp.dot(table[:, BUCKETS + column_width :], row_hot, precision=HIGHEST)
    fine_bias = fine_bias.reshape(HEADS, TOK_DEV, TILE)
    bucket_hot = (buckets[0][:, None] == jnp.arange(BUCKETS, dtype=jnp.int32)[None, :]).astype(
        jnp.float32
    )
    coarse = jnp.dot(bucket_hot, table[:, :BUCKETS].T, precision=HIGHEST)
    alive = live[0].astype(jnp.float32)
    query_heads = queries[0].reshape(TOK_DEV, HEADS, HEAD_DIM)
    upstream_heads = grad_out[0].reshape(TOK_DEV, HEADS, HEAD_DIM)
    own_pairs = jnp.stack(
        [keys[0].reshape(TILES_DEV, TILE, WIDTH), values[0].reshape(TILES_DEV, TILE, WIDTH)], axis=1
    )

    def requested(slot, requester):
        wanted = jnp.clip(slot_tiles[requester, slot] - position * TILES_DEV, 0, TILES_DEV - 1)
        return lax.dynamic_index_in_dim(own_pairs, wanted, 0, keepdims=False)

    fetched = []
    for slot, offset in enumerate(NEAR_OFFSETS):
        requester = jnp.clip(position - offset, 0, axis_size - 1)
        fetched.append(from_behind(requested(slot, requester), "seq", -offset))
    far_requester = (position + half) % axis_size
    fetched.append(from_behind_2(requested(SLOTS - 1, far_requester), "seq", half))
    remote_pairs = jnp.stack(fetched)
    own_group = (own_pairs, coarse[:TILES_DEV], alive[:TILES_DEV])
    remote_group = (remote_pairs, coarse[TILES_DEV:], alive[TILES_DEV:])

    def scores_of(pair, coarse_row):
        key_heads = pair[0].reshape(TILE, HEADS, HEAD_DIM)
        raw = jnp.einsum("qhd,khd->hqk", query_heads, key_heads, preferred_element_type=jnp.float32)
        return raw * scale + coarse_row[:, None, None] + fine_bias

    def products_of(pair):
        value_heads = pair[1].reshape(TILE, HEADS, HEAD_DIM)
        return jnp.einsum(
            "qhd,khd->hqk", upstream_heads, value_heads, preferred_element_type=jnp.float32
        )

    def stats_step(carry, item):
        top, total, weighted = carry
        pair, coarse_row, flag = item
        scores = scores_of(pair, coarse_row)
        attend_grad = products_of(pair)
        keep = flag > 0
        new_top = jnp.where(keep, jnp.maximum(top, jnp.max(scores, axis=2, keepdims=True)), top)
        factor = jnp.exp(top - new_top)
        expo = jnp.exp(scores - new_top) * flag
        added = jnp.sum(expo, axis=2, keepdims=True)
        added_weighted = jnp.sum(expo * attend_grad, axis=2, keepdims=True)
        return ((new_top, total * factor + added, weighted * factor + added_weighted), None)

    stats = (
        jnp.full((HEADS, TOK_DEV, 1), NEGATIVE, jnp.float32),
        jnp.zeros((HEADS, TOK_DEV, 1), jnp.float32),
        jnp.zeros((HEADS, TOK_DEV, 1), jnp.float32),
    )
    stats, _ = lax.scan(stats_step, stats, own_group)
    stats, _ = lax.scan(stats_step, stats, remote_group)
    log_total = stats[0] + jnp.log(stats[1])
    delta = stats[2] / stats[1]

    def grad_step(carry, item):
        query_grad, fine_sum = carry
        pair, coarse_row, flag = item
        scores = scores_of(pair, coarse_row)
        attend = jnp.exp(scores - log_total) * flag
        attend_grad = products_of(pair)
        score_grad = attend * (attend_grad - delta)
        attend_low = attend.astype(jnp.bfloat16)
        grad_low = score_grad.astype(jnp.bfloat16)
        key_heads = pair[0].reshape(TILE, HEADS, HEAD_DIM)
        value_part = jnp.einsum(
            "hqk,qhd->khd", attend_low, upstream_heads, preferred_element_type=jnp.float32
        ).reshape(TILE, WIDTH)
        key_part = (
            jnp.einsum(
                "hqk,qhd->khd", grad_low, query_heads, preferred_element_type=jnp.float32
            ).reshape(TILE, WIDTH)
            * scale
        )
        query_grad = (
            query_grad
            + jnp.einsum("hqk,khd->qhd", grad_low, key_heads, preferred_element_type=jnp.float32)
            * scale
        )
        return (
            (query_grad, fine_sum + score_grad),
            (key_part, value_part, jnp.sum(score_grad, axis=(1, 2))),
        )

    carry = (
        jnp.zeros((TOK_DEV, HEADS, HEAD_DIM), jnp.float32),
        jnp.zeros((HEADS, TOK_DEV, TILE), jnp.float32),
    )
    carry, own_out = lax.scan(grad_step, carry, own_group)
    carry, remote_out = lax.scan(grad_step, carry, remote_group)
    query_grad, fine_sum = carry
    remote_low = jnp.stack([remote_out[0], remote_out[1]], axis=1).astype(jnp.bfloat16)

    def deposit(totals, slot, requester, arrived, weight):
        wanted = jnp.clip(slot_tiles[requester, slot] - position * TILES_DEV, 0, TILES_DEV - 1)
        pick = (jnp.arange(TILES_DEV, dtype=jnp.int32) == wanted).astype(jnp.float32)[
            :, None, None
        ] * weight
        return (
            totals[0] + pick * arrived[0].astype(jnp.float32)[None],
            totals[1] + pick * arrived[1].astype(jnp.float32)[None],
        )

    totals = (own_out[0], own_out[1])
    for slot, offset in enumerate(NEAR_OFFSETS):
        arrived = from_behind(remote_low[slot], "seq", offset)
        requester = jnp.clip(position - offset, 0, axis_size - 1)
        totals = deposit(totals, slot, requester, arrived, 1.0)
    arrived = from_behind_2(remote_low[SLOTS - 1], "seq", half)
    totals = deposit(totals, SLOTS - 1, (position + half) % axis_size, arrived, 1.0)
    block_sums = jnp.concatenate([own_out[2], remote_out[2]], axis=0)
    coarse_grad = jnp.dot(block_sums.T, bucket_hot, precision=HIGHEST)
    flat_sum = fine_sum.reshape(HEADS, TOK_DEV * TILE)
    column_grad = jnp.dot(flat_sum, column_hot.T, precision=HIGHEST)
    row_grad = jnp.dot(flat_sum, row_hot.T, precision=HIGHEST)
    table_grad = jnp.concatenate([coarse_grad, column_grad, row_grad], axis=1)
    summed = lax.psum(table_grad, "seq")
    table_out = lax.psum_scatter(summed, "dp", scatter_dimension=0, tiled=True)
    query_out = query_grad.reshape(1, TOK_DEV, WIDTH).astype(jnp.bfloat16)
    key_out = totals[0].reshape(1, TOK_DEV, WIDTH).astype(jnp.bfloat16)
    value_out = totals[1].reshape(1, TOK_DEV, WIDTH).astype(jnp.bfloat16)
    return (query_out, key_out, value_out, table_out)


def solution(mesh):
    count = mesh.shape["seq"]
    windows = mesh.shape["dp"]
    whole = HEADS % (3 * count) == 0 and count > 2 and count & (count - 1) == 0 and windows & (windows - 1) == 0
    plan = by_heads if whole else by_tiles
    return jax.shard_map(
        plan,
        mesh=mesh,
        in_specs=(
            P("dp", "seq", None),
            P("dp", "seq", None),
            P("dp", "seq", None),
            P("dp", "seq", None),
            P("dp", None),
            P(),
            P("seq", None),
            P("seq", None),
        ),
        out_specs=(P("dp", "seq", None), P("dp", "seq", None), P("dp", "seq", None), P("dp", None)),
        check_vma=False,
    )
```

```python
import functools

import jax
import jax.numpy as jnp
from jax import lax
from jax.experimental import pallas as pl
from jax.experimental.pallas import tpu as pltpu
from jax.sharding import PartitionSpec as P

HEADS = 24
HEAD_DIM = 128
TOK_DEV = 256
TILE = 128
TILE_COLS = 16
SLOTS = 5
BUCKETS = 82
WIDTH = 3072
TILES_DEV = 2
ENTRIES = TILES_DEV + SLOTS
TILE_ROWS = TILE // TILE_COLS
COLUMN_WIDTH = 2 * TILE_COLS - 1
ROW_WIDTH = 2 * TILE_ROWS - 1

NEGATIVE = -1e30
HIGHEST = lax.Precision.HIGHEST
NEAR_OFFSETS = (-1, 1, -2, 2)
LOG2E = 1.4426950408889634
SCALE = HEAD_DIM ** (-0.5)
VMEM_LIMIT = 56 * 1024 * 1024


SIZES = (2, 4, 5, ENTRIES)
ABSOLUTE = 1 << 16
STAMP = 32
META = 16
HBM = pl.BlockSpec(memory_space=pltpu.HBM)
SMEM = pl.BlockSpec(memory_space=pltpu.SMEM)


def pack_body(number, heads, first, count, targets, *refs):
    place_ref, live_ref, bucket_ref = refs[:3]
    arrays = refs[3 : 3 + number]
    outs = refs[3 + number : -4]
    held_ref, meta_ref, in_sem, out_sem = refs[-4:]
    width = heads * HEAD_DIM
    position = place_ref[0]
    span = pl.ds(first * HEAD_DIM, count * width)
    arriving = [
        pltpu.make_async_copy(arrays[a].at[:, span], held_ref.at[a], in_sem.at[a])
        for a in range(number)
    ]
    for copy in arriving:
        copy.start()
    row = lax.broadcasted_iota(jnp.int32, (META, width), 0)
    lane = lax.broadcasted_iota(jnp.int32, (META, width), 1)
    meta = jnp.zeros((META, width), jnp.int32)
    for e in range(ENTRIES):
        meta = jnp.where((row == e) & (lane == 0), bucket_ref[0, e], meta)
        meta = jnp.where((row == e) & (lane == 1), live_ref[0, e], meta)
    meta_ref[...] = meta.astype(jnp.float32).astype(jnp.bfloat16)
    columns, messages = [], []
    for k, (out, at) in targets.items():
        column = (k - ABSOLUTE) * width if k >= ABSOLUTE else (position ^ k) * width
        columns.append(column if k >= ABSOLUTE else pl.multiple_of(column, HEAD_DIM))
        messages.append(outs[out] if at is None else outs[out].at[at])
    leaving = [
        pltpu.make_async_copy(meta_ref, message.at[pl.ds(number * TOK_DEV, META)], out_sem)
        for message in messages
    ]
    for copy in leaving:
        copy.start()
    for a in range(number):
        arriving[a].wait()
        for message, column in zip(messages, columns):
            leaving.append(
                pltpu.make_async_copy(
                    held_ref.at[a, :, pl.ds(column, width)],
                    message.at[pl.ds(a * TOK_DEV, TOK_DEV)],
                    out_sem,
                )
            )
            leaving[-1].start()
    for copy in leaving:
        copy.wait()


def pack(place, live, buckets, arrays, first, heads, count, targets, sizes):
    number = len(arrays)
    rows = number * TOK_DEV + META
    width = heads * HEAD_DIM
    return pl.pallas_call(
        functools.partial(pack_body, number, heads, first, count, targets),
        in_specs=[SMEM] * 3 + [HBM] * number,
        out_specs=[HBM] * len(sizes),
        out_shape=[
            jax.ShapeDtypeStruct((() if size is None else (size,)) + (rows, width), jnp.bfloat16)
            for size in sizes
        ],
        scratch_shapes=[
            pltpu.VMEM((number, TOK_DEV, count * width), jnp.bfloat16),
            pltpu.VMEM((META, width), jnp.bfloat16),
            pltpu.SemaphoreType.DMA((number,)),
            pltpu.SemaphoreType.DMA,
        ],
        compiler_params=pltpu.CompilerParams(vmem_limit_bytes=VMEM_LIMIT),
        cost_estimate=pl.CostEstimate(
            flops=0, bytes_accessed=4 * count * rows * width, transcendentals=0
        ),
    )(place, live, buckets, *arrays)


def unpack_body(number, heads, first, count, held, owned, *refs):
    place_ref = refs[0]
    pairs = count // 2
    blocks = [refs[1 + k // 2].at[k % 2] for k in range(count)]
    outs = refs[1 + pairs + held : 1 + pairs + held + number]
    scratch = refs[1 + pairs + held + number :]
    if owned:
        table_ref, held_ref, in_sem, out_sem, stamp_ref, whole_ref, stamp_sem = scratch
        stamps = [
            pltpu.make_async_copy(
                blocks[k].at[pl.ds(number * TOK_DEV, STAMP)], stamp_ref.at[k], stamp_sem
            )
            for k in range(count)
        ]
    else:
        held_ref, in_sem, out_sem = scratch
    width = heads * HEAD_DIM
    position = place_ref[0]
    arriving = []
    for a in range(number):
        for k in range(count):
            column = pl.multiple_of((position ^ k) * width, HEAD_DIM)
            arriving.append(
                pltpu.make_async_copy(
                    blocks[k].at[pl.ds(a * TOK_DEV, TOK_DEV)],
                    held_ref.at[a, :, pl.ds(column, width)],
                    in_sem.at[a],
                )
            )
            arriving[-1].start()
    if owned:
        for copy in stamps:
            copy.start()
    leaving = []
    for a in range(number):
        for copy in arriving[a * count : (a + 1) * count]:
            copy.wait()
        leaving.append(
            pltpu.make_async_copy(
                held_ref.at[a],
                outs[a].at[:, pl.ds(first * HEAD_DIM, count * width)],
                out_sem,
            )
        )
        leaving[-1].start()
    if owned:
        for copy in stamps:
            copy.wait()
        each = HEADS // count
        for k in range(count):
            parts = stamp_ref[k].astype(jnp.float32)
            rows = parts[0:each] + parts[each : 2 * each] + parts[2 * each : 3 * each]
            source = position ^ k
            for r in range(each):
                head = source * (each - heads) + r if r < each - heads else first + source * heads + r - (each - heads)
                whole_ref[pl.ds(head, 1)] = rows[r : r + 1]
        for r in range(owned):
            table_ref[r : r + 1] = whole_ref[pl.ds(place_ref[1] * owned + r, 1)]
    for copy in leaving:
        copy.wait()


def unpack(place, blocks, number, first, heads, onto, owned):
    pairs = len(blocks)
    count = 2 * pairs
    held = 0 if onto is None else number
    out_specs = [HBM] * number
    out_shape = [jax.ShapeDtypeStruct((TOK_DEV, WIDTH), jnp.bfloat16)] * number
    scratch_shapes = [
        pltpu.VMEM((number, TOK_DEV, count * heads * HEAD_DIM), jnp.bfloat16),
        pltpu.SemaphoreType.DMA((number,)),
        pltpu.SemaphoreType.DMA,
    ]
    if owned:
        out_specs = out_specs + [pl.BlockSpec(memory_space=pltpu.VMEM)]
        out_shape = out_shape + [jax.ShapeDtypeStruct((owned, TILE), jnp.float32)]
        scratch_shapes += [
            pltpu.VMEM((count, STAMP, heads * HEAD_DIM), jnp.bfloat16),
            pltpu.VMEM((HEADS, TILE), jnp.float32),
            pltpu.SemaphoreType.DMA,
        ]
    return pl.pallas_call(
        functools.partial(unpack_body, number, heads, first, count, held, owned),
        in_specs=[SMEM] + [HBM] * (pairs + held),
        out_specs=out_specs,
        out_shape=out_shape,
        input_output_aliases={1 + pairs + a: a for a in range(held)},
        scratch_shapes=scratch_shapes,
        compiler_params=pltpu.CompilerParams(vmem_limit_bytes=VMEM_LIMIT),
        cost_estimate=pl.CostEstimate(
            flops=0, bytes_accessed=4 * count * number * TOK_DEV * heads * HEAD_DIM, transcendentals=0
        ),
    )(place, *blocks, *(onto if onto is not None else ()))


def merge_body(pairs, rows, stamped, *refs):
    cross_ref = refs[0]
    outs = refs[1 + stamped + pairs : 1 + stamped + 2 * pairs]
    held_ref, low_ref, in_sem, out_sem = refs[1 + stamped + 2 * pairs :]
    arriving = [
        pltpu.make_async_copy(
            cross_ref.at[d], held_ref.at[d, pl.ds(0, rows)], in_sem.at[d]
        )
        for d in range(pairs)
    ]
    for copy in arriving:
        copy.start()
    leaving = []
    if stamped:
        low_ref[...] = jnp.zeros_like(low_ref)
        for s in range(2):
            rest = refs[1][s]
            number = rest.shape[0]
            for part in range(3):
                low = rest.astype(jnp.bfloat16).astype(jnp.float32)
                low_ref[s, part * number : (part + 1) * number] = low
                rest = rest - low
        whole = low_ref[...].astype(jnp.bfloat16)
        held_ref[0:2, rows : rows + STAMP] = whole
        for d in range(pairs):
            leaving += [
                pltpu.make_async_copy(
                    held_ref.at[s, pl.ds(rows, STAMP)], outs[d].at[s, pl.ds(rows, STAMP)], out_sem
                )
                for s in range(2)
            ]
            leaving[-2].start()
            leaving[-1].start()
    for d in range(pairs):
        arriving[d].wait()
        leaving.append(
            pltpu.make_async_copy(
                held_ref.at[d, pl.ds(0, rows)], outs[d].at[1, pl.ds(0, rows)], out_sem
            )
        )
        leaving[-1].start()
    for copy in leaving:
        copy.wait()


def merge(cross, messages, table_rows):
    pairs, rows, width = cross.shape
    stamped = 0 if table_rows is None else 1
    shape = messages[0].shape
    return pl.pallas_call(
        functools.partial(merge_body, pairs, rows, stamped),
        in_specs=[HBM] + [pl.BlockSpec(memory_space=pltpu.VMEM)] * stamped + [HBM] * pairs,
        out_specs=[HBM] * pairs,
        out_shape=[jax.ShapeDtypeStruct(shape, jnp.bfloat16)] * pairs,
        input_output_aliases={1 + stamped + d: d for d in range(pairs)},
        scratch_shapes=[
            pltpu.VMEM((pairs,) + shape[1:], jnp.bfloat16),
            pltpu.VMEM((2, STAMP, TILE), jnp.float32),
            pltpu.SemaphoreType.DMA((pairs,)),
            pltpu.SemaphoreType.DMA,
        ],
        compiler_params=pltpu.CompilerParams(vmem_limit_bytes=VMEM_LIMIT),
        cost_estimate=pl.CostEstimate(
            flops=0, bytes_accessed=4 * cross.size, transcendentals=0
        ),
    )(cross, *(() if table_rows is None else (table_rows,)), *messages)


def fold(array, combine):
    parts = [array[r : r + 8] for r in range(0, array.shape[0], 8)]
    while len(parts) > 1:
        parts = [combine(parts[2 * k], parts[2 * k + 1]) for k in range(len(parts) // 2)]
    return parts[0]


def grad_body(count, heads, sources, *refs):
    place_ref, slots_ref, table_ref, bias_ref = refs[:4]
    refs = refs[4:]
    inputs = 1 + max(source for source, _ in sources.values())
    blocks, refs = refs[:inputs], refs[inputs:]
    cross_ref, refs = refs[0], refs[1:]
    pairs, refs = refs[: count // 2], refs[count // 2 :]
    outs = [(pairs[k // 2].at[0], cross_ref.at[k // 2])[k % 2] for k in range(count)]
    fine_ref, coarse_out_ref = refs[:2]
    (
        x_ref,
        y_ref,
        coarse_ref,
        sums_ref,
        score_ref,
        product_ref,
        low_ref,
        key_ref,
        key_grad_ref,
        value_grad_ref,
        in_sem,
        out_sem,
        list_ref,
        tile_ref,
        number_ref,
    ) = refs[2:]
    position = place_ref[0]

    def lanes(h):
        return pl.ds(h * HEAD_DIM, HEAD_DIM)

    arriving = []
    for h in range(heads):
        arriving.append([])
        for k, (source, at) in sources.items():
            block = blocks[source] if at is None else blocks[source].at[at]
            tile = k - ABSOLUTE if k >= ABSOLUTE else position ^ k
            arriving[h].append(
                pltpu.make_async_copy(
                    block.at[:, lanes(h)], x_ref.at[tile, :, lanes(h)], in_sem.at[h]
                )
            )
    leaving = [
        pltpu.make_async_copy(
            y_ref.at[position ^ k, :, lanes(h)],
            outs[k].at[pl.ds(0, 3 * TOK_DEV), lanes(h)],
            out_sem,
        )
        for h in range(heads)
        for k in range(count)
    ]
    for copies in arriving:
        for copy in copies:
            copy.start()
    lane = lax.broadcasted_iota(jnp.int32, (8, TILE), 1)
    transposed = (((1,), (1,)), ((), ()))

    def array_rows(a, begin=0, size=TOK_DEV):
        return pl.ds(a * TOK_DEV + begin, size)

    def meta_of(i):
        meta = x_ref[i, 4 * TOK_DEV : 4 * TOK_DEV + META, 0:TILE].astype(jnp.float32)[:8]
        hot = (lane == meta[:, 0:1].astype(jnp.int32)).astype(jnp.float32)
        return hot, meta[:, 1:2]

    def list_live(i, flag):
        row = lax.broadcasted_iota(jnp.int32, (8, 1), 0)
        code = jnp.sum(jnp.where(flag > 0, 1 << row, 0).astype(jnp.float32)).astype(jnp.int32)
        for e in range(8):
            list_ref[i * 8 + e] = ENTRIES
            tile_ref[i * 8 + e] = (
                slots_ref[i, e - TILES_DEV]
                if TILES_DEV <= e < ENTRIES
                else i * TILES_DEV + e % TILES_DEV
            )
        number = jnp.int32(0)
        for e in range(ENTRIES):
            list_ref[i * 8 + number] = e
            number = number + ((code >> e) & 1)
        list_ref[i * 8 + number] = ENTRIES
        number_ref[i] = number

    for h in range(heads):
        columns = slice(h * HEAD_DIM, (h + 1) * HEAD_DIM)
        key_grad_ref[...] = jnp.zeros_like(key_grad_ref)
        value_grad_ref[...] = jnp.zeros_like(value_grad_ref)
        fine_ref[h] = jnp.zeros_like(fine_ref[h])
        for copy in arriving[h]:
            copy.wait()
        sums_ref[...] = jnp.zeros_like(sums_ref)
        for i in range(count):
            hot, flag = meta_of(i)
            if h == 0:
                list_live(i, flag)
            coarse = jnp.sum(hot * table_ref[h : h + 1, :], axis=1, keepdims=True) * LOG2E
            coarse = jnp.where(flag > 0, coarse, NEGATIVE)
            coarse_ref[i] = jnp.broadcast_to(coarse, (8, TOK_DEV))

        def query_tile(i, size):
            query = x_ref[i, array_rows(0), columns]
            upstream = x_ref[i, array_rows(3), columns]
            entries = [list_ref[i * 8 + s] for s in range(size)]
            tiles = [tile_ref[i * 8 + e] for e in entries]
            coarse = [coarse_ref[i, pl.ds(e, 1)] for e in entries]

            def tile_of(a, s):
                begin = pl.multiple_of(a * TOK_DEV + (tiles[s] % TILES_DEV) * TILE, TILE)
                return x_ref[tiles[s] // TILES_DEV, pl.ds(begin, TILE), columns]

            top = None
            for s in range(size):
                key = tile_of(1, s)
                key_ref[s * TILE : (s + 1) * TILE] = key
                raw = lax.dot_general(key, query, transposed, preferred_element_type=jnp.float32)
                score = raw * (SCALE * LOG2E) + bias_ref[h]
                score_ref[s] = score
                best = fold(score, jnp.maximum) + coarse[s]
                top = best if top is None else jnp.maximum(top, best)
            top = jnp.max(top, axis=0, keepdims=True)
            total = jnp.zeros((8, TOK_DEV), jnp.float32)
            weighted = jnp.zeros((8, TOK_DEV), jnp.float32)
            for s in range(size):
                product = lax.dot_general(
                    tile_of(2, s), upstream, transposed, preferred_element_type=jnp.float32
                )
                expo = jnp.exp2(score_ref[s] - (top - coarse[s]))
                score_ref[s] = expo
                product_ref[s] = product
                total = total + fold(expo, jnp.add)
                weighted = weighted + fold(expo * product, jnp.add)
            inverse = 1.0 / jnp.sum(total, axis=0, keepdims=True)
            delta = jnp.sum(weighted, axis=0, keepdims=True) * inverse
            for s in range(size):
                attend = score_ref[s] * inverse
                grad = attend * (product_ref[s] - delta)
                fine_ref[h] += grad
                sums = jnp.sum(fold(grad, jnp.add), axis=0, keepdims=True)
                sums_ref[i, pl.ds(entries[s], 1)] = sums[:, :TILE] + sums[:, TILE:]
                grad_low = grad.astype(jnp.bfloat16)
                low_ref[s * TILE : (s + 1) * TILE] = grad_low
                value_grad_ref[tiles[s]] += jnp.dot(
                    attend.astype(jnp.bfloat16), upstream, preferred_element_type=jnp.float32
                )
                key_grad_ref[tiles[s]] += jnp.dot(
                    grad_low, query, preferred_element_type=jnp.float32
                )
            query_grad = lax.dot_general(
                key_ref[: size * TILE],
                low_ref[: size * TILE],
                (((0,), (0,)), ((), ())),
                preferred_element_type=jnp.float32,
            )
            y_ref[i, array_rows(0), columns] = (query_grad.T * SCALE).astype(jnp.bfloat16)

        @pl.loop(0, count)
        def _(i):
            number = number_ref[i]
            below = 0
            for size in SIZES:
                pl.when((number > below) & (number <= size))(
                    functools.partial(query_tile, i, size)
                )
                below = size

        coarse_grad = jnp.zeros((1, TILE), jnp.float32)
        for i in range(count):
            hot, _ = meta_of(i)
            sums = jnp.sum(sums_ref[i], axis=1, keepdims=True)
            real = lax.broadcasted_iota(jnp.int32, (8, 1), 0) < ENTRIES
            spread = hot * jnp.where(real, sums, 0.0)
            coarse_grad = coarse_grad + jnp.sum(spread, axis=0, keepdims=True)
        coarse_out_ref[h : h + 1] = coarse_grad

        @pl.loop(0, count)
        def _(i):
            for t in range(TILES_DEV):
                tile = i * TILES_DEV + t
                y_ref[i, array_rows(1, t * TILE, TILE), columns] = (
                    key_grad_ref[tile] * SCALE
                ).astype(jnp.bfloat16)
                y_ref[i, array_rows(2, t * TILE, TILE), columns] = value_grad_ref[tile].astype(
                    jnp.bfloat16
                )

        for copy in leaving[h * count : (h + 1) * count]:
            copy.start()

    for copy in leaving:
        copy.wait()


def window_grads(place, slots, table, bias, blocks, sources, count, more):
    heads = table.shape[0]
    width = heads * HEAD_DIM
    rows = 3 * TOK_DEV
    pairs = count // 2
    work = heads * count * ENTRIES * TILE * TOK_DEV
    vmem = pl.BlockSpec(memory_space=pltpu.VMEM)
    results = pl.pallas_call(
        functools.partial(grad_body, count, heads, sources),
        in_specs=[SMEM, SMEM, vmem, vmem] + [HBM] * len(blocks),
        out_specs=[HBM] * (1 + pairs) + [vmem] * 2,
        out_shape=[jax.ShapeDtypeStruct((pairs, rows, width), jnp.bfloat16)]
        + [jax.ShapeDtypeStruct((2, rows + more, width), jnp.bfloat16)] * pairs
        + [
            jax.ShapeDtypeStruct((heads, TILE, TOK_DEV), jnp.float32),
            jax.ShapeDtypeStruct((heads, TILE), jnp.float32),
        ],
        scratch_shapes=[
            pltpu.VMEM((count, 4 * TOK_DEV + META, width), jnp.bfloat16),
            pltpu.VMEM((count, rows, width), jnp.bfloat16),
            pltpu.VMEM((count, 8, TOK_DEV), jnp.float32),
            pltpu.VMEM((count, 8, TILE), jnp.float32),
            pltpu.VMEM((ENTRIES, TILE, TOK_DEV), jnp.float32),
            pltpu.VMEM((ENTRIES, TILE, TOK_DEV), jnp.float32),
            pltpu.VMEM((ENTRIES * TILE, TOK_DEV), jnp.bfloat16),
            pltpu.VMEM((ENTRIES * TILE, HEAD_DIM), jnp.bfloat16),
            pltpu.VMEM((count * TILES_DEV, TILE, HEAD_DIM), jnp.float32),
            pltpu.VMEM((count * TILES_DEV, TILE, HEAD_DIM), jnp.float32),
            pltpu.SemaphoreType.DMA((heads,)),
            pltpu.SemaphoreType.DMA,
            pltpu.SMEM((count * 8,), jnp.int32),
            pltpu.SMEM((count * 8,), jnp.int32),
            pltpu.SMEM((count,), jnp.int32),
        ],
        compiler_params=pltpu.CompilerParams(vmem_limit_bytes=VMEM_LIMIT),
        cost_estimate=pl.CostEstimate(
            flops=10 * work * HEAD_DIM,
            bytes_accessed=2 * 7 * count * TOK_DEV * width,
            transcendentals=work,
        ),
    )(place, slots, table, bias, *blocks)
    return results[0], list(results[1 : 1 + pairs]), results[1 + pairs], results[2 + pairs]


def fine_bias_of(columns, rows):
    heads = columns.shape[0]
    column = jnp.stack(
        [columns[:, TILE_COLS - 1 - a : 2 * TILE_COLS - 1 - a] for a in range(TILE_COLS)], axis=2
    )
    row = jnp.stack(
        [rows[:, TILE_ROWS - 1 - a : 2 * TILE_ROWS - 1 - a] for a in range(TILE_ROWS)], axis=2
    )
    row = jnp.tile(row, (1, 1, TOK_DEV // TILE))
    column = jnp.tile(column, (1, TILE_ROWS, TOK_DEV // TILE_COLS))
    row = jnp.repeat(jnp.repeat(row, TILE_COLS, axis=1), TILE_COLS, axis=2)
    return (column + row).reshape(heads, TILE, TOK_DEV)


def fine_grads_of(fine):
    heads = fine.shape[0]
    groups = TOK_DEV // TILE
    split = fine.reshape(heads, TILE_ROWS, TILE_COLS, groups, TILE_ROWS, TILE_COLS)
    column = jnp.sum(split, axis=(1, 3, 4)).reshape(heads, -1)
    row = jnp.sum(split, axis=(2, 3, 5)).reshape(heads, -1)

    def hot(size):
        at = jnp.arange(size, dtype=jnp.int32)
        offset = (at[:, None] - at[None, :] + size - 1).reshape(-1, 1)
        return (offset == jnp.arange(2 * size - 1, dtype=jnp.int32)[None, :]).astype(jnp.float32)

    column = jnp.dot(column, hot(TILE_COLS), precision=HIGHEST)
    row = jnp.dot(row, hot(TILE_ROWS), precision=HIGHEST)
    return jnp.concatenate([column, row], axis=1)


def after(array, *others):
    return lax.optimization_barrier((array, *others))[0]


def by_heads(queries, keys, values, grad_out, bias_table, slot_tiles, live, buckets):
    count = lax.axis_size("seq")
    windows = lax.axis_size("dp")
    position = lax.axis_index("seq").astype(jnp.int32)
    place = jnp.stack([position, lax.axis_index("dp").astype(jnp.int32)])
    each = HEADS // count
    chunks = [each - each // 3, each // 3]
    starts = [0, chunks[0] * count]
    arrays = (queries[0], keys[0], values[0], grad_out[0])
    pairs = sorted(range(1, count // 2), key=lambda d: (-bin(d).count("1"), d))
    bent = [d for d in pairs if bin(d).count("1") > 1]
    straight = [d for d in pairs if d not in bent]

    def send(message, k):
        return lax.ppermute(message, "seq", [(i, i ^ k) for i in range(count)])

    def packed(where, chunk, targets, sizes):
        return list(
            pack(where, live, buckets, arrays, starts[chunk], chunks[chunk], count, targets, sizes)
        )

    def grads_of(chunk, blocks, sources, more):
        row = starts[chunk] + position * chunks[chunk]
        part = lax.dynamic_slice_in_dim(table, row, chunks[chunk], 0)
        bias = fine_bias_of(
            part[:, BUCKETS : BUCKETS + COLUMN_WIDTH], part[:, BUCKETS + COLUMN_WIDTH :]
        )
        return window_grads(
            place, slot_tiles, part, bias * LOG2E, blocks, sources, count, more
        )

    def table_rows(fine, coarse):
        return jnp.concatenate([coarse[:, :BUCKETS], fine_grads_of(fine)], axis=1)

    table = bias_table
    step = 1
    while step < windows:
        other = lax.ppermute(table, "dp", [(i, i ^ step) for i in range(windows)])
        table = jnp.where(
            place[1] & step == 0,
            jnp.concatenate([table, other], axis=0),
            jnp.concatenate([other, table], axis=0),
        )
        step *= 2

    held = [0] + straight
    targets = {2 * d: (i, 0) for i, d in enumerate(held)}
    targets.update({2 * d + 1: (len(held), i) for i, d in enumerate(held)})
    direct = [2 * d + core for core in range(2) for d in bent]
    targets.update({k: (len(held) + 1 + i, None) for i, k in enumerate(direct)})
    first = packed(place, 0, targets, [2] * len(held) + [len(held)] + [None] * len(direct))
    ready, cross, single = first[: len(held)], first[len(held)], first[len(held) + 1 :]
    half = len(bent)
    single[:half] = [send(m, k) for m, k in zip(single[:half], direct[:half])]
    ready = list(merge(send(cross, 1), ready, None))
    single[half:] = [send(after(m, ready[0]), k) for m, k in zip(single[half:], direct[half:])]
    ready[1:] = [send(m, 2 * d) for m, d in zip(ready[1:], straight)]
    sources = {2 * d + core: (i, core) for i, d in enumerate(held) for core in range(2)}
    sources.update({k: (len(held) + i, None) for i, k in enumerate(direct)})
    every = {ABSOLUTE + i: (0, i) for i in range(count)}
    (second,) = packed(after(place, ready[0]), 1, every, [count])
    second = lax.all_to_all(after(second, *ready[1:]), "seq", 0, 0)
    cross, first, fine, coarse = grads_of(0, ready + single, sources, 0)

    first_rows = table_rows(fine, coarse)
    first = list(merge(send(cross, 1), first, None))
    for d in pairs:
        first[d] = send(first[d], 2 * d)
    cross, second, fine, coarse = grads_of(1, [second], every, STAMP)
    rows = jnp.concatenate([first_rows, table_rows(fine, coarse)], axis=0)
    step = 1
    while step < windows:
        rows = rows + lax.ppermute(rows, "dp", [(i, i ^ step) for i in range(windows)])
        step *= 2
    second = list(merge(send(cross, 1), second, jnp.stack([rows, send(rows, 1)])))
    for d in pairs:
        second[d] = send(second[d], 2 * d)
    outs = unpack(place, first, 3, starts[0], chunks[0], None, 0)
    outs = unpack(place, second, 3, starts[1], chunks[1], outs, bias_table.shape[0])
    return (outs[0][None], outs[1][None], outs[2][None], outs[3])


def from_behind(block, axis, distance):
    devices = range(lax.axis_size(axis))
    route = [(i - distance, i) for i in devices if i - distance in devices]
    return lax.ppermute(block, axis, route)


def from_behind_2(value, axis, by):
    count = lax.axis_size(axis)
    return lax.ppermute(value, axis, [(i, (i + by) % count) for i in range(count)])


def offset_hots():
    tile_rows = TILE // TILE_COLS
    query_pos = jnp.arange(TOK_DEV, dtype=jnp.int32)[:, None]
    key_pos = jnp.arange(TILE, dtype=jnp.int32)[None, :]
    column_index = key_pos % TILE_COLS - query_pos % TILE_COLS + TILE_COLS - 1
    row_index = key_pos // TILE_COLS - query_pos // TILE_COLS % tile_rows + tile_rows - 1
    column_hot = (
        column_index.reshape(1, -1) == jnp.arange(2 * TILE_COLS - 1, dtype=jnp.int32)[:, None]
    ).astype(jnp.float32)
    row_hot = (
        row_index.reshape(1, -1) == jnp.arange(2 * tile_rows - 1, dtype=jnp.int32)[:, None]
    ).astype(jnp.float32)
    return (column_hot, row_hot)


def by_tiles(queries, keys, values, grad_out, bias_table, slot_tiles, live, buckets):
    axis_size = lax.axis_size("seq")
    position = lax.axis_index("seq")
    half = axis_size // 2
    scale = HEAD_DIM ** (-0.5)
    column_width = 2 * TILE_COLS - 1
    table = lax.all_gather(bias_table, "dp", axis=0, tiled=True)
    column_hot, row_hot = offset_hots()
    fine_bias = jnp.dot(table[:, BUCKETS : BUCKETS + column_width], column_hot, precision=HIGHEST)
    fine_bias = fine_bias + jnp.dot(table[:, BUCKETS + column_width :], row_hot, precision=HIGHEST)
    fine_bias = fine_bias.reshape(HEADS, TOK_DEV, TILE)
    bucket_hot = (buckets[0][:, None] == jnp.arange(BUCKETS, dtype=jnp.int32)[None, :]).astype(
        jnp.float32
    )
    coarse = jnp.dot(bucket_hot, table[:, :BUCKETS].T, precision=HIGHEST)
    alive = live[0].astype(jnp.float32)
    query_heads = queries[0].reshape(TOK_DEV, HEADS, HEAD_DIM)
    upstream_heads = grad_out[0].reshape(TOK_DEV, HEADS, HEAD_DIM)
    own_pairs = jnp.stack(
        [keys[0].reshape(TILES_DEV, TILE, WIDTH), values[0].reshape(TILES_DEV, TILE, WIDTH)], axis=1
    )

    def requested(slot, requester):
        wanted = jnp.clip(slot_tiles[requester, slot] - position * TILES_DEV, 0, TILES_DEV - 1)
        return lax.dynamic_index_in_dim(own_pairs, wanted, 0, keepdims=False)

    fetched = []
    for slot, offset in enumerate(NEAR_OFFSETS):
        requester = jnp.clip(position - offset, 0, axis_size - 1)
        fetched.append(from_behind(requested(slot, requester), "seq", -offset))
    far_requester = (position + half) % axis_size
    fetched.append(from_behind_2(requested(SLOTS - 1, far_requester), "seq", half))
    remote_pairs = jnp.stack(fetched)
    own_group = (own_pairs, coarse[:TILES_DEV], alive[:TILES_DEV])
    remote_group = (remote_pairs, coarse[TILES_DEV:], alive[TILES_DEV:])

    def scores_of(pair, coarse_row):
        key_heads = pair[0].reshape(TILE, HEADS, HEAD_DIM)
        raw = jnp.einsum("qhd,khd->hqk", query_heads, key_heads, preferred_element_type=jnp.float32)
        return raw * scale + coarse_row[:, None, None] + fine_bias

    def products_of(pair):
        value_heads = pair[1].reshape(TILE, HEADS, HEAD_DIM)
        return jnp.einsum(
            "qhd,khd->hqk", upstream_heads, value_heads, preferred_element_type=jnp.float32
        )

    def stats_step(carry, item):
        top, total, weighted = carry
        pair, coarse_row, flag = item
        scores = scores_of(pair, coarse_row)
        attend_grad = products_of(pair)
        keep = flag > 0
        new_top = jnp.where(keep, jnp.maximum(top, jnp.max(scores, axis=2, keepdims=True)), top)
        factor = jnp.exp(top - new_top)
        expo = jnp.exp(scores - new_top) * flag
        added = jnp.sum(expo, axis=2, keepdims=True)
        added_weighted = jnp.sum(expo * attend_grad, axis=2, keepdims=True)
        return ((new_top, total * factor + added, weighted * factor + added_weighted), None)

    stats = (
        jnp.full((HEADS, TOK_DEV, 1), NEGATIVE, jnp.float32),
        jnp.zeros((HEADS, TOK_DEV, 1), jnp.float32),
        jnp.zeros((HEADS, TOK_DEV, 1), jnp.float32),
    )
    stats, _ = lax.scan(stats_step, stats, own_group)
    stats, _ = lax.scan(stats_step, stats, remote_group)
    log_total = stats[0] + jnp.log(stats[1])
    delta = stats[2] / stats[1]

    def grad_step(carry, item):
        query_grad, fine_sum = carry
        pair, coarse_row, flag = item
        scores = scores_of(pair, coarse_row)
        attend = jnp.exp(scores - log_total) * flag
        attend_grad = products_of(pair)
        score_grad = attend * (attend_grad - delta)
        attend_low = attend.astype(jnp.bfloat16)
        grad_low = score_grad.astype(jnp.bfloat16)
        key_heads = pair[0].reshape(TILE, HEADS, HEAD_DIM)
        value_part = jnp.einsum(
            "hqk,qhd->khd", attend_low, upstream_heads, preferred_element_type=jnp.float32
        ).reshape(TILE, WIDTH)
        key_part = (
            jnp.einsum(
                "hqk,qhd->khd", grad_low, query_heads, preferred_element_type=jnp.float32
            ).reshape(TILE, WIDTH)
            * scale
        )
        query_grad = (
            query_grad
            + jnp.einsum("hqk,khd->qhd", grad_low, key_heads, preferred_element_type=jnp.float32)
            * scale
        )
        return (
            (query_grad, fine_sum + score_grad),
            (key_part, value_part, jnp.sum(score_grad, axis=(1, 2))),
        )

    carry = (
        jnp.zeros((TOK_DEV, HEADS, HEAD_DIM), jnp.float32),
        jnp.zeros((HEADS, TOK_DEV, TILE), jnp.float32),
    )
    carry, own_out = lax.scan(grad_step, carry, own_group)
    carry, remote_out = lax.scan(grad_step, carry, remote_group)
    query_grad, fine_sum = carry
    remote_low = jnp.stack([remote_out[0], remote_out[1]], axis=1).astype(jnp.bfloat16)

    def deposit(totals, slot, requester, arrived, weight):
        wanted = jnp.clip(slot_tiles[requester, slot] - position * TILES_DEV, 0, TILES_DEV - 1)
        pick = (jnp.arange(TILES_DEV, dtype=jnp.int32) == wanted).astype(jnp.float32)[
            :, None, None
        ] * weight
        return (
            totals[0] + pick * arrived[0].astype(jnp.float32)[None],
            totals[1] + pick * arrived[1].astype(jnp.float32)[None],
        )

    totals = (own_out[0], own_out[1])
    for slot, offset in enumerate(NEAR_OFFSETS):
        arrived = from_behind(remote_low[slot], "seq", offset)
        requester = jnp.clip(position - offset, 0, axis_size - 1)
        totals = deposit(totals, slot, requester, arrived, 1.0)
    arrived = from_behind_2(remote_low[SLOTS - 1], "seq", half)
    totals = deposit(totals, SLOTS - 1, (position + half) % axis_size, arrived, 1.0)
    block_sums = jnp.concatenate([own_out[2], remote_out[2]], axis=0)
    coarse_grad = jnp.dot(block_sums.T, bucket_hot, precision=HIGHEST)
    flat_sum = fine_sum.reshape(HEADS, TOK_DEV * TILE)
    column_grad = jnp.dot(flat_sum, column_hot.T, precision=HIGHEST)
    row_grad = jnp.dot(flat_sum, row_hot.T, precision=HIGHEST)
    table_grad = jnp.concatenate([coarse_grad, column_grad, row_grad], axis=1)
    summed = lax.psum(table_grad, "seq")
    table_out = lax.psum_scatter(summed, "dp", scatter_dimension=0, tiled=True)
    query_out = query_grad.reshape(1, TOK_DEV, WIDTH).astype(jnp.bfloat16)
    key_out = totals[0].reshape(1, TOK_DEV, WIDTH).astype(jnp.bfloat16)
    value_out = totals[1].reshape(1, TOK_DEV, WIDTH).astype(jnp.bfloat16)
    return (query_out, key_out, value_out, table_out)


def solution(mesh):
    count = mesh.shape["seq"]
    windows = mesh.shape["dp"]
    whole = HEADS % (3 * count) == 0 and count > 2 and count & (count - 1) == 0 and windows & (windows - 1) == 0
    plan = by_heads if whole else by_tiles
    return jax.shard_map(
        plan,
        mesh=mesh,
        in_specs=(
            P("dp", "seq", None),
            P("dp", "seq", None),
            P("dp", "seq", None),
            P("dp", "seq", None),
            P("dp", None),
            P(),
            P("seq", None),
            P("seq", None),
        ),
        out_specs=(P("dp", "seq", None), P("dp", "seq", None), P("dp", "seq", None), P("dp", None)),
        check_vma=False,
    )
```

```python
import functools

import jax
import jax.numpy as jnp
from jax import lax
from jax.experimental import pallas as pl
from jax.experimental.pallas import tpu as pltpu
from jax.sharding import PartitionSpec as P

HEADS = 24
HEAD_DIM = 128
TOK_DEV = 256
TILE = 128
TILE_COLS = 16
SLOTS = 5
BUCKETS = 82
WIDTH = 3072
TILES_DEV = 2
ENTRIES = TILES_DEV + SLOTS
TILE_ROWS = TILE // TILE_COLS
COLUMN_WIDTH = 2 * TILE_COLS - 1
ROW_WIDTH = 2 * TILE_ROWS - 1

NEGATIVE = -1e30
HIGHEST = lax.Precision.HIGHEST
NEAR_OFFSETS = (-1, 1, -2, 2)
LOG2E = 1.4426950408889634
SCALE = HEAD_DIM ** (-0.5)
VMEM_LIMIT = 63 * 1024 * 1024


SIZES = (1, 2, 4, 5, 6, ENTRIES)
ABSOLUTE = 1 << 16
STAMP = 32
META = 16
HBM = pl.BlockSpec(memory_space=pltpu.HBM)
SMEM = pl.BlockSpec(memory_space=pltpu.SMEM)


def pack_body(number, heads, first, count, targets, *refs):
    place_ref, live_ref, bucket_ref = refs[:3]
    arrays = refs[3 : 3 + number]
    outs = refs[3 + number : -4]
    held_ref, meta_ref, in_sem, out_sem = refs[-4:]
    width = heads * HEAD_DIM
    position = place_ref[0]
    span = pl.ds(first * HEAD_DIM, count * width)
    arriving = [
        pltpu.make_async_copy(arrays[a].at[:, span], held_ref.at[a], in_sem.at[a])
        for a in range(number)
    ]
    for copy in arriving:
        copy.start()
    row = lax.broadcasted_iota(jnp.int32, (META, width), 0)
    lane = lax.broadcasted_iota(jnp.int32, (META, width), 1)
    meta = jnp.zeros((META, width), jnp.int32)
    for e in range(ENTRIES):
        meta = jnp.where((row == e) & (lane == 0), bucket_ref[0, e], meta)
        meta = jnp.where((row == e) & (lane == 1), live_ref[0, e], meta)
    meta_ref[...] = meta.astype(jnp.float32).astype(jnp.bfloat16)
    columns, messages = [], []
    for k, (out, at) in targets.items():
        column = (k - ABSOLUTE) * width if k >= ABSOLUTE else (position ^ k) * width
        columns.append(column if k >= ABSOLUTE else pl.multiple_of(column, HEAD_DIM))
        messages.append(outs[out] if at is None else outs[out].at[at])
    leaving = [
        pltpu.make_async_copy(meta_ref, message.at[pl.ds(number * TOK_DEV, META)], out_sem)
        for message in messages
    ]
    for copy in leaving:
        copy.start()
    for a in range(number):
        arriving[a].wait()
        for message, column in zip(messages, columns):
            leaving.append(
                pltpu.make_async_copy(
                    held_ref.at[a, :, pl.ds(column, width)],
                    message.at[pl.ds(a * TOK_DEV, TOK_DEV)],
                    out_sem,
                )
            )
            leaving[-1].start()
    for copy in leaving:
        copy.wait()


def pack(place, live, buckets, arrays, first, heads, count, targets, sizes):
    number = len(arrays)
    rows = number * TOK_DEV + META
    width = heads * HEAD_DIM
    return pl.pallas_call(
        functools.partial(pack_body, number, heads, first, count, targets),
        in_specs=[SMEM] * 3 + [HBM] * number,
        out_specs=[HBM] * len(sizes),
        out_shape=[
            jax.ShapeDtypeStruct((() if size is None else (size,)) + (rows, width), jnp.bfloat16)
            for size in sizes
        ],
        scratch_shapes=[
            pltpu.VMEM((number, TOK_DEV, count * width), jnp.bfloat16),
            pltpu.VMEM((META, width), jnp.bfloat16),
            pltpu.SemaphoreType.DMA((number,)),
            pltpu.SemaphoreType.DMA,
        ],
        compiler_params=pltpu.CompilerParams(vmem_limit_bytes=VMEM_LIMIT),
        cost_estimate=pl.CostEstimate(
            flops=0, bytes_accessed=4 * count * rows * width, transcendentals=0
        ),
    )(place, live, buckets, *arrays)


def unpack_body(number, heads, first, count, held, owned, *refs):
    place_ref = refs[0]
    pairs = count // 2
    blocks = [refs[1 + k // 2].at[k % 2] for k in range(count)]
    outs = refs[1 + pairs + held : 1 + pairs + held + number]
    scratch = refs[1 + pairs + held + number :]
    if owned:
        table_ref, held_ref, in_sem, out_sem, stamp_ref, whole_ref, stamp_sem = scratch
        stamps = [
            pltpu.make_async_copy(
                blocks[k].at[pl.ds(number * TOK_DEV, STAMP)], stamp_ref.at[k], stamp_sem
            )
            for k in range(count)
        ]
    else:
        held_ref, in_sem, out_sem = scratch
    width = heads * HEAD_DIM
    position = place_ref[0]
    arriving, leaving = [], []
    for k in range(count):
        column = pl.multiple_of(first * HEAD_DIM + (position ^ k) * width, HEAD_DIM)
        for a in range(number):
            n = k * number + a
            arriving.append(
                pltpu.make_async_copy(
                    blocks[k].at[pl.ds(a * TOK_DEV, TOK_DEV)], held_ref.at[n], in_sem.at[n]
                )
            )
            leaving.append(
                pltpu.make_async_copy(
                    held_ref.at[n], outs[a].at[:, pl.ds(column, width)], out_sem
                )
            )
            arriving[n].start()
    if owned:
        for copy in stamps:
            copy.start()
    for n in range(count * number):
        arriving[n].wait()
        leaving[n].start()
    if owned:
        for copy in stamps:
            copy.wait()
        each = HEADS // count
        for k in range(count):
            parts = stamp_ref[k].astype(jnp.float32)
            rows = parts[0:each] + parts[each : 2 * each] + parts[2 * each : 3 * each]
            source = position ^ k
            for r in range(each):
                head = source * (each - heads) + r if r < each - heads else first + source * heads + r - (each - heads)
                whole_ref[pl.ds(head, 1)] = rows[r : r + 1]
        for r in range(owned):
            table_ref[r : r + 1] = whole_ref[pl.ds(place_ref[1] * owned + r, 1)]
    for copy in leaving:
        copy.wait()


def unpack(place, blocks, number, first, heads, onto, owned):
    pairs = len(blocks)
    count = 2 * pairs
    held = 0 if onto is None else number
    out_specs = [HBM] * number
    out_shape = [jax.ShapeDtypeStruct((TOK_DEV, WIDTH), jnp.bfloat16)] * number
    scratch_shapes = [
        pltpu.VMEM((count * number, TOK_DEV, heads * HEAD_DIM), jnp.bfloat16),
        pltpu.SemaphoreType.DMA((count * number,)),
        pltpu.SemaphoreType.DMA,
    ]
    if owned:
        out_specs = out_specs + [pl.BlockSpec(memory_space=pltpu.VMEM)]
        out_shape = out_shape + [jax.ShapeDtypeStruct((owned, TILE), jnp.float32)]
        scratch_shapes += [
            pltpu.VMEM((count, STAMP, heads * HEAD_DIM), jnp.bfloat16),
            pltpu.VMEM((HEADS, TILE), jnp.float32),
            pltpu.SemaphoreType.DMA,
        ]
    return pl.pallas_call(
        functools.partial(unpack_body, number, heads, first, count, held, owned),
        in_specs=[SMEM] + [HBM] * (pairs + held),
        out_specs=out_specs,
        out_shape=out_shape,
        input_output_aliases={1 + pairs + a: a for a in range(held)},
        scratch_shapes=scratch_shapes,
        compiler_params=pltpu.CompilerParams(vmem_limit_bytes=VMEM_LIMIT),
        cost_estimate=pl.CostEstimate(
            flops=0, bytes_accessed=4 * count * number * TOK_DEV * heads * HEAD_DIM, transcendentals=0
        ),
    )(place, *blocks, *(onto if onto is not None else ()))


def merge_body(pairs, rows, stamped, *refs):
    cross_ref = refs[0]
    outs = refs[1 + stamped + pairs : 1 + stamped + 2 * pairs]
    held_ref, low_ref, in_sem, out_sem = refs[1 + stamped + 2 * pairs :]
    arriving = [
        pltpu.make_async_copy(
            cross_ref.at[d], held_ref.at[d, pl.ds(0, rows)], in_sem.at[d]
        )
        for d in range(pairs)
    ]
    for copy in arriving:
        copy.start()
    leaving = []
    if stamped:
        low_ref[...] = jnp.zeros_like(low_ref)
        for s in range(2):
            rest = refs[1][s]
            number = rest.shape[0]
            for part in range(3):
                low = rest.astype(jnp.bfloat16).astype(jnp.float32)
                low_ref[s, part * number : (part + 1) * number] = low
                rest = rest - low
        whole = low_ref[...].astype(jnp.bfloat16)
        held_ref[0:2, rows : rows + STAMP] = whole
        for d in range(pairs):
            leaving += [
                pltpu.make_async_copy(
                    held_ref.at[s, pl.ds(rows, STAMP)], outs[d].at[s, pl.ds(rows, STAMP)], out_sem
                )
                for s in range(2)
            ]
            leaving[-2].start()
            leaving[-1].start()
    for d in range(pairs):
        arriving[d].wait()
        leaving.append(
            pltpu.make_async_copy(
                held_ref.at[d, pl.ds(0, rows)], outs[d].at[1, pl.ds(0, rows)], out_sem
            )
        )
        leaving[-1].start()
    for copy in leaving:
        copy.wait()


def merge(cross, messages, table_rows):
    pairs, rows, width = cross.shape
    stamped = 0 if table_rows is None else 1
    shape = messages[0].shape
    return pl.pallas_call(
        functools.partial(merge_body, pairs, rows, stamped),
        in_specs=[HBM] + [pl.BlockSpec(memory_space=pltpu.VMEM)] * stamped + [HBM] * pairs,
        out_specs=[HBM] * pairs,
        out_shape=[jax.ShapeDtypeStruct(shape, jnp.bfloat16)] * pairs,
        input_output_aliases={1 + stamped + d: d for d in range(pairs)},
        scratch_shapes=[
            pltpu.VMEM((pairs,) + shape[1:], jnp.bfloat16),
            pltpu.VMEM((2, STAMP, TILE), jnp.float32),
            pltpu.SemaphoreType.DMA((pairs,)),
            pltpu.SemaphoreType.DMA,
        ],
        compiler_params=pltpu.CompilerParams(vmem_limit_bytes=VMEM_LIMIT),
        cost_estimate=pl.CostEstimate(
            flops=0, bytes_accessed=4 * cross.size, transcendentals=0
        ),
    )(cross, *(() if table_rows is None else (table_rows,)), *messages)


def fold(array, combine):
    parts = [array[r : r + 8] for r in range(0, array.shape[0], 8)]
    while len(parts) > 1:
        parts = [combine(parts[2 * k], parts[2 * k + 1]) for k in range(len(parts) // 2)]
    return parts[0]


def grad_body(count, heads, sources, *refs):
    place_ref, slots_ref, table_ref, bias_ref = refs[:4]
    refs = refs[4:]
    inputs = 1 + max(source for source, _ in sources.values())
    blocks, refs = refs[:inputs], refs[inputs:]
    cross_ref, refs = refs[0], refs[1:]
    pairs, refs = refs[: count // 2], refs[count // 2 :]
    outs = [(pairs[k // 2].at[0], cross_ref.at[k // 2])[k % 2] for k in range(count)]
    fine_ref, coarse_out_ref = refs[:2]
    (
        x_ref,
        y_ref,
        coarse_ref,
        sums_ref,
        score_ref,
        product_ref,
        low_ref,
        key_ref,
        key_grad_ref,
        value_grad_ref,
        in_sem,
        out_sem,
        list_ref,
        tile_ref,
        number_ref,
    ) = refs[2:]
    position = place_ref[0]

    def lanes(h):
        return pl.ds(h * HEAD_DIM, HEAD_DIM)

    arriving = []
    for h in range(heads):
        arriving.append([])
        for k, (source, at) in sources.items():
            block = blocks[source] if at is None else blocks[source].at[at]
            tile = k - ABSOLUTE if k >= ABSOLUTE else position ^ k
            arriving[h].append(
                pltpu.make_async_copy(
                    block.at[:, lanes(h)], x_ref.at[tile, :, lanes(h)], in_sem.at[h]
                )
            )
    leaving = [
        pltpu.make_async_copy(
            y_ref.at[position ^ k, :, lanes(h)],
            outs[k].at[pl.ds(0, 3 * TOK_DEV), lanes(h)],
            out_sem,
        )
        for h in range(heads)
        for k in range(count)
    ]
    for copies in arriving:
        for copy in copies:
            copy.start()
    lane = lax.broadcasted_iota(jnp.int32, (8, TILE), 1)
    transposed = (((1,), (1,)), ((), ()))

    def array_rows(a, begin=0, size=TOK_DEV):
        return pl.ds(a * TOK_DEV + begin, size)

    def meta_of(i):
        meta = x_ref[i, 4 * TOK_DEV : 4 * TOK_DEV + META, 0:TILE].astype(jnp.float32)[:8]
        hot = (lane == meta[:, 0:1].astype(jnp.int32)).astype(jnp.float32)
        return hot, meta[:, 1:2]

    def list_live(i, flag):
        row = lax.broadcasted_iota(jnp.int32, (8, 1), 0)
        code = jnp.sum(jnp.where(flag > 0, 1 << row, 0).astype(jnp.float32)).astype(jnp.int32)
        for e in range(8):
            list_ref[i * 8 + e] = ENTRIES
            tile_ref[i * 8 + e] = (
                slots_ref[i, e - TILES_DEV]
                if TILES_DEV <= e < ENTRIES
                else i * TILES_DEV + e % TILES_DEV
            )
        number = jnp.int32(0)
        for e in range(ENTRIES):
            list_ref[i * 8 + number] = e
            number = number + ((code >> e) & 1)
        list_ref[i * 8 + number] = ENTRIES
        number_ref[i] = number

    every = range(heads)
    columns = [slice(h * HEAD_DIM, (h + 1) * HEAD_DIM) for h in every]
    tiles_all = count * TILES_DEV
    key_grad_ref[...] = jnp.zeros_like(key_grad_ref)
    value_grad_ref[...] = jnp.zeros_like(value_grad_ref)
    fine_ref[...] = jnp.zeros_like(fine_ref)
    sums_ref[...] = jnp.zeros_like(sums_ref)
    for h in every:
        for copy in arriving[h]:
            copy.wait()
    for i in range(count):
        hot, flag = meta_of(i)
        list_live(i, flag)
        for h in every:
            coarse = jnp.sum(hot * table_ref[h : h + 1, :], axis=1, keepdims=True) * LOG2E
            coarse = jnp.where(flag > 0, coarse, NEGATIVE)
            coarse_ref[h, i] = jnp.broadcast_to(coarse, (8, TOK_DEV))

    def query_tile(i, size):
        query = [x_ref[i, array_rows(0), columns[h]] for h in every]
        upstream = [x_ref[i, array_rows(3), columns[h]] for h in every]
        entries = [list_ref[i * 8 + s] for s in range(size)]
        tiles = [tile_ref[i * 8 + e] for e in entries]
        coarse = [[coarse_ref[h, i, pl.ds(e, 1)] for e in entries] for h in every]

        def tile_of(a, s, h):
            begin = pl.multiple_of(a * TOK_DEV + (tiles[s] % TILES_DEV) * TILE, TILE)
            return x_ref[tiles[s] // TILES_DEV, pl.ds(begin, TILE), columns[h]]

        tops = []
        for h in every:
            top = None
            for s in range(size):
                key = tile_of(1, s, h)
                key_ref[h, s * TILE : (s + 1) * TILE] = key
                raw = lax.dot_general(
                    key, query[h], transposed, preferred_element_type=jnp.float32
                )
                score = raw * (SCALE * LOG2E) + bias_ref[h]
                score_ref[h, s] = score
                best = fold(score, jnp.maximum) + coarse[h][s]
                top = best if top is None else jnp.maximum(top, best)
            tops.append(jnp.max(top, axis=0, keepdims=True))
        inverses, deltas = [], []
        for h in every:
            total = jnp.zeros((8, TOK_DEV), jnp.float32)
            weighted = jnp.zeros((8, TOK_DEV), jnp.float32)
            for s in range(size):
                product = lax.dot_general(
                    tile_of(2, s, h), upstream[h], transposed, preferred_element_type=jnp.float32
                )
                expo = jnp.exp2(score_ref[h, s] - (tops[h] - coarse[h][s]))
                score_ref[h, s] = expo
                product_ref[h, s] = product
                total = total + fold(expo, jnp.add)
                weighted = weighted + fold(expo * product, jnp.add)
            inverses.append(1.0 / jnp.sum(total, axis=0, keepdims=True))
            deltas.append(jnp.sum(weighted, axis=0, keepdims=True) * inverses[h])
        for h in every:
            for s in range(size):
                attend = score_ref[h, s] * inverses[h]
                grad = attend * (product_ref[h, s] - deltas[h])
                fine_ref[h] += grad
                sums = jnp.sum(fold(grad, jnp.add), axis=0, keepdims=True)
                sums_ref[h, i, pl.ds(entries[s], 1)] = sums[:, :TILE] + sums[:, TILE:]
                grad_low = grad.astype(jnp.bfloat16)
                low_ref[h, s * TILE : (s + 1) * TILE] = grad_low
                value_grad_ref[h * tiles_all + tiles[s]] += jnp.dot(
                    attend.astype(jnp.bfloat16), upstream[h], preferred_element_type=jnp.float32
                )
                key_grad_ref[h * tiles_all + tiles[s]] += jnp.dot(
                    grad_low, query[h], preferred_element_type=jnp.float32
                )
        for h in every:
            query_grad = lax.dot_general(
                key_ref[h, : size * TILE],
                low_ref[h, : size * TILE],
                (((0,), (0,)), ((), ())),
                preferred_element_type=jnp.float32,
            )
            y_ref[i, array_rows(0), columns[h]] = (query_grad.T * SCALE).astype(jnp.bfloat16)

    @pl.loop(0, count)
    def _(i):
        number = number_ref[i]
        below = 0
        for size in SIZES:
            pl.when((number > below) & (number <= size))(functools.partial(query_tile, i, size))
            below = size

    for h in every:

        @pl.loop(0, count)
        def _(i):
            for t in range(TILES_DEV):
                tile = h * tiles_all + i * TILES_DEV + t
                y_ref[i, array_rows(1, t * TILE, TILE), columns[h]] = (
                    key_grad_ref[tile] * SCALE
                ).astype(jnp.bfloat16)
                y_ref[i, array_rows(2, t * TILE, TILE), columns[h]] = value_grad_ref[tile].astype(
                    jnp.bfloat16
                )

        for copy in leaving[h * count : (h + 1) * count]:
            copy.start()

    for h in every:
        coarse_grad = jnp.zeros((1, TILE), jnp.float32)
        for i in range(count):
            hot, _ = meta_of(i)
            sums = jnp.sum(sums_ref[h, i], axis=1, keepdims=True)
            coarse_grad = coarse_grad + jnp.sum(hot * sums, axis=0, keepdims=True)
        coarse_out_ref[h : h + 1] = coarse_grad

    for copy in leaving:
        copy.wait()


def window_grads(place, slots, table, bias, blocks, sources, count, more):
    heads = table.shape[0]
    width = heads * HEAD_DIM
    rows = 3 * TOK_DEV
    pairs = count // 2
    work = heads * count * ENTRIES * TILE * TOK_DEV
    vmem = pl.BlockSpec(memory_space=pltpu.VMEM)
    results = pl.pallas_call(
        functools.partial(grad_body, count, heads, sources),
        in_specs=[SMEM, SMEM, vmem, vmem] + [HBM] * len(blocks),
        out_specs=[HBM] * (1 + pairs) + [vmem] * 2,
        out_shape=[jax.ShapeDtypeStruct((pairs, rows, width), jnp.bfloat16)]
        + [jax.ShapeDtypeStruct((2, rows + more, width), jnp.bfloat16)] * pairs
        + [
            jax.ShapeDtypeStruct((heads, TILE, TOK_DEV), jnp.float32),
            jax.ShapeDtypeStruct((heads, TILE), jnp.float32),
        ],
        scratch_shapes=[
            pltpu.VMEM((count, 4 * TOK_DEV + META, width), jnp.bfloat16),
            pltpu.VMEM((count, rows, width), jnp.bfloat16),
            pltpu.VMEM((heads, count, 8, TOK_DEV), jnp.float32),
            pltpu.VMEM((heads, count, 8, TILE), jnp.float32),
            pltpu.VMEM((heads, ENTRIES, TILE, TOK_DEV), jnp.float32),
            pltpu.VMEM((heads, ENTRIES, TILE, TOK_DEV), jnp.float32),
            pltpu.VMEM((heads, ENTRIES * TILE, TOK_DEV), jnp.bfloat16),
            pltpu.VMEM((heads, ENTRIES * TILE, HEAD_DIM), jnp.bfloat16),
            pltpu.VMEM((heads * count * TILES_DEV, TILE, HEAD_DIM), jnp.float32),
            pltpu.VMEM((heads * count * TILES_DEV, TILE, HEAD_DIM), jnp.float32),
            pltpu.SemaphoreType.DMA((heads,)),
            pltpu.SemaphoreType.DMA,
            pltpu.SMEM((count * 8,), jnp.int32),
            pltpu.SMEM((count * 8,), jnp.int32),
            pltpu.SMEM((count,), jnp.int32),
        ],
        compiler_params=pltpu.CompilerParams(vmem_limit_bytes=VMEM_LIMIT),
        cost_estimate=pl.CostEstimate(
            flops=10 * work * HEAD_DIM,
            bytes_accessed=2 * 7 * count * TOK_DEV * width,
            transcendentals=work,
        ),
    )(place, slots, table, bias, *blocks)
    return results[0], list(results[1 : 1 + pairs]), results[1 + pairs], results[2 + pairs]


def fine_bias_of(columns, rows):
    heads = columns.shape[0]
    column = jnp.stack(
        [columns[:, TILE_COLS - 1 - a : 2 * TILE_COLS - 1 - a] for a in range(TILE_COLS)], axis=2
    )
    row = jnp.stack(
        [rows[:, TILE_ROWS - 1 - a : 2 * TILE_ROWS - 1 - a] for a in range(TILE_ROWS)], axis=2
    )
    row = jnp.tile(row, (1, 1, TOK_DEV // TILE))
    column = jnp.tile(column, (1, TILE_ROWS, TOK_DEV // TILE_COLS))
    row = jnp.repeat(jnp.repeat(row, TILE_COLS, axis=1), TILE_COLS, axis=2)
    return (column + row).reshape(heads, TILE, TOK_DEV)


def fine_grads_of(fine):
    heads = fine.shape[0]
    groups = TOK_DEV // TILE
    split = fine.reshape(heads, TILE_ROWS, TILE_COLS, groups, TILE_ROWS, TILE_COLS)
    column = jnp.sum(split, axis=(1, 3, 4)).reshape(heads, -1)
    row = jnp.sum(split, axis=(2, 3, 5)).reshape(heads, -1)

    def hot(size):
        at = jnp.arange(size, dtype=jnp.int32)
        offset = (at[:, None] - at[None, :] + size - 1).reshape(-1, 1)
        return (offset == jnp.arange(2 * size - 1, dtype=jnp.int32)[None, :]).astype(jnp.float32)

    column = jnp.dot(column, hot(TILE_COLS), precision=HIGHEST)
    row = jnp.dot(row, hot(TILE_ROWS), precision=HIGHEST)
    return jnp.concatenate([column, row], axis=1)


def after(array, *others):
    return lax.optimization_barrier((array, *others))[0]


def by_heads(queries, keys, values, grad_out, bias_table, slot_tiles, live, buckets):
    count = lax.axis_size("seq")
    windows = lax.axis_size("dp")
    position = lax.axis_index("seq").astype(jnp.int32)
    place = jnp.stack([position, lax.axis_index("dp").astype(jnp.int32)])
    each = HEADS // count
    chunks = [each - each // 3, each // 3]
    starts = [0, chunks[0] * count]
    arrays = (queries[0], keys[0], values[0], grad_out[0])
    pairs = sorted(range(1, count // 2), key=lambda d: (-bin(d).count("1"), d))
    bent = [d for d in pairs if bin(d).count("1") > 1]
    straight = [d for d in pairs if d not in bent]

    def send(message, k):
        return lax.ppermute(message, "seq", [(i, i ^ k) for i in range(count)])

    def packed(where, chunk, targets, sizes):
        return list(
            pack(where, live, buckets, arrays, starts[chunk], chunks[chunk], count, targets, sizes)
        )

    def grads_of(chunk, blocks, sources, more):
        row = starts[chunk] + position * chunks[chunk]
        part = lax.dynamic_slice_in_dim(table, row, chunks[chunk], 0)
        bias = fine_bias_of(
            part[:, BUCKETS : BUCKETS + COLUMN_WIDTH], part[:, BUCKETS + COLUMN_WIDTH :]
        )
        return window_grads(
            place, slot_tiles, part, bias * LOG2E, blocks, sources, count, more
        )

    def table_rows(fine, coarse):
        return jnp.concatenate([coarse[:, :BUCKETS], fine_grads_of(fine)], axis=1)

    table = bias_table
    step = 1
    while step < windows:
        other = lax.ppermute(table, "dp", [(i, i ^ step) for i in range(windows)])
        table = jnp.where(
            place[1] & step == 0,
            jnp.concatenate([table, other], axis=0),
            jnp.concatenate([other, table], axis=0),
        )
        step *= 2

    held = [0] + straight
    targets = {2 * d: (i, 0) for i, d in enumerate(held)}
    targets.update({2 * d + 1: (len(held), i) for i, d in enumerate(held)})
    direct = [2 * d + core for core in range(2) for d in bent]
    targets.update({k: (len(held) + 1 + i, None) for i, k in enumerate(direct)})
    first = packed(place, 0, targets, [2] * len(held) + [len(held)] + [None] * len(direct))
    ready, cross, single = first[: len(held)], first[len(held)], first[len(held) + 1 :]
    half = len(bent)
    single[:half] = [send(m, k) for m, k in zip(single[:half], direct[:half])]
    ready = list(merge(send(cross, 1), ready, None))
    single[half:] = [send(after(m, ready[0]), k) for m, k in zip(single[half:], direct[half:])]
    ready[1:] = [send(m, 2 * d) for m, d in zip(ready[1:], straight)]
    sources = {2 * d + core: (i, core) for i, d in enumerate(held) for core in range(2)}
    sources.update({k: (len(held) + i, None) for i, k in enumerate(direct)})
    every = {ABSOLUTE + i: (0, i) for i in range(count)}
    (second,) = packed(after(place, ready[0]), 1, every, [count])
    second = lax.all_to_all(after(second, *ready[1:]), "seq", 0, 0)
    cross, first, fine, coarse = grads_of(0, ready + single, sources, 0)

    first_rows = table_rows(fine, coarse)
    first = list(merge(send(cross, 1), first, None))
    for d in pairs:
        first[d] = send(first[d], 2 * d)
    cross, second, fine, coarse = grads_of(1, [second], every, STAMP)
    rows = jnp.concatenate([first_rows, table_rows(fine, coarse)], axis=0)
    step = 1
    while step < windows:
        rows = rows + lax.ppermute(rows, "dp", [(i, i ^ step) for i in range(windows)])
        step *= 2
    second = list(merge(send(cross, 1), second, jnp.stack([rows, send(rows, 1)])))
    for d in pairs:
        second[d] = send(second[d], 2 * d)
    outs = unpack(place, first, 3, starts[0], chunks[0], None, 0)
    outs = unpack(place, second, 3, starts[1], chunks[1], outs, bias_table.shape[0])
    return (outs[0][None], outs[1][None], outs[2][None], outs[3])


def from_behind(block, axis, distance):
    devices = range(lax.axis_size(axis))
    route = [(i - distance, i) for i in devices if i - distance in devices]
    return lax.ppermute(block, axis, route)


def from_behind_2(value, axis, by):
    count = lax.axis_size(axis)
    return lax.ppermute(value, axis, [(i, (i + by) % count) for i in range(count)])


def offset_hots():
    tile_rows = TILE // TILE_COLS
    query_pos = jnp.arange(TOK_DEV, dtype=jnp.int32)[:, None]
    key_pos = jnp.arange(TILE, dtype=jnp.int32)[None, :]
    column_index = key_pos % TILE_COLS - query_pos % TILE_COLS + TILE_COLS - 1
    row_index = key_pos // TILE_COLS - query_pos // TILE_COLS % tile_rows + tile_rows - 1
    column_hot = (
        column_index.reshape(1, -1) == jnp.arange(2 * TILE_COLS - 1, dtype=jnp.int32)[:, None]
    ).astype(jnp.float32)
    row_hot = (
        row_index.reshape(1, -1) == jnp.arange(2 * tile_rows - 1, dtype=jnp.int32)[:, None]
    ).astype(jnp.float32)
    return (column_hot, row_hot)


def by_tiles(queries, keys, values, grad_out, bias_table, slot_tiles, live, buckets):
    axis_size = lax.axis_size("seq")
    position = lax.axis_index("seq")
    half = axis_size // 2
    scale = HEAD_DIM ** (-0.5)
    column_width = 2 * TILE_COLS - 1
    table = lax.all_gather(bias_table, "dp", axis=0, tiled=True)
    column_hot, row_hot = offset_hots()
    fine_bias = jnp.dot(table[:, BUCKETS : BUCKETS + column_width], column_hot, precision=HIGHEST)
    fine_bias = fine_bias + jnp.dot(table[:, BUCKETS + column_width :], row_hot, precision=HIGHEST)
    fine_bias = fine_bias.reshape(HEADS, TOK_DEV, TILE)
    bucket_hot = (buckets[0][:, None] == jnp.arange(BUCKETS, dtype=jnp.int32)[None, :]).astype(
        jnp.float32
    )
    coarse = jnp.dot(bucket_hot, table[:, :BUCKETS].T, precision=HIGHEST)
    alive = live[0].astype(jnp.float32)
    query_heads = queries[0].reshape(TOK_DEV, HEADS, HEAD_DIM)
    upstream_heads = grad_out[0].reshape(TOK_DEV, HEADS, HEAD_DIM)
    own_pairs = jnp.stack(
        [keys[0].reshape(TILES_DEV, TILE, WIDTH), values[0].reshape(TILES_DEV, TILE, WIDTH)], axis=1
    )

    def requested(slot, requester):
        wanted = jnp.clip(slot_tiles[requester, slot] - position * TILES_DEV, 0, TILES_DEV - 1)
        return lax.dynamic_index_in_dim(own_pairs, wanted, 0, keepdims=False)

    fetched = []
    for slot, offset in enumerate(NEAR_OFFSETS):
        requester = jnp.clip(position - offset, 0, axis_size - 1)
        fetched.append(from_behind(requested(slot, requester), "seq", -offset))
    far_requester = (position + half) % axis_size
    fetched.append(from_behind_2(requested(SLOTS - 1, far_requester), "seq", half))
    remote_pairs = jnp.stack(fetched)
    own_group = (own_pairs, coarse[:TILES_DEV], alive[:TILES_DEV])
    remote_group = (remote_pairs, coarse[TILES_DEV:], alive[TILES_DEV:])

    def scores_of(pair, coarse_row):
        key_heads = pair[0].reshape(TILE, HEADS, HEAD_DIM)
        raw = jnp.einsum("qhd,khd->hqk", query_heads, key_heads, preferred_element_type=jnp.float32)
        return raw * scale + coarse_row[:, None, None] + fine_bias

    def products_of(pair):
        value_heads = pair[1].reshape(TILE, HEADS, HEAD_DIM)
        return jnp.einsum(
            "qhd,khd->hqk", upstream_heads, value_heads, preferred_element_type=jnp.float32
        )

    def stats_step(carry, item):
        top, total, weighted = carry
        pair, coarse_row, flag = item
        scores = scores_of(pair, coarse_row)
        attend_grad = products_of(pair)
        keep = flag > 0
        new_top = jnp.where(keep, jnp.maximum(top, jnp.max(scores, axis=2, keepdims=True)), top)
        factor = jnp.exp(top - new_top)
        expo = jnp.exp(scores - new_top) * flag
        added = jnp.sum(expo, axis=2, keepdims=True)
        added_weighted = jnp.sum(expo * attend_grad, axis=2, keepdims=True)
        return ((new_top, total * factor + added, weighted * factor + added_weighted), None)

    stats = (
        jnp.full((HEADS, TOK_DEV, 1), NEGATIVE, jnp.float32),
        jnp.zeros((HEADS, TOK_DEV, 1), jnp.float32),
        jnp.zeros((HEADS, TOK_DEV, 1), jnp.float32),
    )
    stats, _ = lax.scan(stats_step, stats, own_group)
    stats, _ = lax.scan(stats_step, stats, remote_group)
    log_total = stats[0] + jnp.log(stats[1])
    delta = stats[2] / stats[1]

    def grad_step(carry, item):
        query_grad, fine_sum = carry
        pair, coarse_row, flag = item
        scores = scores_of(pair, coarse_row)
        attend = jnp.exp(scores - log_total) * flag
        attend_grad = products_of(pair)
        score_grad = attend * (attend_grad - delta)
        attend_low = attend.astype(jnp.bfloat16)
        grad_low = score_grad.astype(jnp.bfloat16)
        key_heads = pair[0].reshape(TILE, HEADS, HEAD_DIM)
        value_part = jnp.einsum(
            "hqk,qhd->khd", attend_low, upstream_heads, preferred_element_type=jnp.float32
        ).reshape(TILE, WIDTH)
        key_part = (
            jnp.einsum(
                "hqk,qhd->khd", grad_low, query_heads, preferred_element_type=jnp.float32
            ).reshape(TILE, WIDTH)
            * scale
        )
        query_grad = (
            query_grad
            + jnp.einsum("hqk,khd->qhd", grad_low, key_heads, preferred_element_type=jnp.float32)
            * scale
        )
        return (
            (query_grad, fine_sum + score_grad),
            (key_part, value_part, jnp.sum(score_grad, axis=(1, 2))),
        )

    carry = (
        jnp.zeros((TOK_DEV, HEADS, HEAD_DIM), jnp.float32),
        jnp.zeros((HEADS, TOK_DEV, TILE), jnp.float32),
    )
    carry, own_out = lax.scan(grad_step, carry, own_group)
    carry, remote_out = lax.scan(grad_step, carry, remote_group)
    query_grad, fine_sum = carry
    remote_low = jnp.stack([remote_out[0], remote_out[1]], axis=1).astype(jnp.bfloat16)

    def deposit(totals, slot, requester, arrived, weight):
        wanted = jnp.clip(slot_tiles[requester, slot] - position * TILES_DEV, 0, TILES_DEV - 1)
        pick = (jnp.arange(TILES_DEV, dtype=jnp.int32) == wanted).astype(jnp.float32)[
            :, None, None
        ] * weight
        return (
            totals[0] + pick * arrived[0].astype(jnp.float32)[None],
            totals[1] + pick * arrived[1].astype(jnp.float32)[None],
        )

    totals = (own_out[0], own_out[1])
    for slot, offset in enumerate(NEAR_OFFSETS):
        arrived = from_behind(remote_low[slot], "seq", offset)
        requester = jnp.clip(position - offset, 0, axis_size - 1)
        totals = deposit(totals, slot, requester, arrived, 1.0)
    arrived = from_behind_2(remote_low[SLOTS - 1], "seq", half)
    totals = deposit(totals, SLOTS - 1, (position + half) % axis_size, arrived, 1.0)
    block_sums = jnp.concatenate([own_out[2], remote_out[2]], axis=0)
    coarse_grad = jnp.dot(block_sums.T, bucket_hot, precision=HIGHEST)
    flat_sum = fine_sum.reshape(HEADS, TOK_DEV * TILE)
    column_grad = jnp.dot(flat_sum, column_hot.T, precision=HIGHEST)
    row_grad = jnp.dot(flat_sum, row_hot.T, precision=HIGHEST)
    table_grad = jnp.concatenate([coarse_grad, column_grad, row_grad], axis=1)
    summed = lax.psum(table_grad, "seq")
    table_out = lax.psum_scatter(summed, "dp", scatter_dimension=0, tiled=True)
    query_out = query_grad.reshape(1, TOK_DEV, WIDTH).astype(jnp.bfloat16)
    key_out = totals[0].reshape(1, TOK_DEV, WIDTH).astype(jnp.bfloat16)
    value_out = totals[1].reshape(1, TOK_DEV, WIDTH).astype(jnp.bfloat16)
    return (query_out, key_out, value_out, table_out)


def solution(mesh):
    count = mesh.shape["seq"]
    windows = mesh.shape["dp"]
    whole = HEADS % (3 * count) == 0 and count > 2 and count & (count - 1) == 0 and windows & (windows - 1) == 0
    plan = by_heads if whole else by_tiles
    return jax.shard_map(
        plan,
        mesh=mesh,
        in_specs=(
            P("dp", "seq", None),
            P("dp", "seq", None),
            P("dp", "seq", None),
            P("dp", "seq", None),
            P("dp", None),
            P(),
            P("seq", None),
            P("seq", None),
        ),
        out_specs=(P("dp", "seq", None), P("dp", "seq", None), P("dp", "seq", None), P("dp", None)),
        check_vma=False,
    )
```

```python
import functools

import jax
import jax.numpy as jnp
from jax import lax
from jax.experimental import pallas as pl
from jax.experimental.pallas import tpu as pltpu
from jax.sharding import PartitionSpec as P

HEADS = 24
HEAD_DIM = 128
TOK_DEV = 256
TILE = 128
TILE_COLS = 16
SLOTS = 5
BUCKETS = 82
WIDTH = 3072
TILES_DEV = 2
ENTRIES = TILES_DEV + SLOTS
TILE_ROWS = TILE // TILE_COLS
COLUMN_WIDTH = 2 * TILE_COLS - 1
ROW_WIDTH = 2 * TILE_ROWS - 1

NEGATIVE = -1e30
HIGHEST = lax.Precision.HIGHEST
NEAR_OFFSETS = (-1, 1, -2, 2)
LOG2E = 1.4426950408889634
SCALE = HEAD_DIM ** (-0.5)
VMEM_LIMIT = 67000000


SIZES = (1, 2, 4, 5, 6, ENTRIES)
ABSOLUTE = 1 << 16
STAMP = 16
META = 16
HBM = pl.BlockSpec(memory_space=pltpu.HBM)
SMEM = pl.BlockSpec(memory_space=pltpu.SMEM)


def pack_body(number, heads, first, count, targets, *refs):
    live_ref, bucket_ref = refs[:2]
    arrays = refs[2 : 2 + number]
    outs = refs[2 + number : -4]
    held_ref, meta_ref, in_sem, out_sem = refs[-4:]
    width = heads * HEAD_DIM
    position = lax.axis_index("seq")
    span = pl.ds(first * HEAD_DIM, count * width)
    arriving = [
        pltpu.make_async_copy(arrays[a].at[:, span], held_ref.at[a], in_sem.at[a])
        for a in range(number)
    ]
    for copy in arriving:
        copy.start()
    row = lax.broadcasted_iota(jnp.int32, (META, width), 0)
    lane = lax.broadcasted_iota(jnp.int32, (META, width), 1)
    meta = jnp.zeros((META, width), jnp.int32)
    for e in range(ENTRIES):
        meta = jnp.where((row == e) & (lane == 0), bucket_ref[0, e], meta)
        meta = jnp.where((row == e) & (lane == 1), live_ref[0, e], meta)
    meta_ref[...] = meta.astype(jnp.float32).astype(jnp.bfloat16)
    columns, messages = [], []
    for k, (out, at) in targets.items():
        column = (k - ABSOLUTE) * width if k >= ABSOLUTE else (position ^ k) * width
        columns.append(column if k >= ABSOLUTE else pl.multiple_of(column, HEAD_DIM))
        messages.append(outs[out] if at is None else outs[out].at[at])
    leaving = [
        pltpu.make_async_copy(meta_ref, message.at[pl.ds(number * TOK_DEV, META)], out_sem)
        for message in messages
    ]
    for copy in leaving:
        copy.start()
    for a in range(number):
        arriving[a].wait()
        for message, column in zip(messages, columns):
            leaving.append(
                pltpu.make_async_copy(
                    held_ref.at[a, :, pl.ds(column, width)],
                    message.at[pl.ds(a * TOK_DEV, TOK_DEV)],
                    out_sem,
                )
            )
            leaving[-1].start()
    for copy in leaving:
        copy.wait()


def pack(live, buckets, arrays, first, heads, count, targets, sizes):
    number = len(arrays)
    rows = number * TOK_DEV + META
    width = heads * HEAD_DIM
    return pl.pallas_call(
        functools.partial(pack_body, number, heads, first, count, targets),
        in_specs=[SMEM] * 2 + [HBM] * number,
        out_specs=[HBM] * len(sizes),
        out_shape=[
            jax.ShapeDtypeStruct((() if size is None else (size,)) + (rows, width), jnp.bfloat16)
            for size in sizes
        ],
        scratch_shapes=[
            pltpu.VMEM((number, TOK_DEV, count * width), jnp.bfloat16),
            pltpu.VMEM((META, width), jnp.bfloat16),
            pltpu.SemaphoreType.DMA((number,)),
            pltpu.SemaphoreType.DMA,
        ],
        compiler_params=pltpu.CompilerParams(vmem_limit_bytes=VMEM_LIMIT),
        cost_estimate=pl.CostEstimate(
            flops=0, bytes_accessed=4 * count * rows * width, transcendentals=0
        ),
    )(live, buckets, *arrays)


def unpack_body(number, heads, first, count, held, owned, *refs):
    place_ref = refs[0]
    pairs = count // 2
    blocks = [refs[1 + k // 2].at[k % 2] for k in range(count)]
    outs = refs[1 + pairs + held : 1 + pairs + held + number]
    scratch = refs[1 + pairs + held + number :]
    if owned:
        table_ref, held_ref, in_sem, out_sem, stamp_ref, whole_ref, stamp_sem = scratch
        stamps = [
            pltpu.make_async_copy(
                blocks[k].at[pl.ds(number * TOK_DEV, STAMP)], stamp_ref.at[k], stamp_sem
            )
            for k in range(count)
        ]
    else:
        held_ref, in_sem, out_sem = scratch
    width = heads * HEAD_DIM
    position = place_ref[0]
    arriving, leaving = [], []
    for k in range(count):
        column = pl.multiple_of(first * HEAD_DIM + (position ^ k) * width, HEAD_DIM)
        for a in range(number):
            n = k * number + a
            arriving.append(
                pltpu.make_async_copy(
                    blocks[k].at[pl.ds(a * TOK_DEV, TOK_DEV)], held_ref.at[n], in_sem.at[n]
                )
            )
            leaving.append(
                pltpu.make_async_copy(
                    held_ref.at[n], outs[a].at[:, pl.ds(column, width)], out_sem
                )
            )
            arriving[n].start()
    if owned:
        for copy in stamps:
            copy.start()
    for n in range(count * number):
        arriving[n].wait()
        leaving[n].start()
    if owned:
        for copy in stamps:
            copy.wait()
        each = HEADS // count
        for k in range(count):
            parts = stamp_ref[k].astype(jnp.float32)
            rows = parts[0:each] + parts[each : 2 * each] + parts[2 * each : 3 * each]
            source = position ^ k
            for r in range(each):
                head = source * (each - heads) + r if r < each - heads else first + source * heads + r - (each - heads)
                whole_ref[pl.ds(head, 1)] = rows[r : r + 1]
        for r in range(owned):
            table_ref[r : r + 1] = whole_ref[pl.ds(place_ref[1] * owned + r, 1)]
    for copy in leaving:
        copy.wait()


def unpack(place, blocks, number, first, heads, onto, owned):
    pairs = len(blocks)
    count = 2 * pairs
    held = 0 if onto is None else number
    out_specs = [HBM] * number
    out_shape = [jax.ShapeDtypeStruct((TOK_DEV, WIDTH), jnp.bfloat16)] * number
    scratch_shapes = [
        pltpu.VMEM((count * number, TOK_DEV, heads * HEAD_DIM), jnp.bfloat16),
        pltpu.SemaphoreType.DMA((count * number,)),
        pltpu.SemaphoreType.DMA,
    ]
    if owned:
        out_specs = out_specs + [pl.BlockSpec(memory_space=pltpu.VMEM)]
        out_shape = out_shape + [jax.ShapeDtypeStruct((owned, TILE), jnp.float32)]
        scratch_shapes += [
            pltpu.VMEM((count, STAMP, heads * HEAD_DIM), jnp.bfloat16),
            pltpu.VMEM((HEADS, TILE), jnp.float32),
            pltpu.SemaphoreType.DMA,
        ]
    return pl.pallas_call(
        functools.partial(unpack_body, number, heads, first, count, held, owned),
        in_specs=[SMEM] + [HBM] * (pairs + held),
        out_specs=out_specs,
        out_shape=out_shape,
        input_output_aliases={1 + pairs + a: a for a in range(held)},
        scratch_shapes=scratch_shapes,
        compiler_params=pltpu.CompilerParams(vmem_limit_bytes=VMEM_LIMIT),
        cost_estimate=pl.CostEstimate(
            flops=0, bytes_accessed=4 * count * number * TOK_DEV * heads * HEAD_DIM, transcendentals=0
        ),
    )(place, *blocks, *(onto if onto is not None else ()))


def merge_body(pairs, rows, stamped, *refs):
    cross_ref = refs[0]
    outs = refs[1 + stamped + pairs : 1 + stamped + 2 * pairs]
    held_ref, low_ref, in_sem, out_sem = refs[1 + stamped + 2 * pairs :]
    arriving = [
        pltpu.make_async_copy(
            cross_ref.at[d], held_ref.at[d, pl.ds(0, rows)], in_sem.at[d]
        )
        for d in range(pairs)
    ]
    for copy in arriving:
        copy.start()
    leaving = []
    if stamped:
        low_ref[...] = jnp.zeros_like(low_ref)
        for s in range(2):
            rest = refs[1][s]
            number = rest.shape[0]
            for part in range(3):
                low = rest.astype(jnp.bfloat16).astype(jnp.float32)
                low_ref[s, part * number : (part + 1) * number] = low
                rest = rest - low
        whole = low_ref[...].astype(jnp.bfloat16)
        held_ref[0:2, rows : rows + STAMP] = whole
        for d in range(pairs):
            leaving += [
                pltpu.make_async_copy(
                    held_ref.at[s, pl.ds(rows, STAMP)], outs[d].at[s, pl.ds(rows, STAMP)], out_sem
                )
                for s in range(2)
            ]
            leaving[-2].start()
            leaving[-1].start()
    for d in range(pairs):
        arriving[d].wait()
        leaving.append(
            pltpu.make_async_copy(
                held_ref.at[d, pl.ds(0, rows)], outs[d].at[1, pl.ds(0, rows)], out_sem
            )
        )
        leaving[-1].start()
    for copy in leaving:
        copy.wait()


def merge(cross, messages, table_rows):
    pairs, rows, width = cross.shape
    stamped = 0 if table_rows is None else 1
    shape = messages[0].shape
    return pl.pallas_call(
        functools.partial(merge_body, pairs, rows, stamped),
        in_specs=[HBM] + [pl.BlockSpec(memory_space=pltpu.VMEM)] * stamped + [HBM] * pairs,
        out_specs=[HBM] * pairs,
        out_shape=[jax.ShapeDtypeStruct(shape, jnp.bfloat16)] * pairs,
        input_output_aliases={1 + stamped + d: d for d in range(pairs)},
        scratch_shapes=[
            pltpu.VMEM((pairs,) + shape[1:], jnp.bfloat16),
            pltpu.VMEM((2, STAMP, TILE), jnp.float32),
            pltpu.SemaphoreType.DMA((pairs,)),
            pltpu.SemaphoreType.DMA,
        ],
        compiler_params=pltpu.CompilerParams(vmem_limit_bytes=VMEM_LIMIT),
        cost_estimate=pl.CostEstimate(
            flops=0, bytes_accessed=4 * cross.size, transcendentals=0
        ),
    )(cross, *(() if table_rows is None else (table_rows,)), *messages)


def fold(array, combine):
    parts = [array[r : r + 8] for r in range(0, array.shape[0], 8)]
    while len(parts) > 1:
        parts = [combine(parts[2 * k], parts[2 * k + 1]) for k in range(len(parts) // 2)]
    return parts[0]


def grad_body(count, heads, sources, *refs):
    place_ref, slots_ref, table_ref, bias_ref = refs[:4]
    refs = refs[4:]
    inputs = 1 + max(source for source, _ in sources.values())
    blocks, refs = refs[:inputs], refs[inputs:]
    cross_ref, refs = refs[0], refs[1:]
    pairs, refs = refs[: count // 2], refs[count // 2 :]
    outs = [(pairs[k // 2].at[0], cross_ref.at[k // 2])[k % 2] for k in range(count)]
    fine_ref, coarse_out_ref = refs[:2]
    (
        x_ref,
        y_ref,
        coarse_ref,
        sums_ref,
        score_ref,
        product_ref,
        low_ref,
        key_ref,
        key_grad_ref,
        value_grad_ref,
        in_sem,
        out_sem,
        list_ref,
        tile_ref,
        number_ref,
    ) = refs[2:]
    position = place_ref[0]

    def lanes(h):
        return pl.ds(h * HEAD_DIM, HEAD_DIM)

    arriving = []
    for h in range(heads):
        arriving.append([])
        for k, (source, at) in sources.items():
            block = blocks[source] if at is None else blocks[source].at[at]
            tile = k - ABSOLUTE if k >= ABSOLUTE else position ^ k
            arriving[h].append(
                pltpu.make_async_copy(
                    block.at[:, lanes(h)], x_ref.at[tile, :, lanes(h)], in_sem.at[h]
                )
            )
    leaving = [
        pltpu.make_async_copy(
            y_ref.at[position ^ k, :, lanes(h)],
            outs[k].at[pl.ds(0, 3 * TOK_DEV), lanes(h)],
            out_sem,
        )
        for h in range(heads)
        for k in range(count)
    ]
    for copies in arriving:
        for copy in copies:
            copy.start()
    lane = lax.broadcasted_iota(jnp.int32, (8, TILE), 1)
    transposed = (((1,), (1,)), ((), ()))

    def array_rows(a, begin=0, size=TOK_DEV):
        return pl.ds(a * TOK_DEV + begin, size)

    def meta_of(i):
        meta = x_ref[i, 4 * TOK_DEV : 4 * TOK_DEV + META, 0:TILE].astype(jnp.float32)[:8]
        hot = (lane == meta[:, 0:1].astype(jnp.int32)).astype(jnp.float32)
        return hot, meta[:, 1:2]

    def list_live(i, flag):
        row = lax.broadcasted_iota(jnp.int32, (8, 1), 0)
        code = jnp.sum(jnp.where(flag > 0, 1 << row, 0).astype(jnp.float32)).astype(jnp.int32)
        for e in range(8):
            list_ref[i * 8 + e] = ENTRIES
            tile_ref[i * 8 + e] = (
                slots_ref[i, e - TILES_DEV]
                if TILES_DEV <= e < ENTRIES
                else i * TILES_DEV + e % TILES_DEV
            )
        number = jnp.int32(0)
        for e in range(ENTRIES):
            list_ref[i * 8 + number] = e
            number = number + ((code >> e) & 1)
        list_ref[i * 8 + number] = ENTRIES
        number_ref[i] = number

    every = range(heads)
    columns = [slice(h * HEAD_DIM, (h + 1) * HEAD_DIM) for h in every]
    tiles_all = count * TILES_DEV
    key_grad_ref[...] = jnp.zeros_like(key_grad_ref)
    value_grad_ref[...] = jnp.zeros_like(value_grad_ref)
    fine_ref[...] = jnp.zeros_like(fine_ref)
    sums_ref[...] = jnp.zeros_like(sums_ref)
    for h in every:
        for copy in arriving[h]:
            copy.wait()
    for i in range(count):
        hot, flag = meta_of(i)
        list_live(i, flag)
        for h in every:
            coarse = jnp.sum(hot * table_ref[h : h + 1, :], axis=1, keepdims=True) * LOG2E
            coarse = jnp.where(flag > 0, coarse, NEGATIVE)
            coarse_ref[h, i] = jnp.broadcast_to(coarse, (8, TOK_DEV))

    def query_tile(i, size):
        query = [x_ref[i, array_rows(0), columns[h]] for h in every]
        upstream = [x_ref[i, array_rows(3), columns[h]] for h in every]
        entries = [list_ref[i * 8 + s] for s in range(size)]
        tiles = [tile_ref[i * 8 + e] for e in entries]
        coarse = [[coarse_ref[h, i, pl.ds(e, 1)] for e in entries] for h in every]

        def tile_of(a, s, h):
            begin = pl.multiple_of(a * TOK_DEV + (tiles[s] % TILES_DEV) * TILE, TILE)
            return x_ref[tiles[s] // TILES_DEV, pl.ds(begin, TILE), columns[h]]

        tops = []
        for h in every:
            top = None
            for s in range(size):
                key = tile_of(1, s, h)
                key_ref[h, s * TILE : (s + 1) * TILE] = key
                raw = lax.dot_general(
                    key, query[h], transposed, preferred_element_type=jnp.float32
                )
                score = raw * (SCALE * LOG2E) + bias_ref[h]
                score_ref[h, s] = score
                best = fold(score, jnp.maximum) + coarse[h][s]
                top = best if top is None else jnp.maximum(top, best)
            tops.append(jnp.max(top, axis=0, keepdims=True))
        inverses, deltas = [], []
        for h in every:
            total = jnp.zeros((8, TOK_DEV), jnp.float32)
            weighted = jnp.zeros((8, TOK_DEV), jnp.float32)
            for s in range(size):
                product = lax.dot_general(
                    tile_of(2, s, h), upstream[h], transposed, preferred_element_type=jnp.float32
                )
                expo = jnp.exp2(score_ref[h, s] - (tops[h] - coarse[h][s]))
                score_ref[h, s] = expo
                product_ref[h, s] = product
                total = total + fold(expo, jnp.add)
                weighted = weighted + fold(expo * product, jnp.add)
            inverses.append(1.0 / jnp.sum(total, axis=0, keepdims=True))
            deltas.append(jnp.sum(weighted, axis=0, keepdims=True) * inverses[h])
        for h in every:
            for s in range(size):
                attend = score_ref[h, s] * inverses[h]
                grad = attend * (product_ref[h, s] - deltas[h])
                fine_ref[h] += grad
                sums = jnp.sum(fold(grad, jnp.add), axis=0, keepdims=True)
                sums_ref[h, i, pl.ds(entries[s], 1)] = sums[:, :TILE] + sums[:, TILE:]
                grad_low = grad.astype(jnp.bfloat16)
                low_ref[h, s * TILE : (s + 1) * TILE] = grad_low
                value_grad_ref[h * tiles_all + tiles[s]] += jnp.dot(
                    attend.astype(jnp.bfloat16), upstream[h], preferred_element_type=jnp.float32
                )
                key_grad_ref[h * tiles_all + tiles[s]] += jnp.dot(
                    grad_low, query[h], preferred_element_type=jnp.float32
                )
        for h in every:
            query_grad = lax.dot_general(
                key_ref[h, : size * TILE],
                low_ref[h, : size * TILE],
                (((0,), (0,)), ((), ())),
                preferred_element_type=jnp.float32,
            )
            y_ref[i, array_rows(0), columns[h]] = (query_grad.T * SCALE).astype(jnp.bfloat16)

    @pl.loop(0, count)
    def _(i):
        number = number_ref[i]
        below = 0
        for size in SIZES:
            pl.when((number > below) & (number <= size))(functools.partial(query_tile, i, size))
            below = size

    for h in every:

        @pl.loop(0, count)
        def _(i):
            for t in range(TILES_DEV):
                tile = h * tiles_all + i * TILES_DEV + t
                y_ref[i, array_rows(1, t * TILE, TILE), columns[h]] = (
                    key_grad_ref[tile] * SCALE
                ).astype(jnp.bfloat16)
                y_ref[i, array_rows(2, t * TILE, TILE), columns[h]] = value_grad_ref[tile].astype(
                    jnp.bfloat16
                )

        for copy in leaving[h * count : (h + 1) * count]:
            copy.start()

    for h in every:
        coarse_grad = jnp.zeros((1, TILE), jnp.float32)
        for i in range(count):
            hot, _ = meta_of(i)
            sums = jnp.sum(sums_ref[h, i], axis=1, keepdims=True)
            coarse_grad = coarse_grad + jnp.sum(hot * sums, axis=0, keepdims=True)
        coarse_out_ref[h : h + 1] = coarse_grad

    for copy in leaving:
        copy.wait()


def window_grads(place, slots, table, bias, blocks, sources, count, more):
    heads = table.shape[0]
    width = heads * HEAD_DIM
    rows = 3 * TOK_DEV
    pairs = count // 2
    work = heads * count * ENTRIES * TILE * TOK_DEV
    vmem = pl.BlockSpec(memory_space=pltpu.VMEM)
    results = pl.pallas_call(
        functools.partial(grad_body, count, heads, sources),
        in_specs=[SMEM, SMEM, vmem, vmem] + [HBM] * len(blocks),
        out_specs=[HBM] * (1 + pairs) + [vmem] * 2,
        out_shape=[jax.ShapeDtypeStruct((pairs, rows, width), jnp.bfloat16)]
        + [jax.ShapeDtypeStruct((2, rows + more, width), jnp.bfloat16)] * pairs
        + [
            jax.ShapeDtypeStruct((heads, TILE, TOK_DEV), jnp.float32),
            jax.ShapeDtypeStruct((heads, TILE), jnp.float32),
        ],
        scratch_shapes=[
            pltpu.VMEM((count, 4 * TOK_DEV + META, width), jnp.bfloat16),
            pltpu.VMEM((count, rows, width), jnp.bfloat16),
            pltpu.VMEM((heads, count, 8, TOK_DEV), jnp.float32),
            pltpu.VMEM((heads, count, 8, TILE), jnp.float32),
            pltpu.VMEM((heads, ENTRIES, TILE, TOK_DEV), jnp.float32),
            pltpu.VMEM((heads, ENTRIES, TILE, TOK_DEV), jnp.float32),
            pltpu.VMEM((heads, ENTRIES * TILE, TOK_DEV), jnp.bfloat16),
            pltpu.VMEM((heads, ENTRIES * TILE, HEAD_DIM), jnp.bfloat16),
            pltpu.VMEM((heads * count * TILES_DEV, TILE, HEAD_DIM), jnp.float32),
            pltpu.VMEM((heads * count * TILES_DEV, TILE, HEAD_DIM), jnp.float32),
            pltpu.SemaphoreType.DMA((heads,)),
            pltpu.SemaphoreType.DMA,
            pltpu.SMEM((count * 8,), jnp.int32),
            pltpu.SMEM((count * 8,), jnp.int32),
            pltpu.SMEM((count,), jnp.int32),
        ],
        compiler_params=pltpu.CompilerParams(vmem_limit_bytes=VMEM_LIMIT),
        cost_estimate=pl.CostEstimate(
            flops=10 * work * HEAD_DIM,
            bytes_accessed=2 * 7 * count * TOK_DEV * width,
            transcendentals=work,
        ),
    )(place, slots, table, bias, *blocks)
    return results[0], list(results[1 : 1 + pairs]), results[1 + pairs], results[2 + pairs]


def fine_bias_of(columns, rows):
    heads = columns.shape[0]
    column = jnp.stack(
        [columns[:, TILE_COLS - 1 - a : 2 * TILE_COLS - 1 - a] for a in range(TILE_COLS)], axis=2
    )
    row = jnp.stack(
        [rows[:, TILE_ROWS - 1 - a : 2 * TILE_ROWS - 1 - a] for a in range(TILE_ROWS)], axis=2
    )
    row = jnp.tile(row, (1, 1, TOK_DEV // TILE))
    column = jnp.tile(column, (1, TILE_ROWS, TOK_DEV // TILE_COLS))
    row = jnp.repeat(jnp.repeat(row, TILE_COLS, axis=1), TILE_COLS, axis=2)
    return (column + row).reshape(heads, TILE, TOK_DEV)


def fine_grads_of(fine):
    heads = fine.shape[0]
    groups = TOK_DEV // TILE
    split = fine.reshape(heads, TILE_ROWS, TILE_COLS, groups, TILE_ROWS, TILE_COLS)
    column = jnp.sum(split, axis=(1, 3, 4)).reshape(heads, -1)
    row = jnp.sum(split, axis=(2, 3, 5)).reshape(heads, -1)

    def hot(size):
        at = jnp.arange(size, dtype=jnp.int32)
        offset = (at[:, None] - at[None, :] + size - 1).reshape(-1, 1)
        return (offset == jnp.arange(2 * size - 1, dtype=jnp.int32)[None, :]).astype(jnp.float32)

    column = jnp.dot(column, hot(TILE_COLS), precision=HIGHEST)
    row = jnp.dot(row, hot(TILE_ROWS), precision=HIGHEST)
    return jnp.concatenate([column, row], axis=1)


def after(array, *others):
    return lax.optimization_barrier((array, *others))[0]


def by_heads(queries, keys, values, grad_out, bias_table, slot_tiles, live, buckets):
    count = lax.axis_size("seq")
    windows = lax.axis_size("dp")
    position = lax.axis_index("seq").astype(jnp.int32)
    place = jnp.stack([position, lax.axis_index("dp").astype(jnp.int32)])
    each = HEADS // count
    chunks = [each - each // 3, each // 3]
    starts = [0, chunks[0] * count]
    arrays = (queries[0], keys[0], values[0], grad_out[0])
    pairs = sorted(range(1, count // 2), key=lambda d: (-bin(d).count("1"), d))
    bent = [d for d in pairs if bin(d).count("1") > 1]
    straight = [d for d in pairs if d not in bent]

    def send(message, k):
        return lax.ppermute(message, "seq", [(i, i ^ k) for i in range(count)])

    def packed(flags, chunk, targets, sizes):
        return list(
            pack(flags, buckets, arrays, starts[chunk], chunks[chunk], count, targets, sizes)
        )

    def grads_of(chunk, blocks, sources, more):
        row = starts[chunk] + position * chunks[chunk]
        part = lax.dynamic_slice_in_dim(table, row, chunks[chunk], 0)
        bias = fine_bias_of(
            part[:, BUCKETS : BUCKETS + COLUMN_WIDTH], part[:, BUCKETS + COLUMN_WIDTH :]
        )
        return window_grads(
            place, slot_tiles, part, bias * LOG2E, blocks, sources, count, more
        )

    def table_rows(fine, coarse):
        return jnp.concatenate([coarse[:, :BUCKETS], fine_grads_of(fine)], axis=1)

    table = bias_table
    step = 1
    while step < windows:
        other = lax.ppermute(table, "dp", [(i, i ^ step) for i in range(windows)])
        table = jnp.where(
            place[1] & step == 0,
            jnp.concatenate([table, other], axis=0),
            jnp.concatenate([other, table], axis=0),
        )
        step *= 2

    held = [0] + straight
    targets = {2 * d: (i, 0) for i, d in enumerate(held)}
    targets.update({2 * d + 1: (len(held), i) for i, d in enumerate(held)})
    direct = [2 * d + core for core in range(2) for d in bent]
    targets.update({k: (len(held) + 1 + i, None) for i, k in enumerate(direct)})
    first = packed(live, 0, targets, [2] * len(held) + [len(held)] + [None] * len(direct))
    ready, cross, single = first[: len(held)], first[len(held)], first[len(held) + 1 :]
    half = len(bent)
    single[:half] = [send(m, k) for m, k in zip(single[:half], direct[:half])]
    ready = list(merge(send(cross, 1), ready, None))
    single[half:] = [send(after(m, ready[0]), k) for m, k in zip(single[half:], direct[half:])]
    ready[1:] = [send(m, 2 * d) for m, d in zip(ready[1:], straight)]
    sources = {2 * d + core: (i, core) for i, d in enumerate(held) for core in range(2)}
    sources.update({k: (len(held) + i, None) for i, k in enumerate(direct)})
    every = {ABSOLUTE + i: (0, i) for i in range(count)}
    (second,) = packed(after(live, ready[0]), 1, every, [count])
    second = lax.all_to_all(after(second, *ready[1:]), "seq", 0, 0)
    cross, first, fine, coarse = grads_of(0, ready + single, sources, 0)

    first_rows = table_rows(fine, coarse)
    first = list(merge(send(cross, 1), first, None))
    for d in pairs:
        first[d] = send(first[d], 2 * d)
    cross, second, fine, coarse = grads_of(1, [second], every, STAMP)
    rows = jnp.concatenate([first_rows, table_rows(fine, coarse)], axis=0)
    step = 1
    while step < windows:
        rows = rows + lax.ppermute(rows, "dp", [(i, i ^ step) for i in range(windows)])
        step *= 2
    second = list(merge(send(cross, 1), second, jnp.stack([rows, send(rows, 1)])))
    for d in pairs:
        second[d] = send(second[d], 2 * d)
    outs = unpack(place, first, 3, starts[0], chunks[0], None, 0)
    outs = unpack(place, second, 3, starts[1], chunks[1], outs, bias_table.shape[0])
    return (outs[0][None], outs[1][None], outs[2][None], outs[3])


def from_behind(block, axis, distance):
    devices = range(lax.axis_size(axis))
    route = [(i - distance, i) for i in devices if i - distance in devices]
    return lax.ppermute(block, axis, route)


def from_behind_2(value, axis, by):
    count = lax.axis_size(axis)
    return lax.ppermute(value, axis, [(i, (i + by) % count) for i in range(count)])


def offset_hots():
    tile_rows = TILE // TILE_COLS
    query_pos = jnp.arange(TOK_DEV, dtype=jnp.int32)[:, None]
    key_pos = jnp.arange(TILE, dtype=jnp.int32)[None, :]
    column_index = key_pos % TILE_COLS - query_pos % TILE_COLS + TILE_COLS - 1
    row_index = key_pos // TILE_COLS - query_pos // TILE_COLS % tile_rows + tile_rows - 1
    column_hot = (
        column_index.reshape(1, -1) == jnp.arange(2 * TILE_COLS - 1, dtype=jnp.int32)[:, None]
    ).astype(jnp.float32)
    row_hot = (
        row_index.reshape(1, -1) == jnp.arange(2 * tile_rows - 1, dtype=jnp.int32)[:, None]
    ).astype(jnp.float32)
    return (column_hot, row_hot)


def by_tiles(queries, keys, values, grad_out, bias_table, slot_tiles, live, buckets):
    axis_size = lax.axis_size("seq")
    position = lax.axis_index("seq")
    half = axis_size // 2
    scale = HEAD_DIM ** (-0.5)
    column_width = 2 * TILE_COLS - 1
    table = lax.all_gather(bias_table, "dp", axis=0, tiled=True)
    column_hot, row_hot = offset_hots()
    fine_bias = jnp.dot(table[:, BUCKETS : BUCKETS + column_width], column_hot, precision=HIGHEST)
    fine_bias = fine_bias + jnp.dot(table[:, BUCKETS + column_width :], row_hot, precision=HIGHEST)
    fine_bias = fine_bias.reshape(HEADS, TOK_DEV, TILE)
    bucket_hot = (buckets[0][:, None] == jnp.arange(BUCKETS, dtype=jnp.int32)[None, :]).astype(
        jnp.float32
    )
    coarse = jnp.dot(bucket_hot, table[:, :BUCKETS].T, precision=HIGHEST)
    alive = live[0].astype(jnp.float32)
    query_heads = queries[0].reshape(TOK_DEV, HEADS, HEAD_DIM)
    upstream_heads = grad_out[0].reshape(TOK_DEV, HEADS, HEAD_DIM)
    own_pairs = jnp.stack(
        [keys[0].reshape(TILES_DEV, TILE, WIDTH), values[0].reshape(TILES_DEV, TILE, WIDTH)], axis=1
    )

    def requested(slot, requester):
        wanted = jnp.clip(slot_tiles[requester, slot] - position * TILES_DEV, 0, TILES_DEV - 1)
        return lax.dynamic_index_in_dim(own_pairs, wanted, 0, keepdims=False)

    fetched = []
    for slot, offset in enumerate(NEAR_OFFSETS):
        requester = jnp.clip(position - offset, 0, axis_size - 1)
        fetched.append(from_behind(requested(slot, requester), "seq", -offset))
    far_requester = (position + half) % axis_size
    fetched.append(from_behind_2(requested(SLOTS - 1, far_requester), "seq", half))
    remote_pairs = jnp.stack(fetched)
    own_group = (own_pairs, coarse[:TILES_DEV], alive[:TILES_DEV])
    remote_group = (remote_pairs, coarse[TILES_DEV:], alive[TILES_DEV:])

    def scores_of(pair, coarse_row):
        key_heads = pair[0].reshape(TILE, HEADS, HEAD_DIM)
        raw = jnp.einsum("qhd,khd->hqk", query_heads, key_heads, preferred_element_type=jnp.float32)
        return raw * scale + coarse_row[:, None, None] + fine_bias

    def products_of(pair):
        value_heads = pair[1].reshape(TILE, HEADS, HEAD_DIM)
        return jnp.einsum(
            "qhd,khd->hqk", upstream_heads, value_heads, preferred_element_type=jnp.float32
        )

    def stats_step(carry, item):
        top, total, weighted = carry
        pair, coarse_row, flag = item
        scores = scores_of(pair, coarse_row)
        attend_grad = products_of(pair)
        keep = flag > 0
        new_top = jnp.where(keep, jnp.maximum(top, jnp.max(scores, axis=2, keepdims=True)), top)
        factor = jnp.exp(top - new_top)
        expo = jnp.exp(scores - new_top) * flag
        added = jnp.sum(expo, axis=2, keepdims=True)
        added_weighted = jnp.sum(expo * attend_grad, axis=2, keepdims=True)
        return ((new_top, total * factor + added, weighted * factor + added_weighted), None)

    stats = (
        jnp.full((HEADS, TOK_DEV, 1), NEGATIVE, jnp.float32),
        jnp.zeros((HEADS, TOK_DEV, 1), jnp.float32),
        jnp.zeros((HEADS, TOK_DEV, 1), jnp.float32),
    )
    stats, _ = lax.scan(stats_step, stats, own_group)
    stats, _ = lax.scan(stats_step, stats, remote_group)
    log_total = stats[0] + jnp.log(stats[1])
    delta = stats[2] / stats[1]

    def grad_step(carry, item):
        query_grad, fine_sum = carry
        pair, coarse_row, flag = item
        scores = scores_of(pair, coarse_row)
        attend = jnp.exp(scores - log_total) * flag
        attend_grad = products_of(pair)
        score_grad = attend * (attend_grad - delta)
        attend_low = attend.astype(jnp.bfloat16)
        grad_low = score_grad.astype(jnp.bfloat16)
        key_heads = pair[0].reshape(TILE, HEADS, HEAD_DIM)
        value_part = jnp.einsum(
            "hqk,qhd->khd", attend_low, upstream_heads, preferred_element_type=jnp.float32
        ).reshape(TILE, WIDTH)
        key_part = (
            jnp.einsum(
                "hqk,qhd->khd", grad_low, query_heads, preferred_element_type=jnp.float32
            ).reshape(TILE, WIDTH)
            * scale
        )
        query_grad = (
            query_grad
            + jnp.einsum("hqk,khd->qhd", grad_low, key_heads, preferred_element_type=jnp.float32)
            * scale
        )
        return (
            (query_grad, fine_sum + score_grad),
            (key_part, value_part, jnp.sum(score_grad, axis=(1, 2))),
        )

    carry = (
        jnp.zeros((TOK_DEV, HEADS, HEAD_DIM), jnp.float32),
        jnp.zeros((HEADS, TOK_DEV, TILE), jnp.float32),
    )
    carry, own_out = lax.scan(grad_step, carry, own_group)
    carry, remote_out = lax.scan(grad_step, carry, remote_group)
    query_grad, fine_sum = carry
    remote_low = jnp.stack([remote_out[0], remote_out[1]], axis=1).astype(jnp.bfloat16)

    def deposit(totals, slot, requester, arrived, weight):
        wanted = jnp.clip(slot_tiles[requester, slot] - position * TILES_DEV, 0, TILES_DEV - 1)
        pick = (jnp.arange(TILES_DEV, dtype=jnp.int32) == wanted).astype(jnp.float32)[
            :, None, None
        ] * weight
        return (
            totals[0] + pick * arrived[0].astype(jnp.float32)[None],
            totals[1] + pick * arrived[1].astype(jnp.float32)[None],
        )

    totals = (own_out[0], own_out[1])
    for slot, offset in enumerate(NEAR_OFFSETS):
        arrived = from_behind(remote_low[slot], "seq", offset)
        requester = jnp.clip(position - offset, 0, axis_size - 1)
        totals = deposit(totals, slot, requester, arrived, 1.0)
    arrived = from_behind_2(remote_low[SLOTS - 1], "seq", half)
    totals = deposit(totals, SLOTS - 1, (position + half) % axis_size, arrived, 1.0)
    block_sums = jnp.concatenate([own_out[2], remote_out[2]], axis=0)
    coarse_grad = jnp.dot(block_sums.T, bucket_hot, precision=HIGHEST)
    flat_sum = fine_sum.reshape(HEADS, TOK_DEV * TILE)
    column_grad = jnp.dot(flat_sum, column_hot.T, precision=HIGHEST)
    row_grad = jnp.dot(flat_sum, row_hot.T, precision=HIGHEST)
    table_grad = jnp.concatenate([coarse_grad, column_grad, row_grad], axis=1)
    summed = lax.psum(table_grad, "seq")
    table_out = lax.psum_scatter(summed, "dp", scatter_dimension=0, tiled=True)
    query_out = query_grad.reshape(1, TOK_DEV, WIDTH).astype(jnp.bfloat16)
    key_out = totals[0].reshape(1, TOK_DEV, WIDTH).astype(jnp.bfloat16)
    value_out = totals[1].reshape(1, TOK_DEV, WIDTH).astype(jnp.bfloat16)
    return (query_out, key_out, value_out, table_out)


def solution(mesh):
    count = mesh.shape["seq"]
    windows = mesh.shape["dp"]
    whole = HEADS % (3 * count) == 0 and count > 2 and count & (count - 1) == 0 and windows & (windows - 1) == 0
    plan = by_heads if whole else by_tiles
    return jax.shard_map(
        plan,
        mesh=mesh,
        in_specs=(
            P("dp", "seq", None),
            P("dp", "seq", None),
            P("dp", "seq", None),
            P("dp", "seq", None),
            P("dp", None),
            P(),
            P("seq", None),
            P("seq", None),
        ),
        out_specs=(P("dp", "seq", None), P("dp", "seq", None), P("dp", "seq", None), P("dp", None)),
        check_vma=False,
    )
```

```python
import functools

import jax
import jax.numpy as jnp
from jax import lax
from jax.experimental import pallas as pl
from jax.experimental.pallas import tpu as pltpu
from jax.sharding import PartitionSpec as P

HEADS = 24
HEAD_DIM = 128
TOK_DEV = 256
TILE = 128
TILE_COLS = 16
SLOTS = 5
BUCKETS = 82
WIDTH = 3072
TILES_DEV = 2
ENTRIES = TILES_DEV + SLOTS
TILE_ROWS = TILE // TILE_COLS
COLUMN_WIDTH = 2 * TILE_COLS - 1
ROW_WIDTH = 2 * TILE_ROWS - 1

NEGATIVE = -1e30
HIGHEST = lax.Precision.HIGHEST
NEAR_OFFSETS = (-1, 1, -2, 2)
LOG2E = 1.4426950408889634
SCALE = HEAD_DIM ** (-0.5)
VMEM_LIMIT = 67000000


SIZES = (1, 2, 4, 5, 6, ENTRIES)
ABSOLUTE = 1 << 16
STAMP = 16
META = 16
HBM = pl.BlockSpec(memory_space=pltpu.HBM)
SMEM = pl.BlockSpec(memory_space=pltpu.SMEM)


def pack_body(number, heads, first, count, targets, *refs):
    live_ref, bucket_ref = refs[:2]
    arrays = refs[2 : 2 + number]
    outs = refs[2 + number : -4]
    held_ref, meta_ref, in_sem, out_sem = refs[-4:]
    width = heads * HEAD_DIM
    position = lax.axis_index("seq")
    span = pl.ds(first * HEAD_DIM, count * width)
    arriving = [
        pltpu.make_async_copy(arrays[a].at[:, span], held_ref.at[a], in_sem.at[a])
        for a in range(number)
    ]
    for copy in arriving:
        copy.start()
    row = lax.broadcasted_iota(jnp.int32, (META, width), 0)
    lane = lax.broadcasted_iota(jnp.int32, (META, width), 1)
    meta = jnp.zeros((META, width), jnp.int32)
    for e in range(ENTRIES):
        meta = jnp.where((row == e) & (lane == 0), bucket_ref[0, e], meta)
        meta = jnp.where((row == e) & (lane == 1), live_ref[0, e], meta)
    meta_ref[...] = meta.astype(jnp.float32).astype(jnp.bfloat16)
    columns, messages = [], []
    for k, (out, at) in targets.items():
        column = (k - ABSOLUTE) * width if k >= ABSOLUTE else (position ^ k) * width
        columns.append(column if k >= ABSOLUTE else pl.multiple_of(column, HEAD_DIM))
        messages.append(outs[out] if at is None else outs[out].at[at])
    leaving = [
        pltpu.make_async_copy(meta_ref, message.at[pl.ds(number * TOK_DEV, META)], out_sem)
        for message in messages
    ]
    for copy in leaving:
        copy.start()
    for a in range(number):
        arriving[a].wait()
        for message, column in zip(messages, columns):
            leaving.append(
                pltpu.make_async_copy(
                    held_ref.at[a, :, pl.ds(column, width)],
                    message.at[pl.ds(a * TOK_DEV, TOK_DEV)],
                    out_sem,
                )
            )
            leaving[-1].start()
    for copy in leaving:
        copy.wait()


def pack(live, buckets, arrays, first, heads, count, targets, sizes):
    number = len(arrays)
    rows = number * TOK_DEV + META
    width = heads * HEAD_DIM
    return pl.pallas_call(
        functools.partial(pack_body, number, heads, first, count, targets),
        in_specs=[SMEM] * 2 + [HBM] * number,
        out_specs=[HBM] * len(sizes),
        out_shape=[
            jax.ShapeDtypeStruct((() if size is None else (size,)) + (rows, width), jnp.bfloat16)
            for size in sizes
        ],
        scratch_shapes=[
            pltpu.VMEM((number, TOK_DEV, count * width), jnp.bfloat16),
            pltpu.VMEM((META, width), jnp.bfloat16),
            pltpu.SemaphoreType.DMA((number,)),
            pltpu.SemaphoreType.DMA,
        ],
        compiler_params=pltpu.CompilerParams(vmem_limit_bytes=VMEM_LIMIT),
        cost_estimate=pl.CostEstimate(
            flops=0, bytes_accessed=4 * count * rows * width, transcendentals=0
        ),
    )(live, buckets, *arrays)


def unpack_body(number, heads, first, count, held, owned, *refs):
    place_ref = refs[0]
    pairs = count // 2
    blocks = [refs[1 + k // 2].at[k % 2] for k in range(count)]
    outs = refs[1 + pairs + held : 1 + pairs + held + number]
    scratch = refs[1 + pairs + held + number :]
    if owned:
        table_ref, held_ref, in_sem, out_sem, stamp_ref, whole_ref, stamp_sem = scratch
        stamps = [
            pltpu.make_async_copy(
                blocks[k].at[pl.ds(number * TOK_DEV, STAMP)], stamp_ref.at[k], stamp_sem
            )
            for k in range(count)
        ]
    else:
        held_ref, in_sem, out_sem = scratch
    width = heads * HEAD_DIM
    position = place_ref[0]
    arriving, leaving = [], []
    for k in range(count):
        column = pl.multiple_of(first * HEAD_DIM + (position ^ k) * width, HEAD_DIM)
        for a in range(number):
            n = k * number + a
            arriving.append(
                pltpu.make_async_copy(
                    blocks[k].at[pl.ds(a * TOK_DEV, TOK_DEV)], held_ref.at[n], in_sem.at[n]
                )
            )
            leaving.append(
                pltpu.make_async_copy(
                    held_ref.at[n], outs[a].at[:, pl.ds(column, width)], out_sem
                )
            )
            arriving[n].start()
    if owned:
        for copy in stamps:
            copy.start()
    for n in range(count * number):
        arriving[n].wait()
        leaving[n].start()
    if owned:
        for copy in stamps:
            copy.wait()
        each = HEADS // count
        for k in range(count):
            parts = stamp_ref[k].astype(jnp.float32)
            rows = parts[0:each] + parts[each : 2 * each] + parts[2 * each : 3 * each]
            source = position ^ k
            for r in range(each):
                head = source * (each - heads) + r if r < each - heads else first + source * heads + r - (each - heads)
                whole_ref[pl.ds(head, 1)] = rows[r : r + 1]
        for r in range(owned):
            table_ref[r : r + 1] = whole_ref[pl.ds(place_ref[1] * owned + r, 1)]
    for copy in leaving:
        copy.wait()


def unpack(place, blocks, number, first, heads, onto, owned):
    pairs = len(blocks)
    count = 2 * pairs
    held = 0 if onto is None else number
    out_specs = [HBM] * number
    out_shape = [jax.ShapeDtypeStruct((TOK_DEV, WIDTH), jnp.bfloat16)] * number
    scratch_shapes = [
        pltpu.VMEM((count * number, TOK_DEV, heads * HEAD_DIM), jnp.bfloat16),
        pltpu.SemaphoreType.DMA((count * number,)),
        pltpu.SemaphoreType.DMA,
    ]
    if owned:
        out_specs = out_specs + [pl.BlockSpec(memory_space=pltpu.VMEM)]
        out_shape = out_shape + [jax.ShapeDtypeStruct((owned, TILE), jnp.float32)]
        scratch_shapes += [
            pltpu.VMEM((count, STAMP, heads * HEAD_DIM), jnp.bfloat16),
            pltpu.VMEM((HEADS, TILE), jnp.float32),
            pltpu.SemaphoreType.DMA,
        ]
    return pl.pallas_call(
        functools.partial(unpack_body, number, heads, first, count, held, owned),
        in_specs=[SMEM] + [HBM] * (pairs + held),
        out_specs=out_specs,
        out_shape=out_shape,
        input_output_aliases={1 + pairs + a: a for a in range(held)},
        scratch_shapes=scratch_shapes,
        compiler_params=pltpu.CompilerParams(vmem_limit_bytes=VMEM_LIMIT),
        cost_estimate=pl.CostEstimate(
            flops=0, bytes_accessed=4 * count * number * TOK_DEV * heads * HEAD_DIM, transcendentals=0
        ),
    )(place, *blocks, *(onto if onto is not None else ()))


def merge_body(pairs, rows, stamped, *refs):
    cross_ref = refs[0]
    outs = refs[1 + stamped + pairs : 1 + stamped + 2 * pairs]
    held_ref, low_ref, in_sem, out_sem = refs[1 + stamped + 2 * pairs :]
    arriving = [
        pltpu.make_async_copy(
            cross_ref.at[d], held_ref.at[d, pl.ds(0, rows)], in_sem.at[d]
        )
        for d in range(pairs)
    ]
    for copy in arriving:
        copy.start()
    leaving = []
    if stamped:
        low_ref[...] = jnp.zeros_like(low_ref)
        for s in range(2):
            rest = refs[1][s]
            number = rest.shape[0]
            for part in range(3):
                low = rest.astype(jnp.bfloat16).astype(jnp.float32)
                low_ref[s, part * number : (part + 1) * number] = low
                rest = rest - low
        whole = low_ref[...].astype(jnp.bfloat16)
        held_ref[0:2, rows : rows + STAMP] = whole
        for d in range(pairs):
            leaving += [
                pltpu.make_async_copy(
                    held_ref.at[s, pl.ds(rows, STAMP)], outs[d].at[s, pl.ds(rows, STAMP)], out_sem
                )
                for s in range(2)
            ]
            leaving[-2].start()
            leaving[-1].start()
    for d in range(pairs):
        arriving[d].wait()
        leaving.append(
            pltpu.make_async_copy(
                held_ref.at[d, pl.ds(0, rows)], outs[d].at[1, pl.ds(0, rows)], out_sem
            )
        )
        leaving[-1].start()
    for copy in leaving:
        copy.wait()


def merge(cross, messages, table_rows):
    pairs, rows, width = cross.shape
    stamped = 0 if table_rows is None else 1
    shape = messages[0].shape
    return pl.pallas_call(
        functools.partial(merge_body, pairs, rows, stamped),
        in_specs=[HBM] + [pl.BlockSpec(memory_space=pltpu.VMEM)] * stamped + [HBM] * pairs,
        out_specs=[HBM] * pairs,
        out_shape=[jax.ShapeDtypeStruct(shape, jnp.bfloat16)] * pairs,
        input_output_aliases={1 + stamped + d: d for d in range(pairs)},
        scratch_shapes=[
            pltpu.VMEM((pairs,) + shape[1:], jnp.bfloat16),
            pltpu.VMEM((2, STAMP, TILE), jnp.float32),
            pltpu.SemaphoreType.DMA((pairs,)),
            pltpu.SemaphoreType.DMA,
        ],
        compiler_params=pltpu.CompilerParams(vmem_limit_bytes=VMEM_LIMIT),
        cost_estimate=pl.CostEstimate(
            flops=0, bytes_accessed=4 * cross.size, transcendentals=0
        ),
    )(cross, *(() if table_rows is None else (table_rows,)), *messages)


def fold(array, combine):
    parts = [array[r : r + 8] for r in range(0, array.shape[0], 8)]
    while len(parts) > 1:
        parts = [combine(parts[2 * k], parts[2 * k + 1]) for k in range(len(parts) // 2)]
    return parts[0]


def grad_body(count, heads, sources, *refs):
    place_ref, slots_ref, table_ref, bias_ref = refs[:4]
    refs = refs[4:]
    inputs = 1 + max(source for source, _ in sources.values())
    blocks, refs = refs[:inputs], refs[inputs:]
    cross_ref, refs = refs[0], refs[1:]
    pairs, refs = refs[: count // 2], refs[count // 2 :]
    outs = [(pairs[k // 2].at[0], cross_ref.at[k // 2])[k % 2] for k in range(count)]
    fine_ref, coarse_out_ref = refs[:2]
    (
        x_ref,
        y_ref,
        coarse_ref,
        sums_ref,
        score_ref,
        product_ref,
        low_ref,
        key_ref,
        key_grad_ref,
        value_grad_ref,
        in_sem,
        out_sem,
        list_ref,
        tile_ref,
        number_ref,
    ) = refs[2:]
    position = place_ref[0]

    def lanes(h):
        return pl.ds(h * HEAD_DIM, HEAD_DIM)

    arriving = []
    for h in range(heads):
        arriving.append([])
        for k, (source, at) in sources.items():
            block = blocks[source] if at is None else blocks[source].at[at]
            tile = k - ABSOLUTE if k >= ABSOLUTE else position ^ k
            arriving[h].append(
                pltpu.make_async_copy(
                    block.at[:, lanes(h)], x_ref.at[tile, :, lanes(h)], in_sem.at[h]
                )
            )
    def leaving(h, begin, size):
        return [
            pltpu.make_async_copy(
                y_ref.at[position ^ k, pl.ds(begin, size), lanes(h)],
                outs[k].at[pl.ds(begin, size), lanes(h)],
                out_sem,
            )
            for k in range(count)
        ]

    for copies in arriving:
        for copy in copies:
            copy.start()
    lane = lax.broadcasted_iota(jnp.int32, (8, TILE), 1)
    transposed = (((1,), (1,)), ((), ()))

    def array_rows(a, begin=0, size=TOK_DEV):
        return pl.ds(a * TOK_DEV + begin, size)

    def meta_of(i):
        meta = x_ref[i, 4 * TOK_DEV : 4 * TOK_DEV + META, 0:TILE].astype(jnp.float32)[:8]
        hot = (lane == meta[:, 0:1].astype(jnp.int32)).astype(jnp.float32)
        return hot, meta[:, 1:2]

    def list_live(i, flag):
        row = lax.broadcasted_iota(jnp.int32, (8, 1), 0)
        code = jnp.sum(jnp.where(flag > 0, 1 << row, 0).astype(jnp.float32)).astype(jnp.int32)
        for e in range(8):
            list_ref[i * 8 + e] = ENTRIES
            tile_ref[i * 8 + e] = (
                slots_ref[i, e - TILES_DEV]
                if TILES_DEV <= e < ENTRIES
                else i * TILES_DEV + e % TILES_DEV
            )
        number = jnp.int32(0)
        for e in range(ENTRIES):
            list_ref[i * 8 + number] = e
            number = number + ((code >> e) & 1)
        list_ref[i * 8 + number] = ENTRIES
        number_ref[i] = number

    every = range(heads)
    columns = [slice(h * HEAD_DIM, (h + 1) * HEAD_DIM) for h in every]
    tiles_all = count * TILES_DEV
    key_grad_ref[...] = jnp.zeros_like(key_grad_ref)
    value_grad_ref[...] = jnp.zeros_like(value_grad_ref)
    fine_ref[...] = jnp.zeros_like(fine_ref)
    sums_ref[...] = jnp.zeros_like(sums_ref)
    for copy in arriving[0]:
        copy.wait()
    for i in range(count):
        hot, flag = meta_of(i)
        list_live(i, flag)
        for h in every:
            coarse = jnp.sum(hot * table_ref[h : h + 1, :], axis=1, keepdims=True) * LOG2E
            coarse = jnp.where(flag > 0, coarse, NEGATIVE)
            coarse_ref[h, i] = jnp.broadcast_to(coarse, (8, TOK_DEV))
    for copies in arriving[1:]:
        for copy in copies:
            copy.wait()

    def query_tile(i, size):
        query = [x_ref[i, array_rows(0), columns[h]] for h in every]
        upstream = [x_ref[i, array_rows(3), columns[h]] for h in every]
        entries = [list_ref[i * 8 + s] for s in range(size)]
        tiles = [tile_ref[i * 8 + e] for e in entries]
        coarse = [[coarse_ref[h, i, pl.ds(e, 1)] for e in entries] for h in every]

        def tile_of(a, s, h):
            begin = pl.multiple_of(a * TOK_DEV + (tiles[s] % TILES_DEV) * TILE, TILE)
            return x_ref[tiles[s] // TILES_DEV, pl.ds(begin, TILE), columns[h]]

        tops = []
        for h in every:
            top = None
            for s in range(size):
                key = tile_of(1, s, h)
                key_ref[h, s * TILE : (s + 1) * TILE] = key
                raw = lax.dot_general(
                    key, query[h], transposed, preferred_element_type=jnp.float32
                )
                score = raw * (SCALE * LOG2E) + bias_ref[h]
                score_ref[h, s] = score
                best = fold(score, jnp.maximum) + coarse[h][s]
                top = best if top is None else jnp.maximum(top, best)
            tops.append(jnp.max(top, axis=0, keepdims=True))
        inverses, deltas = [], []
        for h in every:
            total = jnp.zeros((8, TOK_DEV), jnp.float32)
            weighted = jnp.zeros((8, TOK_DEV), jnp.float32)
            for s in range(size):
                product = lax.dot_general(
                    tile_of(2, s, h), upstream[h], transposed, preferred_element_type=jnp.float32
                )
                expo = jnp.exp2(score_ref[h, s] - (tops[h] - coarse[h][s]))
                score_ref[h, s] = expo
                product_ref[h, s] = product
                total = total + fold(expo, jnp.add)
                weighted = weighted + fold(expo * product, jnp.add)
            inverses.append(1.0 / jnp.sum(total, axis=0, keepdims=True))
            deltas.append(jnp.sum(weighted, axis=0, keepdims=True) * inverses[h])
        for h in every:
            for s in range(size):
                attend = score_ref[h, s] * inverses[h]
                grad = attend * (product_ref[h, s] - deltas[h])
                fine_ref[h] += grad
                sums = jnp.sum(fold(grad, jnp.add), axis=0, keepdims=True)
                sums_ref[h, i, pl.ds(entries[s], 1)] = sums[:, :TILE] + sums[:, TILE:]
                grad_low = grad.astype(jnp.bfloat16)
                low_ref[h, s * TILE : (s + 1) * TILE] = grad_low
                value_grad_ref[h * tiles_all + tiles[s]] += jnp.dot(
                    attend.astype(jnp.bfloat16), upstream[h], preferred_element_type=jnp.float32
                )
                key_grad_ref[h * tiles_all + tiles[s]] += jnp.dot(
                    grad_low, query[h], preferred_element_type=jnp.float32
                )
        for h in every:
            query_grad = lax.dot_general(
                key_ref[h, : size * TILE],
                low_ref[h, : size * TILE],
                (((0,), (0,)), ((), ())),
                preferred_element_type=jnp.float32,
            )
            y_ref[i, array_rows(0), columns[h]] = (query_grad.T * SCALE).astype(jnp.bfloat16)

    @pl.loop(0, count)
    def _(i):
        number = number_ref[i]
        below = 0
        for size in SIZES:
            pl.when((number > below) & (number <= size))(functools.partial(query_tile, i, size))
            below = size

    started = []
    for h in every:
        started += leaving(h, 0, TOK_DEV)
    for copy in started:
        copy.start()
    for h in every:

        @pl.loop(0, count)
        def _(i):
            for t in range(TILES_DEV):
                tile = h * tiles_all + i * TILES_DEV + t
                y_ref[i, array_rows(1, t * TILE, TILE), columns[h]] = (
                    key_grad_ref[tile] * SCALE
                ).astype(jnp.bfloat16)
                y_ref[i, array_rows(2, t * TILE, TILE), columns[h]] = value_grad_ref[tile].astype(
                    jnp.bfloat16
                )

        rest = leaving(h, TOK_DEV, 2 * TOK_DEV)
        for copy in rest:
            copy.start()
        started += rest

    for h in every:
        coarse_grad = jnp.zeros((1, TILE), jnp.float32)
        for i in range(count):
            hot, _ = meta_of(i)
            sums = jnp.sum(sums_ref[h, i], axis=1, keepdims=True)
            coarse_grad = coarse_grad + jnp.sum(hot * sums, axis=0, keepdims=True)
        coarse_out_ref[h : h + 1] = coarse_grad

    for copy in started:
        copy.wait()


def window_grads(place, slots, table, bias, blocks, sources, count, more):
    heads = table.shape[0]
    width = heads * HEAD_DIM
    rows = 3 * TOK_DEV
    pairs = count // 2
    work = heads * count * ENTRIES * TILE * TOK_DEV
    vmem = pl.BlockSpec(memory_space=pltpu.VMEM)
    results = pl.pallas_call(
        functools.partial(grad_body, count, heads, sources),
        in_specs=[SMEM, SMEM, vmem, vmem] + [HBM] * len(blocks),
        out_specs=[HBM] * (1 + pairs) + [vmem] * 2,
        out_shape=[jax.ShapeDtypeStruct((pairs, rows, width), jnp.bfloat16)]
        + [jax.ShapeDtypeStruct((2, rows + more, width), jnp.bfloat16)] * pairs
        + [
            jax.ShapeDtypeStruct((heads, TILE, TOK_DEV), jnp.float32),
            jax.ShapeDtypeStruct((heads, TILE), jnp.float32),
        ],
        scratch_shapes=[
            pltpu.VMEM((count, 4 * TOK_DEV + META, width), jnp.bfloat16),
            pltpu.VMEM((count, rows, width), jnp.bfloat16),
            pltpu.VMEM((heads, count, 8, TOK_DEV), jnp.float32),
            pltpu.VMEM((heads, count, 8, TILE), jnp.float32),
            pltpu.VMEM((heads, ENTRIES, TILE, TOK_DEV), jnp.float32),
            pltpu.VMEM((heads, ENTRIES, TILE, TOK_DEV), jnp.float32),
            pltpu.VMEM((heads, ENTRIES * TILE, TOK_DEV), jnp.bfloat16),
            pltpu.VMEM((heads, ENTRIES * TILE, HEAD_DIM), jnp.bfloat16),
            pltpu.VMEM((heads * count * TILES_DEV, TILE, HEAD_DIM), jnp.float32),
            pltpu.VMEM((heads * count * TILES_DEV, TILE, HEAD_DIM), jnp.float32),
            pltpu.SemaphoreType.DMA((heads,)),
            pltpu.SemaphoreType.DMA,
            pltpu.SMEM((count * 8,), jnp.int32),
            pltpu.SMEM((count * 8,), jnp.int32),
            pltpu.SMEM((count,), jnp.int32),
        ],
        compiler_params=pltpu.CompilerParams(vmem_limit_bytes=VMEM_LIMIT),
        cost_estimate=pl.CostEstimate(
            flops=10 * work * HEAD_DIM,
            bytes_accessed=2 * 7 * count * TOK_DEV * width,
            transcendentals=work,
        ),
    )(place, slots, table, bias, *blocks)
    return results[0], list(results[1 : 1 + pairs]), results[1 + pairs], results[2 + pairs]


def fine_bias_of(columns, rows):
    heads = columns.shape[0]
    column = jnp.stack(
        [columns[:, TILE_COLS - 1 - a : 2 * TILE_COLS - 1 - a] for a in range(TILE_COLS)], axis=2
    )
    row = jnp.stack(
        [rows[:, TILE_ROWS - 1 - a : 2 * TILE_ROWS - 1 - a] for a in range(TILE_ROWS)], axis=2
    )
    row = jnp.tile(row, (1, 1, TOK_DEV // TILE))
    column = jnp.tile(column, (1, TILE_ROWS, TOK_DEV // TILE_COLS))
    row = jnp.repeat(jnp.repeat(row, TILE_COLS, axis=1), TILE_COLS, axis=2)
    return (column + row).reshape(heads, TILE, TOK_DEV)


def fine_grads_of(fine):
    heads = fine.shape[0]
    groups = TOK_DEV // TILE
    split = fine.reshape(heads, TILE_ROWS, TILE_COLS, groups, TILE_ROWS, TILE_COLS)
    column = jnp.sum(split, axis=(1, 3, 4)).reshape(heads, -1)
    row = jnp.sum(split, axis=(2, 3, 5)).reshape(heads, -1)

    def hot(size):
        at = jnp.arange(size, dtype=jnp.int32)
        offset = (at[:, None] - at[None, :] + size - 1).reshape(-1, 1)
        return (offset == jnp.arange(2 * size - 1, dtype=jnp.int32)[None, :]).astype(jnp.float32)

    column = jnp.dot(column, hot(TILE_COLS), precision=HIGHEST)
    row = jnp.dot(row, hot(TILE_ROWS), precision=HIGHEST)
    return jnp.concatenate([column, row], axis=1)


def after(array, *others):
    return lax.optimization_barrier((array, *others))[0]


def by_heads(queries, keys, values, grad_out, bias_table, slot_tiles, live, buckets):
    count = lax.axis_size("seq")
    windows = lax.axis_size("dp")
    position = lax.axis_index("seq").astype(jnp.int32)
    place = jnp.stack([position, lax.axis_index("dp").astype(jnp.int32)])
    each = HEADS // count
    chunks = [each - each // 3, each // 3]
    starts = [0, chunks[0] * count]
    arrays = (queries[0], keys[0], values[0], grad_out[0])
    pairs = sorted(range(1, count // 2), key=lambda d: (-bin(d).count("1"), d))
    bent = [d for d in pairs if bin(d).count("1") > 1]
    straight = [d for d in pairs if d not in bent]

    def send(message, k):
        return lax.ppermute(message, "seq", [(i, i ^ k) for i in range(count)])

    def packed(flags, chunk, targets, sizes):
        return list(
            pack(flags, buckets, arrays, starts[chunk], chunks[chunk], count, targets, sizes)
        )

    def grads_of(chunk, blocks, sources, more):
        row = starts[chunk] + position * chunks[chunk]
        part = lax.dynamic_slice_in_dim(table, row, chunks[chunk], 0)
        bias = fine_bias_of(
            part[:, BUCKETS : BUCKETS + COLUMN_WIDTH], part[:, BUCKETS + COLUMN_WIDTH :]
        )
        return window_grads(
            place, slot_tiles, part, bias * LOG2E, blocks, sources, count, more
        )

    def table_rows(fine, coarse):
        return jnp.concatenate([coarse[:, :BUCKETS], fine_grads_of(fine)], axis=1)

    table = bias_table
    step = 1
    while step < windows:
        other = lax.ppermute(table, "dp", [(i, i ^ step) for i in range(windows)])
        table = jnp.where(
            place[1] & step == 0,
            jnp.concatenate([table, other], axis=0),
            jnp.concatenate([other, table], axis=0),
        )
        step *= 2

    held = [0] + straight
    targets = {2 * d: (i, 0) for i, d in enumerate(held)}
    targets.update({2 * d + 1: (len(held), i) for i, d in enumerate(held)})
    direct = [2 * d + core for core in range(2) for d in bent]
    targets.update({k: (len(held) + 1 + i, None) for i, k in enumerate(direct)})
    first = packed(live, 0, targets, [2] * len(held) + [len(held)] + [None] * len(direct))
    ready, cross, single = first[: len(held)], first[len(held)], first[len(held) + 1 :]
    half = len(bent)
    single[:half] = [send(m, k) for m, k in zip(single[:half], direct[:half])]
    ready = list(merge(send(cross, 1), ready, None))
    single[half:] = [send(after(m, ready[0]), k) for m, k in zip(single[half:], direct[half:])]
    ready[1:] = [send(m, 2 * d) for m, d in zip(ready[1:], straight)]
    sources = {2 * d + core: (i, core) for i, d in enumerate(held) for core in range(2)}
    sources.update({k: (len(held) + i, None) for i, k in enumerate(direct)})
    every = {ABSOLUTE + i: (0, i) for i in range(count)}
    (second,) = packed(after(live, ready[0]), 1, every, [count])
    second = lax.all_to_all(after(second, *ready[1:]), "seq", 0, 0)
    cross, first, fine, coarse = grads_of(0, ready + single, sources, 0)

    first_rows = table_rows(fine, coarse)
    first = list(merge(send(cross, 1), first, None))
    for d in pairs:
        first[d] = send(first[d], 2 * d)
    cross, second, fine, coarse = grads_of(1, [second], every, STAMP)
    rows = jnp.concatenate([first_rows, table_rows(fine, coarse)], axis=0)
    step = 1
    while step < windows:
        rows = rows + lax.ppermute(rows, "dp", [(i, i ^ step) for i in range(windows)])
        step *= 2
    second = list(merge(send(cross, 1), second, jnp.stack([rows, send(rows, 1)])))
    for d in pairs:
        second[d] = send(second[d], 2 * d)
    outs = unpack(place, first, 3, starts[0], chunks[0], None, 0)
    outs = unpack(place, second, 3, starts[1], chunks[1], outs, bias_table.shape[0])
    return (outs[0][None], outs[1][None], outs[2][None], outs[3])


def from_behind(block, axis, distance):
    devices = range(lax.axis_size(axis))
    route = [(i - distance, i) for i in devices if i - distance in devices]
    return lax.ppermute(block, axis, route)


def from_behind_2(value, axis, by):
    count = lax.axis_size(axis)
    return lax.ppermute(value, axis, [(i, (i + by) % count) for i in range(count)])


def offset_hots():
    tile_rows = TILE // TILE_COLS
    query_pos = jnp.arange(TOK_DEV, dtype=jnp.int32)[:, None]
    key_pos = jnp.arange(TILE, dtype=jnp.int32)[None, :]
    column_index = key_pos % TILE_COLS - query_pos % TILE_COLS + TILE_COLS - 1
    row_index = key_pos // TILE_COLS - query_pos // TILE_COLS % tile_rows + tile_rows - 1
    column_hot = (
        column_index.reshape(1, -1) == jnp.arange(2 * TILE_COLS - 1, dtype=jnp.int32)[:, None]
    ).astype(jnp.float32)
    row_hot = (
        row_index.reshape(1, -1) == jnp.arange(2 * tile_rows - 1, dtype=jnp.int32)[:, None]
    ).astype(jnp.float32)
    return (column_hot, row_hot)


def by_tiles(queries, keys, values, grad_out, bias_table, slot_tiles, live, buckets):
    axis_size = lax.axis_size("seq")
    position = lax.axis_index("seq")
    half = axis_size // 2
    scale = HEAD_DIM ** (-0.5)
    column_width = 2 * TILE_COLS - 1
    table = lax.all_gather(bias_table, "dp", axis=0, tiled=True)
    column_hot, row_hot = offset_hots()
    fine_bias = jnp.dot(table[:, BUCKETS : BUCKETS + column_width], column_hot, precision=HIGHEST)
    fine_bias = fine_bias + jnp.dot(table[:, BUCKETS + column_width :], row_hot, precision=HIGHEST)
    fine_bias = fine_bias.reshape(HEADS, TOK_DEV, TILE)
    bucket_hot = (buckets[0][:, None] == jnp.arange(BUCKETS, dtype=jnp.int32)[None, :]).astype(
        jnp.float32
    )
    coarse = jnp.dot(bucket_hot, table[:, :BUCKETS].T, precision=HIGHEST)
    alive = live[0].astype(jnp.float32)
    query_heads = queries[0].reshape(TOK_DEV, HEADS, HEAD_DIM)
    upstream_heads = grad_out[0].reshape(TOK_DEV, HEADS, HEAD_DIM)
    own_pairs = jnp.stack(
        [keys[0].reshape(TILES_DEV, TILE, WIDTH), values[0].reshape(TILES_DEV, TILE, WIDTH)], axis=1
    )

    def requested(slot, requester):
        wanted = jnp.clip(slot_tiles[requester, slot] - position * TILES_DEV, 0, TILES_DEV - 1)
        return lax.dynamic_index_in_dim(own_pairs, wanted, 0, keepdims=False)

    fetched = []
    for slot, offset in enumerate(NEAR_OFFSETS):
        requester = jnp.clip(position - offset, 0, axis_size - 1)
        fetched.append(from_behind(requested(slot, requester), "seq", -offset))
    far_requester = (position + half) % axis_size
    fetched.append(from_behind_2(requested(SLOTS - 1, far_requester), "seq", half))
    remote_pairs = jnp.stack(fetched)
    own_group = (own_pairs, coarse[:TILES_DEV], alive[:TILES_DEV])
    remote_group = (remote_pairs, coarse[TILES_DEV:], alive[TILES_DEV:])

    def scores_of(pair, coarse_row):
        key_heads = pair[0].reshape(TILE, HEADS, HEAD_DIM)
        raw = jnp.einsum("qhd,khd->hqk", query_heads, key_heads, preferred_element_type=jnp.float32)
        return raw * scale + coarse_row[:, None, None] + fine_bias

    def products_of(pair):
        value_heads = pair[1].reshape(TILE, HEADS, HEAD_DIM)
        return jnp.einsum(
            "qhd,khd->hqk", upstream_heads, value_heads, preferred_element_type=jnp.float32
        )

    def stats_step(carry, item):
        top, total, weighted = carry
        pair, coarse_row, flag = item
        scores = scores_of(pair, coarse_row)
        attend_grad = products_of(pair)
        keep = flag > 0
        new_top = jnp.where(keep, jnp.maximum(top, jnp.max(scores, axis=2, keepdims=True)), top)
        factor = jnp.exp(top - new_top)
        expo = jnp.exp(scores - new_top) * flag
        added = jnp.sum(expo, axis=2, keepdims=True)
        added_weighted = jnp.sum(expo * attend_grad, axis=2, keepdims=True)
        return ((new_top, total * factor + added, weighted * factor + added_weighted), None)

    stats = (
        jnp.full((HEADS, TOK_DEV, 1), NEGATIVE, jnp.float32),
        jnp.zeros((HEADS, TOK_DEV, 1), jnp.float32),
        jnp.zeros((HEADS, TOK_DEV, 1), jnp.float32),
    )
    stats, _ = lax.scan(stats_step, stats, own_group)
    stats, _ = lax.scan(stats_step, stats, remote_group)
    log_total = stats[0] + jnp.log(stats[1])
    delta = stats[2] / stats[1]

    def grad_step(carry, item):
        query_grad, fine_sum = carry
        pair, coarse_row, flag = item
        scores = scores_of(pair, coarse_row)
        attend = jnp.exp(scores - log_total) * flag
        attend_grad = products_of(pair)
        score_grad = attend * (attend_grad - delta)
        attend_low = attend.astype(jnp.bfloat16)
        grad_low = score_grad.astype(jnp.bfloat16)
        key_heads = pair[0].reshape(TILE, HEADS, HEAD_DIM)
        value_part = jnp.einsum(
            "hqk,qhd->khd", attend_low, upstream_heads, preferred_element_type=jnp.float32
        ).reshape(TILE, WIDTH)
        key_part = (
            jnp.einsum(
                "hqk,qhd->khd", grad_low, query_heads, preferred_element_type=jnp.float32
            ).reshape(TILE, WIDTH)
            * scale
        )
        query_grad = (
            query_grad
            + jnp.einsum("hqk,khd->qhd", grad_low, key_heads, preferred_element_type=jnp.float32)
            * scale
        )
        return (
            (query_grad, fine_sum + score_grad),
            (key_part, value_part, jnp.sum(score_grad, axis=(1, 2))),
        )

    carry = (
        jnp.zeros((TOK_DEV, HEADS, HEAD_DIM), jnp.float32),
        jnp.zeros((HEADS, TOK_DEV, TILE), jnp.float32),
    )
    carry, own_out = lax.scan(grad_step, carry, own_group)
    carry, remote_out = lax.scan(grad_step, carry, remote_group)
    query_grad, fine_sum = carry
    remote_low = jnp.stack([remote_out[0], remote_out[1]], axis=1).astype(jnp.bfloat16)

    def deposit(totals, slot, requester, arrived, weight):
        wanted = jnp.clip(slot_tiles[requester, slot] - position * TILES_DEV, 0, TILES_DEV - 1)
        pick = (jnp.arange(TILES_DEV, dtype=jnp.int32) == wanted).astype(jnp.float32)[
            :, None, None
        ] * weight
        return (
            totals[0] + pick * arrived[0].astype(jnp.float32)[None],
            totals[1] + pick * arrived[1].astype(jnp.float32)[None],
        )

    totals = (own_out[0], own_out[1])
    for slot, offset in enumerate(NEAR_OFFSETS):
        arrived = from_behind(remote_low[slot], "seq", offset)
        requester = jnp.clip(position - offset, 0, axis_size - 1)
        totals = deposit(totals, slot, requester, arrived, 1.0)
    arrived = from_behind_2(remote_low[SLOTS - 1], "seq", half)
    totals = deposit(totals, SLOTS - 1, (position + half) % axis_size, arrived, 1.0)
    block_sums = jnp.concatenate([own_out[2], remote_out[2]], axis=0)
    coarse_grad = jnp.dot(block_sums.T, bucket_hot, precision=HIGHEST)
    flat_sum = fine_sum.reshape(HEADS, TOK_DEV * TILE)
    column_grad = jnp.dot(flat_sum, column_hot.T, precision=HIGHEST)
    row_grad = jnp.dot(flat_sum, row_hot.T, precision=HIGHEST)
    table_grad = jnp.concatenate([coarse_grad, column_grad, row_grad], axis=1)
    summed = lax.psum(table_grad, "seq")
    table_out = lax.psum_scatter(summed, "dp", scatter_dimension=0, tiled=True)
    query_out = query_grad.reshape(1, TOK_DEV, WIDTH).astype(jnp.bfloat16)
    key_out = totals[0].reshape(1, TOK_DEV, WIDTH).astype(jnp.bfloat16)
    value_out = totals[1].reshape(1, TOK_DEV, WIDTH).astype(jnp.bfloat16)
    return (query_out, key_out, value_out, table_out)


def solution(mesh):
    count = mesh.shape["seq"]
    windows = mesh.shape["dp"]
    whole = HEADS % (3 * count) == 0 and count > 2 and count & (count - 1) == 0 and windows & (windows - 1) == 0
    plan = by_heads if whole else by_tiles
    return jax.shard_map(
        plan,
        mesh=mesh,
        in_specs=(
            P("dp", "seq", None),
            P("dp", "seq", None),
            P("dp", "seq", None),
            P("dp", "seq", None),
            P("dp", None),
            P(),
            P("seq", None),
            P("seq", None),
        ),
        out_specs=(P("dp", "seq", None), P("dp", "seq", None), P("dp", "seq", None), P("dp", None)),
        check_vma=False,
    )
```

```python
import functools

import jax
import jax.numpy as jnp
from jax import lax
from jax.experimental import pallas as pl
from jax.experimental.pallas import tpu as pltpu
from jax.sharding import PartitionSpec as P

HEADS = 24
HEAD_DIM = 128
TOK_DEV = 256
TILE = 128
TILE_COLS = 16
SLOTS = 5
BUCKETS = 82
WIDTH = 3072
TILES_DEV = 2
ENTRIES = TILES_DEV + SLOTS
TILE_ROWS = TILE // TILE_COLS
COLUMN_WIDTH = 2 * TILE_COLS - 1
ROW_WIDTH = 2 * TILE_ROWS - 1

NEGATIVE = -1e30
HIGHEST = lax.Precision.HIGHEST
NEAR_OFFSETS = (-1, 1, -2, 2)
LOG2E = 1.4426950408889634
SCALE = HEAD_DIM ** (-0.5)
VMEM_LIMIT = 67000000


SIZES = tuple(range(1, ENTRIES + 1))
ABSOLUTE = 1 << 16
STAMP = 16
META = 16
HBM = pl.BlockSpec(memory_space=pltpu.HBM)
SMEM = pl.BlockSpec(memory_space=pltpu.SMEM)


def pack_body(number, heads, first, count, targets, *refs):
    live_ref, bucket_ref = refs[:2]
    arrays = refs[2 : 2 + number]
    outs = refs[2 + number : -4]
    held_ref, meta_ref, in_sem, out_sem = refs[-4:]
    width = heads * HEAD_DIM
    position = lax.axis_index("seq")
    span = pl.ds(first * HEAD_DIM, count * width)
    arriving = [
        pltpu.make_async_copy(arrays[a].at[:, span], held_ref.at[a], in_sem.at[a])
        for a in range(number)
    ]
    for copy in arriving:
        copy.start()
    row = lax.broadcasted_iota(jnp.int32, (META, width), 0)
    lane = lax.broadcasted_iota(jnp.int32, (META, width), 1)
    meta = jnp.zeros((META, width), jnp.int32)
    for e in range(ENTRIES):
        meta = jnp.where((row == e) & (lane == 0), bucket_ref[0, e], meta)
        meta = jnp.where((row == e) & (lane == 1), live_ref[0, e], meta)
    meta_ref[...] = meta.astype(jnp.float32).astype(jnp.bfloat16)
    columns, messages = [], []
    for k, (out, at) in targets.items():
        column = (k - ABSOLUTE) * width if k >= ABSOLUTE else (position ^ k) * width
        columns.append(column if k >= ABSOLUTE else pl.multiple_of(column, HEAD_DIM))
        messages.append(outs[out] if at is None else outs[out].at[at])
    leaving = [
        pltpu.make_async_copy(meta_ref, message.at[pl.ds(number * TOK_DEV, META)], out_sem)
        for message in messages
    ]
    for copy in leaving:
        copy.start()
    for a in range(number):
        arriving[a].wait()
        for message, column in zip(messages, columns):
            leaving.append(
                pltpu.make_async_copy(
                    held_ref.at[a, :, pl.ds(column, width)],
                    message.at[pl.ds(a * TOK_DEV, TOK_DEV)],
                    out_sem,
                )
            )
            leaving[-1].start()
    for copy in leaving:
        copy.wait()


def pack(live, buckets, arrays, first, heads, count, targets, sizes):
    number = len(arrays)
    rows = number * TOK_DEV + META
    width = heads * HEAD_DIM
    return pl.pallas_call(
        functools.partial(pack_body, number, heads, first, count, targets),
        in_specs=[SMEM] * 2 + [HBM] * number,
        out_specs=[HBM] * len(sizes),
        out_shape=[
            jax.ShapeDtypeStruct((() if size is None else (size,)) + (rows, width), jnp.bfloat16)
            for size in sizes
        ],
        scratch_shapes=[
            pltpu.VMEM((number, TOK_DEV, count * width), jnp.bfloat16),
            pltpu.VMEM((META, width), jnp.bfloat16),
            pltpu.SemaphoreType.DMA((number,)),
            pltpu.SemaphoreType.DMA,
        ],
        compiler_params=pltpu.CompilerParams(vmem_limit_bytes=VMEM_LIMIT),
        cost_estimate=pl.CostEstimate(
            flops=0, bytes_accessed=4 * count * rows * width, transcendentals=0
        ),
    )(live, buckets, *arrays)


def unpack_body(number, heads, first, count, held, owned, *refs):
    place_ref = refs[0]
    pairs = count // 2
    blocks = [refs[1 + k // 2].at[k % 2] for k in range(count)]
    outs = refs[1 + pairs + held : 1 + pairs + held + number]
    scratch = refs[1 + pairs + held + number :]
    if owned:
        table_ref, held_ref, in_sem, out_sem, stamp_ref, whole_ref, stamp_sem = scratch
        stamps = [
            pltpu.make_async_copy(
                blocks[k].at[pl.ds(number * TOK_DEV, STAMP)], stamp_ref.at[k], stamp_sem
            )
            for k in range(count)
        ]
    else:
        held_ref, in_sem, out_sem = scratch
    width = heads * HEAD_DIM
    position = place_ref[0]
    arriving, leaving = [], []
    for k in range(count):
        column = pl.multiple_of(first * HEAD_DIM + (position ^ k) * width, HEAD_DIM)
        for a in range(number):
            n = k * number + a
            arriving.append(
                pltpu.make_async_copy(
                    blocks[k].at[pl.ds(a * TOK_DEV, TOK_DEV)], held_ref.at[n], in_sem.at[n]
                )
            )
            leaving.append(
                pltpu.make_async_copy(
                    held_ref.at[n], outs[a].at[:, pl.ds(column, width)], out_sem
                )
            )
            arriving[n].start()
    if owned:
        for copy in stamps:
            copy.start()
    for n in range(count * number):
        arriving[n].wait()
        leaving[n].start()
    if owned:
        for copy in stamps:
            copy.wait()
        each = HEADS // count
        for k in range(count):
            parts = stamp_ref[k].astype(jnp.float32)
            rows = parts[0:each] + parts[each : 2 * each] + parts[2 * each : 3 * each]
            source = position ^ k
            for r in range(each):
                head = source * (each - heads) + r if r < each - heads else first + source * heads + r - (each - heads)
                whole_ref[pl.ds(head, 1)] = rows[r : r + 1]
        for r in range(owned):
            table_ref[r : r + 1] = whole_ref[pl.ds(place_ref[1] * owned + r, 1)]
    for copy in leaving:
        copy.wait()


def unpack(place, blocks, number, first, heads, onto, owned):
    pairs = len(blocks)
    count = 2 * pairs
    held = 0 if onto is None else number
    out_specs = [HBM] * number
    out_shape = [jax.ShapeDtypeStruct((TOK_DEV, WIDTH), jnp.bfloat16)] * number
    scratch_shapes = [
        pltpu.VMEM((count * number, TOK_DEV, heads * HEAD_DIM), jnp.bfloat16),
        pltpu.SemaphoreType.DMA((count * number,)),
        pltpu.SemaphoreType.DMA,
    ]
    if owned:
        out_specs = out_specs + [pl.BlockSpec(memory_space=pltpu.VMEM)]
        out_shape = out_shape + [jax.ShapeDtypeStruct((owned, TILE), jnp.float32)]
        scratch_shapes += [
            pltpu.VMEM((count, STAMP, heads * HEAD_DIM), jnp.bfloat16),
            pltpu.VMEM((HEADS, TILE), jnp.float32),
            pltpu.SemaphoreType.DMA,
        ]
    return pl.pallas_call(
        functools.partial(unpack_body, number, heads, first, count, held, owned),
        in_specs=[SMEM] + [HBM] * (pairs + held),
        out_specs=out_specs,
        out_shape=out_shape,
        input_output_aliases={1 + pairs + a: a for a in range(held)},
        scratch_shapes=scratch_shapes,
        compiler_params=pltpu.CompilerParams(vmem_limit_bytes=VMEM_LIMIT),
        cost_estimate=pl.CostEstimate(
            flops=0, bytes_accessed=4 * count * number * TOK_DEV * heads * HEAD_DIM, transcendentals=0
        ),
    )(place, *blocks, *(onto if onto is not None else ()))


def merge_body(pairs, rows, stamped, *refs):
    cross_ref = refs[0]
    outs = refs[1 + stamped + pairs : 1 + stamped + 2 * pairs]
    held_ref, low_ref, in_sem, out_sem = refs[1 + stamped + 2 * pairs :]
    arriving = [
        pltpu.make_async_copy(
            cross_ref.at[d], held_ref.at[d, pl.ds(0, rows)], in_sem.at[d]
        )
        for d in range(pairs)
    ]
    for copy in arriving:
        copy.start()
    leaving = []
    if stamped:
        low_ref[...] = jnp.zeros_like(low_ref)
        for s in range(2):
            rest = refs[1][s]
            number = rest.shape[0]
            for part in range(3):
                low = rest.astype(jnp.bfloat16).astype(jnp.float32)
                low_ref[s, part * number : (part + 1) * number] = low
                rest = rest - low
        whole = low_ref[...].astype(jnp.bfloat16)
        held_ref[0:2, rows : rows + STAMP] = whole
        for d in range(pairs):
            leaving += [
                pltpu.make_async_copy(
                    held_ref.at[s, pl.ds(rows, STAMP)], outs[d].at[s, pl.ds(rows, STAMP)], out_sem
                )
                for s in range(2)
            ]
            leaving[-2].start()
            leaving[-1].start()
    for d in range(pairs):
        arriving[d].wait()
        leaving.append(
            pltpu.make_async_copy(
                held_ref.at[d, pl.ds(0, rows)], outs[d].at[1, pl.ds(0, rows)], out_sem
            )
        )
        leaving[-1].start()
    for copy in leaving:
        copy.wait()


def merge(cross, messages, table_rows):
    pairs, rows, width = cross.shape
    stamped = 0 if table_rows is None else 1
    shape = messages[0].shape
    return pl.pallas_call(
        functools.partial(merge_body, pairs, rows, stamped),
        in_specs=[HBM] + [pl.BlockSpec(memory_space=pltpu.VMEM)] * stamped + [HBM] * pairs,
        out_specs=[HBM] * pairs,
        out_shape=[jax.ShapeDtypeStruct(shape, jnp.bfloat16)] * pairs,
        input_output_aliases={1 + stamped + d: d for d in range(pairs)},
        scratch_shapes=[
            pltpu.VMEM((pairs,) + shape[1:], jnp.bfloat16),
            pltpu.VMEM((2, STAMP, TILE), jnp.float32),
            pltpu.SemaphoreType.DMA((pairs,)),
            pltpu.SemaphoreType.DMA,
        ],
        compiler_params=pltpu.CompilerParams(vmem_limit_bytes=VMEM_LIMIT),
        cost_estimate=pl.CostEstimate(
            flops=0, bytes_accessed=4 * cross.size, transcendentals=0
        ),
    )(cross, *(() if table_rows is None else (table_rows,)), *messages)


def fold(array, combine):
    parts = [array[r : r + 8] for r in range(0, array.shape[0], 8)]
    while len(parts) > 1:
        parts = [combine(parts[2 * k], parts[2 * k + 1]) for k in range(len(parts) // 2)]
    return parts[0]


def grad_body(count, heads, sources, *refs):
    place_ref, slots_ref, table_ref, bias_ref = refs[:4]
    refs = refs[4:]
    inputs = 1 + max(source for source, _ in sources.values())
    blocks, refs = refs[:inputs], refs[inputs:]
    cross_ref, refs = refs[0], refs[1:]
    pairs, refs = refs[: count // 2], refs[count // 2 :]
    outs = [(pairs[k // 2].at[0], cross_ref.at[k // 2])[k % 2] for k in range(count)]
    fine_ref, coarse_out_ref = refs[:2]
    (
        x_ref,
        y_ref,
        coarse_ref,
        sums_ref,
        score_ref,
        product_ref,
        low_ref,
        key_ref,
        key_grad_ref,
        value_grad_ref,
        in_sem,
        out_sem,
        list_ref,
        tile_ref,
        number_ref,
    ) = refs[2:]
    position = place_ref[0]

    def lanes(h):
        return pl.ds(h * HEAD_DIM, HEAD_DIM)

    arriving = []
    for h in range(heads):
        arriving.append([])
        for k, (source, at) in sources.items():
            block = blocks[source] if at is None else blocks[source].at[at]
            tile = k - ABSOLUTE if k >= ABSOLUTE else position ^ k
            arriving[h].append(
                pltpu.make_async_copy(
                    block.at[:, lanes(h)], x_ref.at[tile, :, lanes(h)], in_sem.at[h]
                )
            )
    def leaving(h, begin, size):
        return [
            pltpu.make_async_copy(
                y_ref.at[position ^ k, pl.ds(begin, size), lanes(h)],
                outs[k].at[pl.ds(begin, size), lanes(h)],
                out_sem,
            )
            for k in range(count)
        ]

    for copies in arriving:
        for copy in copies:
            copy.start()
    lane = lax.broadcasted_iota(jnp.int32, (8, TILE), 1)
    transposed = (((1,), (1,)), ((), ()))

    def array_rows(a, begin=0, size=TOK_DEV):
        return pl.ds(a * TOK_DEV + begin, size)

    def meta_of(i):
        meta = x_ref[i, 4 * TOK_DEV : 4 * TOK_DEV + META, 0:TILE].astype(jnp.float32)[:8]
        hot = (lane == meta[:, 0:1].astype(jnp.int32)).astype(jnp.float32)
        return hot, meta[:, 1:2]

    def list_live(i, flag):
        row = lax.broadcasted_iota(jnp.int32, (8, 1), 0)
        code = jnp.sum(jnp.where(flag > 0, 1 << row, 0).astype(jnp.float32)).astype(jnp.int32)
        for e in range(8):
            list_ref[i * 8 + e] = ENTRIES
            tile_ref[i * 8 + e] = (
                slots_ref[i, e - TILES_DEV]
                if TILES_DEV <= e < ENTRIES
                else i * TILES_DEV + e % TILES_DEV
            )
        number = jnp.int32(0)
        for e in range(ENTRIES):
            list_ref[i * 8 + number] = e
            number = number + ((code >> e) & 1)
        list_ref[i * 8 + number] = ENTRIES
        number_ref[i] = number

    every = range(heads)
    columns = [slice(h * HEAD_DIM, (h + 1) * HEAD_DIM) for h in every]
    tiles_all = count * TILES_DEV
    key_grad_ref[...] = jnp.zeros_like(key_grad_ref)
    value_grad_ref[...] = jnp.zeros_like(value_grad_ref)
    fine_ref[...] = jnp.zeros_like(fine_ref)
    sums_ref[...] = jnp.zeros_like(sums_ref)
    for copy in arriving[0]:
        copy.wait()
    for i in range(count):
        hot, flag = meta_of(i)
        list_live(i, flag)
        for h in every:
            coarse = jnp.sum(hot * table_ref[h : h + 1, :], axis=1, keepdims=True) * LOG2E
            coarse = jnp.where(flag > 0, coarse, NEGATIVE)
            coarse_ref[h, i] = jnp.broadcast_to(coarse, (8, TOK_DEV))
    for copies in arriving[1:]:
        for copy in copies:
            copy.wait()

    def query_tile(i, size):
        query = [x_ref[i, array_rows(0), columns[h]] for h in every]
        upstream = [x_ref[i, array_rows(3), columns[h]] for h in every]
        entries = [list_ref[i * 8 + s] for s in range(size)]
        tiles = [tile_ref[i * 8 + e] for e in entries]
        coarse = [[coarse_ref[h, i, pl.ds(e, 1)] for e in entries] for h in every]

        def tile_of(a, s, h):
            begin = pl.multiple_of(a * TOK_DEV + (tiles[s] % TILES_DEV) * TILE, TILE)
            return x_ref[tiles[s] // TILES_DEV, pl.ds(begin, TILE), columns[h]]

        tops = []
        for h in every:
            top = None
            for s in range(size):
                key = tile_of(1, s, h)
                key_ref[h, s * TILE : (s + 1) * TILE] = key
                raw = lax.dot_general(
                    key, query[h], transposed, preferred_element_type=jnp.float32
                )
                score = raw * (SCALE * LOG2E) + bias_ref[h]
                score_ref[h, s] = score
                best = fold(score, jnp.maximum) + coarse[h][s]
                top = best if top is None else jnp.maximum(top, best)
            tops.append(jnp.max(top, axis=0, keepdims=True))
        inverses, deltas = [], []
        for h in every:
            total = jnp.zeros((8, TOK_DEV), jnp.float32)
            weighted = jnp.zeros((8, TOK_DEV), jnp.float32)
            for s in range(size):
                product = lax.dot_general(
                    tile_of(2, s, h), upstream[h], transposed, preferred_element_type=jnp.float32
                )
                expo = jnp.exp2(score_ref[h, s] - (tops[h] - coarse[h][s]))
                score_ref[h, s] = expo
                product_ref[h, s] = product
                total = total + fold(expo, jnp.add)
                weighted = weighted + fold(expo * product, jnp.add)
            inverses.append(1.0 / jnp.sum(total, axis=0, keepdims=True))
            deltas.append(jnp.sum(weighted, axis=0, keepdims=True) * inverses[h])
        for h in every:
            for s in range(size):
                attend = score_ref[h, s] * inverses[h]
                grad = attend * (product_ref[h, s] - deltas[h])
                fine_ref[h] += grad
                sums = jnp.sum(fold(grad, jnp.add), axis=0, keepdims=True)
                sums_ref[h, i, pl.ds(entries[s], 1)] = sums[:, :TILE] + sums[:, TILE:]
                grad_low = grad.astype(jnp.bfloat16)
                low_ref[h, s * TILE : (s + 1) * TILE] = grad_low
                value_grad_ref[h * tiles_all + tiles[s]] += jnp.dot(
                    attend.astype(jnp.bfloat16), upstream[h], preferred_element_type=jnp.float32
                )
                key_grad_ref[h * tiles_all + tiles[s]] += jnp.dot(
                    grad_low, query[h], preferred_element_type=jnp.float32
                )
        for h in every:
            query_grad = lax.dot_general(
                key_ref[h, : size * TILE],
                low_ref[h, : size * TILE],
                (((0,), (0,)), ((), ())),
                preferred_element_type=jnp.float32,
            )
            y_ref[i, array_rows(0), columns[h]] = (query_grad.T * SCALE).astype(jnp.bfloat16)

    @pl.loop(0, count)
    def _(i):
        number = number_ref[i]
        below = 0
        for size in SIZES:
            pl.when((number > below) & (number <= size))(functools.partial(query_tile, i, size))
            below = size

    started = []
    for h in every:
        started += leaving(h, 0, TOK_DEV)
    for copy in started:
        copy.start()
    for h in every:

        @pl.loop(0, count)
        def _(i):
            for t in range(TILES_DEV):
                tile = h * tiles_all + i * TILES_DEV + t
                y_ref[i, array_rows(1, t * TILE, TILE), columns[h]] = (
                    key_grad_ref[tile] * SCALE
                ).astype(jnp.bfloat16)
                y_ref[i, array_rows(2, t * TILE, TILE), columns[h]] = value_grad_ref[tile].astype(
                    jnp.bfloat16
                )

        rest = leaving(h, TOK_DEV, 2 * TOK_DEV)
        for copy in rest:
            copy.start()
        started += rest

    for h in every:
        coarse_grad = jnp.zeros((1, TILE), jnp.float32)
        for i in range(count):
            hot, _ = meta_of(i)
            sums = jnp.sum(sums_ref[h, i], axis=1, keepdims=True)
            coarse_grad = coarse_grad + jnp.sum(hot * sums, axis=0, keepdims=True)
        coarse_out_ref[h : h + 1] = coarse_grad

    for copy in started:
        copy.wait()


def window_grads(place, slots, table, bias, blocks, sources, count, more):
    heads = table.shape[0]
    width = heads * HEAD_DIM
    rows = 3 * TOK_DEV
    pairs = count // 2
    work = heads * count * ENTRIES * TILE * TOK_DEV
    vmem = pl.BlockSpec(memory_space=pltpu.VMEM)
    results = pl.pallas_call(
        functools.partial(grad_body, count, heads, sources),
        in_specs=[SMEM, SMEM, vmem, vmem] + [HBM] * len(blocks),
        out_specs=[HBM] * (1 + pairs) + [vmem] * 2,
        out_shape=[jax.ShapeDtypeStruct((pairs, rows, width), jnp.bfloat16)]
        + [jax.ShapeDtypeStruct((2, rows + more, width), jnp.bfloat16)] * pairs
        + [
            jax.ShapeDtypeStruct((heads, TILE, TOK_DEV), jnp.float32),
            jax.ShapeDtypeStruct((heads, TILE), jnp.float32),
        ],
        scratch_shapes=[
            pltpu.VMEM((count, 4 * TOK_DEV + META, width), jnp.bfloat16),
            pltpu.VMEM((count, rows, width), jnp.bfloat16),
            pltpu.VMEM((heads, count, 8, TOK_DEV), jnp.float32),
            pltpu.VMEM((heads, count, 8, TILE), jnp.float32),
            pltpu.VMEM((heads, ENTRIES, TILE, TOK_DEV), jnp.float32),
            pltpu.VMEM((heads, ENTRIES, TILE, TOK_DEV), jnp.float32),
            pltpu.VMEM((heads, ENTRIES * TILE, TOK_DEV), jnp.bfloat16),
            pltpu.VMEM((heads, ENTRIES * TILE, HEAD_DIM), jnp.bfloat16),
            pltpu.VMEM((heads * count * TILES_DEV, TILE, HEAD_DIM), jnp.float32),
            pltpu.VMEM((heads * count * TILES_DEV, TILE, HEAD_DIM), jnp.float32),
            pltpu.SemaphoreType.DMA((heads,)),
            pltpu.SemaphoreType.DMA,
            pltpu.SMEM((count * 8,), jnp.int32),
            pltpu.SMEM((count * 8,), jnp.int32),
            pltpu.SMEM((count,), jnp.int32),
        ],
        compiler_params=pltpu.CompilerParams(vmem_limit_bytes=VMEM_LIMIT),
        cost_estimate=pl.CostEstimate(
            flops=10 * work * HEAD_DIM,
            bytes_accessed=2 * 7 * count * TOK_DEV * width,
            transcendentals=work,
        ),
    )(place, slots, table, bias, *blocks)
    return results[0], list(results[1 : 1 + pairs]), results[1 + pairs], results[2 + pairs]


def fine_bias_of(columns, rows):
    heads = columns.shape[0]
    column = jnp.stack(
        [columns[:, TILE_COLS - 1 - a : 2 * TILE_COLS - 1 - a] for a in range(TILE_COLS)], axis=2
    )
    row = jnp.stack(
        [rows[:, TILE_ROWS - 1 - a : 2 * TILE_ROWS - 1 - a] for a in range(TILE_ROWS)], axis=2
    )
    row = jnp.tile(row, (1, 1, TOK_DEV // TILE))
    column = jnp.tile(column, (1, TILE_ROWS, TOK_DEV // TILE_COLS))
    row = jnp.repeat(jnp.repeat(row, TILE_COLS, axis=1), TILE_COLS, axis=2)
    return (column + row).reshape(heads, TILE, TOK_DEV)


def fine_grads_of(fine):
    heads = fine.shape[0]
    groups = TOK_DEV // TILE
    split = fine.reshape(heads, TILE_ROWS, TILE_COLS, groups, TILE_ROWS, TILE_COLS)
    column = jnp.sum(split, axis=(1, 3, 4)).reshape(heads, -1)
    row = jnp.sum(split, axis=(2, 3, 5)).reshape(heads, -1)

    def hot(size):
        at = jnp.arange(size, dtype=jnp.int32)
        offset = (at[:, None] - at[None, :] + size - 1).reshape(-1, 1)
        return (offset == jnp.arange(2 * size - 1, dtype=jnp.int32)[None, :]).astype(jnp.float32)

    column = jnp.dot(column, hot(TILE_COLS), precision=HIGHEST)
    row = jnp.dot(row, hot(TILE_ROWS), precision=HIGHEST)
    return jnp.concatenate([column, row], axis=1)


def after(array, *others):
    return lax.optimization_barrier((array, *others))[0]


def by_heads(queries, keys, values, grad_out, bias_table, slot_tiles, live, buckets):
    count = lax.axis_size("seq")
    windows = lax.axis_size("dp")
    position = lax.axis_index("seq").astype(jnp.int32)
    place = jnp.stack([position, lax.axis_index("dp").astype(jnp.int32)])
    each = HEADS // count
    chunks = [each - each // 3, each // 3]
    starts = [0, chunks[0] * count]
    arrays = (queries[0], keys[0], values[0], grad_out[0])
    pairs = sorted(range(1, count // 2), key=lambda d: (-bin(d).count("1"), d))
    bent = [d for d in pairs if bin(d).count("1") > 1]
    straight = [d for d in pairs if d not in bent]

    def send(message, k):
        return lax.ppermute(message, "seq", [(i, i ^ k) for i in range(count)])

    def packed(flags, chunk, targets, sizes):
        return list(
            pack(flags, buckets, arrays, starts[chunk], chunks[chunk], count, targets, sizes)
        )

    def grads_of(chunk, blocks, sources, more):
        part, bias = parts[chunk]
        return window_grads(
            place, slot_tiles, part, bias, blocks, sources, count, more
        )

    def table_rows(fine, coarse):
        return jnp.concatenate([coarse[:, :BUCKETS], fine_grads_of(fine)], axis=1)

    table = bias_table
    step = 1
    while step < windows:
        other = lax.ppermute(table, "dp", [(i, i ^ step) for i in range(windows)])
        table = jnp.where(
            place[1] & step == 0,
            jnp.concatenate([table, other], axis=0),
            jnp.concatenate([other, table], axis=0),
        )
        step *= 2

    held = [0] + straight
    targets = {2 * d: (i, 0) for i, d in enumerate(held)}
    targets.update({2 * d + 1: (len(held), i) for i, d in enumerate(held)})
    direct = [2 * d + core for core in range(2) for d in bent]
    targets.update({k: (len(held) + 1 + i, None) for i, k in enumerate(direct)})
    first = packed(live, 0, targets, [2] * len(held) + [len(held)] + [None] * len(direct))
    ready, cross, single = first[: len(held)], first[len(held)], first[len(held) + 1 :]
    half = len(bent)
    single[:half] = [send(m, k) for m, k in zip(single[:half], direct[:half])]
    ready = list(merge(send(cross, 1), ready, None))
    single[half:] = [send(after(m, ready[0]), k) for m, k in zip(single[half:], direct[half:])]
    ready[1:] = [send(m, 2 * d) for m, d in zip(ready[1:], straight)]
    sources = {2 * d + core: (i, core) for i, d in enumerate(held) for core in range(2)}
    sources.update({k: (len(held) + i, None) for i, k in enumerate(direct)})
    every = {ABSOLUTE + i: (0, i) for i in range(count)}
    (second,) = packed(after(live, ready[0]), 1, every, [count])
    second = lax.all_to_all(after(second, *ready[1:]), "seq", 0, 0)
    parts = []
    for begin, heads in zip(starts, chunks):
        part = lax.dynamic_slice_in_dim(table, begin + position * heads, heads, 0)
        bias = fine_bias_of(
            part[:, BUCKETS : BUCKETS + COLUMN_WIDTH], part[:, BUCKETS + COLUMN_WIDTH :]
        )
        parts.append((part, bias * LOG2E))
    parts[0], parts[1] = lax.optimization_barrier((parts[0], parts[1]))
    cross, first, fine, coarse = grads_of(0, ready + single, sources, 0)

    first_rows = table_rows(fine, coarse)
    first = list(merge(send(cross, 1), first, None))
    for d in pairs:
        first[d] = send(first[d], 2 * d)
    cross, second, fine, coarse = grads_of(1, [second], every, STAMP)
    rows = jnp.concatenate([first_rows, table_rows(fine, coarse)], axis=0)
    step = 1
    while step < windows:
        rows = rows + lax.ppermute(rows, "dp", [(i, i ^ step) for i in range(windows)])
        step *= 2
    second = list(merge(send(cross, 1), second, jnp.stack([rows, send(rows, 1)])))
    for d in pairs:
        second[d] = send(second[d], 2 * d)
    outs = unpack(place, first, 3, starts[0], chunks[0], None, 0)
    outs = unpack(place, second, 3, starts[1], chunks[1], outs, bias_table.shape[0])
    return (outs[0][None], outs[1][None], outs[2][None], outs[3])


def from_behind(block, axis, distance):
    devices = range(lax.axis_size(axis))
    route = [(i - distance, i) for i in devices if i - distance in devices]
    return lax.ppermute(block, axis, route)


def from_behind_2(value, axis, by):
    count = lax.axis_size(axis)
    return lax.ppermute(value, axis, [(i, (i + by) % count) for i in range(count)])


def offset_hots():
    tile_rows = TILE // TILE_COLS
    query_pos = jnp.arange(TOK_DEV, dtype=jnp.int32)[:, None]
    key_pos = jnp.arange(TILE, dtype=jnp.int32)[None, :]
    column_index = key_pos % TILE_COLS - query_pos % TILE_COLS + TILE_COLS - 1
    row_index = key_pos // TILE_COLS - query_pos // TILE_COLS % tile_rows + tile_rows - 1
    column_hot = (
        column_index.reshape(1, -1) == jnp.arange(2 * TILE_COLS - 1, dtype=jnp.int32)[:, None]
    ).astype(jnp.float32)
    row_hot = (
        row_index.reshape(1, -1) == jnp.arange(2 * tile_rows - 1, dtype=jnp.int32)[:, None]
    ).astype(jnp.float32)
    return (column_hot, row_hot)


def by_tiles(queries, keys, values, grad_out, bias_table, slot_tiles, live, buckets):
    axis_size = lax.axis_size("seq")
    position = lax.axis_index("seq")
    half = axis_size // 2
    scale = HEAD_DIM ** (-0.5)
    column_width = 2 * TILE_COLS - 1
    table = lax.all_gather(bias_table, "dp", axis=0, tiled=True)
    column_hot, row_hot = offset_hots()
    fine_bias = jnp.dot(table[:, BUCKETS : BUCKETS + column_width], column_hot, precision=HIGHEST)
    fine_bias = fine_bias + jnp.dot(table[:, BUCKETS + column_width :], row_hot, precision=HIGHEST)
    fine_bias = fine_bias.reshape(HEADS, TOK_DEV, TILE)
    bucket_hot = (buckets[0][:, None] == jnp.arange(BUCKETS, dtype=jnp.int32)[None, :]).astype(
        jnp.float32
    )
    coarse = jnp.dot(bucket_hot, table[:, :BUCKETS].T, precision=HIGHEST)
    alive = live[0].astype(jnp.float32)
    query_heads = queries[0].reshape(TOK_DEV, HEADS, HEAD_DIM)
    upstream_heads = grad_out[0].reshape(TOK_DEV, HEADS, HEAD_DIM)
    own_pairs = jnp.stack(
        [keys[0].reshape(TILES_DEV, TILE, WIDTH), values[0].reshape(TILES_DEV, TILE, WIDTH)], axis=1
    )

    def requested(slot, requester):
        wanted = jnp.clip(slot_tiles[requester, slot] - position * TILES_DEV, 0, TILES_DEV - 1)
        return lax.dynamic_index_in_dim(own_pairs, wanted, 0, keepdims=False)

    fetched = []
    for slot, offset in enumerate(NEAR_OFFSETS):
        requester = jnp.clip(position - offset, 0, axis_size - 1)
        fetched.append(from_behind(requested(slot, requester), "seq", -offset))
    far_requester = (position + half) % axis_size
    fetched.append(from_behind_2(requested(SLOTS - 1, far_requester), "seq", half))
    remote_pairs = jnp.stack(fetched)
    own_group = (own_pairs, coarse[:TILES_DEV], alive[:TILES_DEV])
    remote_group = (remote_pairs, coarse[TILES_DEV:], alive[TILES_DEV:])

    def scores_of(pair, coarse_row):
        key_heads = pair[0].reshape(TILE, HEADS, HEAD_DIM)
        raw = jnp.einsum("qhd,khd->hqk", query_heads, key_heads, preferred_element_type=jnp.float32)
        return raw * scale + coarse_row[:, None, None] + fine_bias

    def products_of(pair):
        value_heads = pair[1].reshape(TILE, HEADS, HEAD_DIM)
        return jnp.einsum(
            "qhd,khd->hqk", upstream_heads, value_heads, preferred_element_type=jnp.float32
        )

    def stats_step(carry, item):
        top, total, weighted = carry
        pair, coarse_row, flag = item
        scores = scores_of(pair, coarse_row)
        attend_grad = products_of(pair)
        keep = flag > 0
        new_top = jnp.where(keep, jnp.maximum(top, jnp.max(scores, axis=2, keepdims=True)), top)
        factor = jnp.exp(top - new_top)
        expo = jnp.exp(scores - new_top) * flag
        added = jnp.sum(expo, axis=2, keepdims=True)
        added_weighted = jnp.sum(expo * attend_grad, axis=2, keepdims=True)
        return ((new_top, total * factor + added, weighted * factor + added_weighted), None)

    stats = (
        jnp.full((HEADS, TOK_DEV, 1), NEGATIVE, jnp.float32),
        jnp.zeros((HEADS, TOK_DEV, 1), jnp.float32),
        jnp.zeros((HEADS, TOK_DEV, 1), jnp.float32),
    )
    stats, _ = lax.scan(stats_step, stats, own_group)
    stats, _ = lax.scan(stats_step, stats, remote_group)
    log_total = stats[0] + jnp.log(stats[1])
    delta = stats[2] / stats[1]

    def grad_step(carry, item):
        query_grad, fine_sum = carry
        pair, coarse_row, flag = item
        scores = scores_of(pair, coarse_row)
        attend = jnp.exp(scores - log_total) * flag
        attend_grad = products_of(pair)
        score_grad = attend * (attend_grad - delta)
        attend_low = attend.astype(jnp.bfloat16)
        grad_low = score_grad.astype(jnp.bfloat16)
        key_heads = pair[0].reshape(TILE, HEADS, HEAD_DIM)
        value_part = jnp.einsum(
            "hqk,qhd->khd", attend_low, upstream_heads, preferred_element_type=jnp.float32
        ).reshape(TILE, WIDTH)
        key_part = (
            jnp.einsum(
                "hqk,qhd->khd", grad_low, query_heads, preferred_element_type=jnp.float32
            ).reshape(TILE, WIDTH)
            * scale
        )
        query_grad = (
            query_grad
            + jnp.einsum("hqk,khd->qhd", grad_low, key_heads, preferred_element_type=jnp.float32)
            * scale
        )
        return (
            (query_grad, fine_sum + score_grad),
            (key_part, value_part, jnp.sum(score_grad, axis=(1, 2))),
        )

    carry = (
        jnp.zeros((TOK_DEV, HEADS, HEAD_DIM), jnp.float32),
        jnp.zeros((HEADS, TOK_DEV, TILE), jnp.float32),
    )
    carry, own_out = lax.scan(grad_step, carry, own_group)
    carry, remote_out = lax.scan(grad_step, carry, remote_group)
    query_grad, fine_sum = carry
    remote_low = jnp.stack([remote_out[0], remote_out[1]], axis=1).astype(jnp.bfloat16)

    def deposit(totals, slot, requester, arrived, weight):
        wanted = jnp.clip(slot_tiles[requester, slot] - position * TILES_DEV, 0, TILES_DEV - 1)
        pick = (jnp.arange(TILES_DEV, dtype=jnp.int32) == wanted).astype(jnp.float32)[
            :, None, None
        ] * weight
        return (
            totals[0] + pick * arrived[0].astype(jnp.float32)[None],
            totals[1] + pick * arrived[1].astype(jnp.float32)[None],
        )

    totals = (own_out[0], own_out[1])
    for slot, offset in enumerate(NEAR_OFFSETS):
        arrived = from_behind(remote_low[slot], "seq", offset)
        requester = jnp.clip(position - offset, 0, axis_size - 1)
        totals = deposit(totals, slot, requester, arrived, 1.0)
    arrived = from_behind_2(remote_low[SLOTS - 1], "seq", half)
    totals = deposit(totals, SLOTS - 1, (position + half) % axis_size, arrived, 1.0)
    block_sums = jnp.concatenate([own_out[2], remote_out[2]], axis=0)
    coarse_grad = jnp.dot(block_sums.T, bucket_hot, precision=HIGHEST)
    flat_sum = fine_sum.reshape(HEADS, TOK_DEV * TILE)
    column_grad = jnp.dot(flat_sum, column_hot.T, precision=HIGHEST)
    row_grad = jnp.dot(flat_sum, row_hot.T, precision=HIGHEST)
    table_grad = jnp.concatenate([coarse_grad, column_grad, row_grad], axis=1)
    summed = lax.psum(table_grad, "seq")
    table_out = lax.psum_scatter(summed, "dp", scatter_dimension=0, tiled=True)
    query_out = query_grad.reshape(1, TOK_DEV, WIDTH).astype(jnp.bfloat16)
    key_out = totals[0].reshape(1, TOK_DEV, WIDTH).astype(jnp.bfloat16)
    value_out = totals[1].reshape(1, TOK_DEV, WIDTH).astype(jnp.bfloat16)
    return (query_out, key_out, value_out, table_out)


def solution(mesh):
    count = mesh.shape["seq"]
    windows = mesh.shape["dp"]
    whole = HEADS % (3 * count) == 0 and count > 2 and count & (count - 1) == 0 and windows & (windows - 1) == 0
    plan = by_heads if whole else by_tiles
    return jax.shard_map(
        plan,
        mesh=mesh,
        in_specs=(
            P("dp", "seq", None),
            P("dp", "seq", None),
            P("dp", "seq", None),
            P("dp", "seq", None),
            P("dp", None),
            P(),
            P("seq", None),
            P("seq", None),
        ),
        out_specs=(P("dp", "seq", None), P("dp", "seq", None), P("dp", "seq", None), P("dp", None)),
        check_vma=False,
    )
```
